32 devices in a mesh: sub: 4 (over y, x), mem: 8 (over z, core).
Axes of the slice: x: 2, y: 2, z: 4, core: 2. Of those that a mesh axis runs over, the one named last changes fastest.
Arguments:
- member_state: bfloat16 [2, 512, 32, 1024], P(None, 'mem', 'sub'), may hold values from -6 to 6
- hx_values: bfloat16 [2, 512, 4, 16, 512], P(None, 'mem', 'sub'), may hold values from -6 to 6
- obs_value: bfloat16 [2, 4, 16, 512], P(None, 'sub', 'mem'), may hold values from -6 to 6
- obs_var: bfloat16 [2, 4, 16, 512], P(None, 'sub', 'mem'), may hold values from 0.25 to 4
- courant: float32 [2, 1024], replicated, may hold values from -0.95 to 0.95
Outputs:
- forecast: bfloat16 [2, 512, 32, 1024], P(None, 'mem', 'sub')
The draws below stay inside these ranges and needn't reach their ends.
All inputs are finite; a program needn't handle non-finite values. Where the reference program divides by a largest or mean magnitude, that divisor is 1e-20 or more.
Results may differ from the reference program's by a relative error of at most 0.011.
Values may be sent and summed in bfloat16 or wider, within the bound.
No kernel may reach another device: no remote copies, remote signals or barrier semaphores. Data moves between devices by JAX's collectives and lax.ppermute only.
A program may use at most 128 MiB of HBM per device.

```python
import math
import jax
import jax.numpy as jnp
from jax import lax

SLABS = 2
K = 512
OWN = 512
CA = 8
CB = 64
ITERS = 4
STEPS = 4
PATCH_A = 4
PATCH_B = 16
GA = 32
GB = 1024


def steps_of(stream_key, extent, cuts, smallest, top_value):
    def one(dim, parts):
        steps = jax.random.uniform(jax.random.fold_in(jax.random.fold_in(stream_key, 6), dim), (parts,), jnp.float32, smallest / len(cuts), top_value / len(cuts))
        return jnp.repeat(jnp.exp(steps), extent[dim] // parts).reshape((-1,) + (1,) * (len(extent) - dim - 1))

    loudness = one(*cuts[0])
    for cut in cuts[1:]:
        loudness = loudness * one(*cut)
    return loudness


def scatter_about(key, dims, width, most, cuts=(), kind=jnp.bfloat16):
    drawn = jax.random.normal(key, dims, jnp.float32) * width
    if len(cuts) > 0:
        drawn = steps_of(key, dims, cuts, -0.22, 0.18) * drawn
    return jnp.clip(drawn, min=-most, max=most).astype(kind)


def setup_inputs(seed: int = 0) -> dict:
    streams_of = jax.random.split(jax.random.key(seed), 6)
    return {
        "member_state": scatter_about(streams_of[0], (SLABS, K, GA, GB), 1.0, 6.0, ((1, 8), (2, 4))),
        "hx_values": scatter_about(streams_of[1], (SLABS, K, PATCH_A, PATCH_B, OWN), 1.0, 6.0, ((1, 8), (2, 4))),
        "obs_value": scatter_about(streams_of[2], (SLABS, PATCH_A, PATCH_B, OWN), 1.0, 6.0, ((1, 4), (2, 8))),
        "obs_var": jnp.clip(jnp.exp(math.log(4.0) - 2.7725887 * jax.random.uniform(streams_of[3], (SLABS, PATCH_A, PATCH_B, OWN), jnp.float32) ** steps_of(streams_of[3], (SLABS, PATCH_A, PATCH_B, OWN), ((1, 4), (2, 8)), -0.2, 0.2)), 0.25, 4.0).astype(jnp.bfloat16),
        "courant": jnp.clip(jax.random.uniform(streams_of[4], (SLABS, GB), jnp.float32, -0.95, 0.95), -0.95, 0.95),
    }


def mult(left, right):
    left, right = lax.optimization_barrier((left, right))
    return jnp.dot(left.astype(jnp.float32), right.astype(jnp.float32), precision=lax.Precision.HIGHEST)

def patch_update(hx_rows, obs_rows, var_rows, members):
    total = hx_rows.shape[0]
    obs_count = hx_rows.shape[1]
    half_rows = obs_count // 4
    taper_rows = (jnp.arange(half_rows, dtype=jnp.float32) + 1.0) / (half_rows + 1.0)
    local_weight = jnp.concatenate([taper_rows, jnp.ones((2 * half_rows,), jnp.float32), taper_rows[::-1]])
    hx_float = hx_rows.astype(jnp.float32)
    obs_mean = lax.optimization_barrier(jnp.mean(hx_float, axis=0))
    centred = hx_float - obs_mean
    y_pert = centred.astype(jnp.bfloat16)
    weighted = (centred * (local_weight / var_rows)).astype(jnp.bfloat16)
    identity = jnp.eye(total, dtype=jnp.float32)
    system = (total - 1.0) * identity + mult(weighted, y_pert.T)
    row_bound = jnp.max(lax.optimization_barrier(jnp.sum(jnp.abs(system), axis=1)))
    sqrt_iterate = system / row_bound
    inv_iterate = identity
    for iteration in range(ITERS):
        product = mult(inv_iterate.astype(jnp.bfloat16), sqrt_iterate.astype(jnp.bfloat16))
        correction = 1.5 * identity - 0.5 * product
        correction_half = correction.astype(jnp.bfloat16)
        sqrt_iterate = mult(sqrt_iterate.astype(jnp.bfloat16), correction_half)
        inv_iterate = mult(correction_half, inv_iterate.astype(jnp.bfloat16))
    innovation = obs_rows - obs_mean
    projected = lax.optimization_barrier(jnp.sum(weighted.astype(jnp.float32) * innovation, axis=1))
    halfway = jnp.dot(inv_iterate, projected, precision=lax.Precision.HIGHEST)
    mean_weight = jnp.dot(inv_iterate, halfway, precision=lax.Precision.HIGHEST) / row_bound
    transform = (jnp.sqrt((total - 1.0) / row_bound) * inv_iterate + mean_weight[:, None]).astype(jnp.bfloat16)
    member_vals = members.reshape(total, -1).astype(jnp.float32)
    state_mean = lax.optimization_barrier(jnp.mean(member_vals, axis=0))
    state_pert = (member_vals - state_mean).astype(jnp.bfloat16)
    analysis = state_mean + mult(transform.T, state_pert)
    return analysis.astype(jnp.bfloat16).reshape(members.shape)

def advect(u_west, u_here, u_east, speed):
    return u_here - 0.5 * speed * (u_east - u_west) + 0.5 * speed * speed * (u_east - 2.0 * u_here + u_west)

def reference(member_state, hx_values, obs_value, obs_var, courant):
    members_total = member_state.shape[1]
    patch_total = SLABS * PATCH_A * PATCH_B
    half_rows = OWN // 2

    def one_patch(patch_index):
        slab_index = patch_index // (PATCH_A * PATCH_B)
        remain = patch_index % (PATCH_A * PATCH_B)
        patch_a = remain // PATCH_B
        patch_b = remain % PATCH_B
        west_patch = (patch_a + PATCH_A - 1) % PATCH_A
        east_patch = (patch_a + 1) % PATCH_A
        anchor = jnp.zeros((), jnp.int32)

        def hx_of(where):
            piece = lax.dynamic_slice(hx_values, (slab_index.astype(jnp.int32), anchor, where.astype(jnp.int32), patch_b.astype(jnp.int32), anchor), (1, members_total, 1, 1, OWN))
            return piece.reshape(members_total, OWN)

        def obs_of(source, where):
            piece = lax.dynamic_slice(source, (slab_index.astype(jnp.int32), where.astype(jnp.int32), patch_b.astype(jnp.int32), anchor), (1, 1, 1, OWN))
            return piece.reshape(OWN).astype(jnp.float32)
        hx_rows = jnp.concatenate([hx_of(west_patch)[:, half_rows:], hx_of(patch_a), hx_of(east_patch)[:, :half_rows]], axis=1)
        obs_rows = jnp.concatenate([obs_of(obs_value, west_patch)[half_rows:], obs_of(obs_value, patch_a), obs_of(obs_value, east_patch)[:half_rows]])
        var_rows = jnp.concatenate([obs_of(obs_var, west_patch)[half_rows:], obs_of(obs_var, patch_a), obs_of(obs_var, east_patch)[:half_rows]])
        members = lax.dynamic_slice(member_state, (slab_index.astype(jnp.int32), anchor, (patch_a * CA).astype(jnp.int32), (patch_b * CB).astype(jnp.int32)), (1, members_total, CA, CB))
        members = members.reshape(members_total, CA, CB)
        return patch_update(hx_rows, obs_rows, var_rows, members)
    analysis = lax.map(one_patch, jnp.arange(patch_total, dtype=jnp.int32))
    analysis = analysis.reshape(SLABS, PATCH_A, PATCH_B, members_total, CA, CB)
    analysis = analysis.transpose(0, 3, 1, 4, 2, 5).reshape(SLABS, members_total, GA, GB)
    fields = analysis.astype(jnp.float32)
    speed = courant[:, None, None, :]
    for step_index in range(STEPS):
        west_cells = jnp.roll(fields, 1, axis=2)
        east_cells = jnp.roll(fields, -1, axis=2)
        fields = advect(west_cells, fields, east_cells, speed)
    return fields.astype(jnp.bfloat16)
```

```python
import jax
import jax.numpy as jnp
import numpy as np
from jax import lax
from jax.experimental import pallas as pl
from jax.experimental.pallas import tpu as pltpu
from jax.sharding import PartitionSpec as P

ITERS = 4
STEPS = 4
F32 = jnp.float32
BF16 = jnp.bfloat16
VMEM_LIMIT = 48 * 1024 * 1024


def params(count):
    return pltpu.CompilerParams(
        dimension_semantics=("arbitrary",) * count, vmem_limit_bytes=VMEM_LIMIT
    )


def permutation(order):
    matrix = np.zeros((order.size, order.size), np.float32)
    matrix[np.arange(order.size), order.reshape(-1)] = 1.0
    return matrix.astype(jnp.bfloat16)


def permuted(matrix, rows):
    return jnp.dot(matrix, rows, preferred_element_type=F32).astype(BF16)


def pack_obs_kernel(order, rows, out):
    _, width, owners, block, own = out.shape
    flat = rows[...].reshape(order.shape[0], own)
    out[...] = permuted(order[...], flat).reshape(1, width, owners, block, own)


def pack_obs(hx_values, width):
    slabs, local, _, patches, own = hx_values.shape
    owners = patches // width
    block = 16
    index = np.arange(block * patches).reshape(block, owners, width)
    order = permutation(index.transpose(2, 1, 0))
    return pl.pallas_call(
        pack_obs_kernel,
        grid=(slabs, local // block),
        in_specs=[
            pl.BlockSpec(order.shape, lambda s, g: (0, 0)),
            pl.BlockSpec((1, block, 1, patches, own), lambda s, g: (s, g, 0, 0, 0)),
        ],
        out_specs=pl.BlockSpec((1, width, owners, block, own), lambda s, g: (s, 0, 0, g, 0)),
        out_shape=jax.ShapeDtypeStruct((slabs, width, owners, local, own), BF16),
        compiler_params=params(2),
    )(order, hx_values)


def lane_order(width, lanes):
    index = np.arange(width * lanes).reshape(width, width, lanes // width)
    return permutation(index.transpose(1, 0, 2)).T


def pack_state_kernel(order, swap, cells, out):
    _, width, owners, block, size = out.shape
    lanes = cells.shape[3] // owners
    tiles = size // lanes
    rows = permuted(order[...], cells[...].reshape(order.shape[0], cells.shape[3]))
    parts = []
    for owner in range(owners):
        for tile in range(tiles):
            pieces = [
                rows[
                    (half * tiles + tile) * block : (half * tiles + tile + 1) * block,
                    owner * lanes : (owner + 1) * lanes,
                ]
                for half in range(width)
            ]
            parts.append(jnp.concatenate(pieces, axis=1))
    mixed = permuted_lanes(jnp.concatenate(parts, axis=0), swap[...])
    for owner in range(owners):
        for tile in range(tiles):
            at = (owner * tiles + tile) * block
            for part in range(width):
                out[0, part, owner, :, tile * lanes : (tile + 1) * lanes] = mixed[
                    at : at + block, part * lanes : (part + 1) * lanes
                ]


def permuted_lanes(rows, matrix):
    return jnp.dot(rows, matrix, preferred_element_type=F32).astype(BF16)


def pack_state(member_state, width, owners):
    slabs, local, cells_a, cols = member_state.shape
    lanes = cols // owners
    size = cells_a * lanes // width
    block = 32
    index = np.arange(block * cells_a).reshape(block, cells_a)
    order = permutation(index.T)
    swap = lane_order(width, lanes)
    return pl.pallas_call(
        pack_state_kernel,
        grid=(slabs, local // block),
        in_specs=[
            pl.BlockSpec(order.shape, lambda s, g: (0, 0)),
            pl.BlockSpec(swap.shape, lambda s, g: (0, 0)),
            pl.BlockSpec((1, block, cells_a, cols), lambda s, g: (s, g, 0, 0)),
        ],
        out_specs=pl.BlockSpec((1, width, owners, block, size), lambda s, g: (s, 0, 0, g, 0)),
        out_shape=jax.ShapeDtypeStruct((slabs, width, owners, local, size), BF16),
        compiler_params=params(2),
    )(order, swap, member_state)


def unpack_state_kernel(order, swap, packed, out):
    _, width, owners, block, size = packed.shape
    cells_a = out.shape[2]
    tiles = cells_a // width
    lanes = size // tiles
    parts = []
    for owner in range(owners):
        for tile in range(tiles):
            pieces = [
                packed[0, part, owner, :, tile * lanes : (tile + 1) * lanes]
                for part in range(width)
            ]
            parts.append(jnp.concatenate(pieces, axis=1))
    mixed = permuted_lanes(jnp.concatenate(parts, axis=0), swap[...])
    columns = []
    for owner in range(owners):
        rows = []
        for cell in range(cells_a):
            half, tile = cell // tiles, cell % tiles
            at = (owner * tiles + tile) * block
            rows.append(mixed[at : at + block, half * lanes : (half + 1) * lanes])
        columns.append(jnp.concatenate(rows, axis=0))
    rows = permuted(order[...], jnp.concatenate(columns, axis=1))
    out[...] = rows.reshape(out.shape)


def unpack_state(packed, cells_a):
    slabs, width, owners, local, size = packed.shape
    lanes = size * width // cells_a
    cols = owners * lanes
    block = 32
    index = np.arange(block * cells_a).reshape(cells_a, block)
    order = permutation(index.T)
    swap = lane_order(width, lanes).T
    return pl.pallas_call(
        unpack_state_kernel,
        grid=(slabs, local // block),
        in_specs=[
            pl.BlockSpec(order.shape, lambda s, g: (0, 0)),
            pl.BlockSpec(swap.shape, lambda s, g: (0, 0)),
            pl.BlockSpec((1, width, owners, block, size), lambda s, g: (s, 0, 0, g, 0)),
        ],
        out_specs=pl.BlockSpec((1, block, cells_a, cols), lambda s, g: (s, g, 0, 0)),
        out_shape=jax.ShapeDtypeStruct((slabs, local, cells_a, cols), BF16),
        compiler_params=params(2),
    )(order, swap, packed)


def dot_bf16(left, right):
    return jnp.dot(left, right, preferred_element_type=F32)


def transform_kernel(before, middle, after, obs, scale, out, pert, weighted):
    total = middle.shape[1]
    half = before.shape[2]
    projected = jnp.zeros((total, 1), F32)
    start = 0
    for part in (before, middle, after):
        span = part.shape[2]
        for at in range(0, span, half):
            cols = slice(start, start + half)
            values = part[0, :, at : at + half].astype(F32)
            mean = jnp.sum(values, axis=0, keepdims=True) * (1.0 / total)
            centred = values - mean
            pert[:, cols] = centred.astype(BF16)
            scaled = (centred * scale[0, :, cols]).astype(BF16)
            weighted[:, cols] = scaled
            innovation = obs[0, :, cols] - mean
            projected += jnp.sum(scaled.astype(F32) * innovation, axis=1, keepdims=True)
            start += half
    rows = lax.broadcasted_iota(jnp.int32, (total, total), 0)
    columns = lax.broadcasted_iota(jnp.int32, (total, total), 1)
    diagonal = rows == columns
    gram = lax.dot_general(
        weighted[...], pert[...], (((1,), (1,)), ((), ())), preferred_element_type=F32
    )
    system = jnp.where(diagonal, total - 1.0, 0.0) + gram
    bound = jnp.max(jnp.sum(jnp.abs(system), axis=1, keepdims=True), axis=0, keepdims=True)
    root = (system / bound).astype(BF16)
    inverse = None
    for iteration in range(ITERS):
        product = root.astype(F32) if inverse is None else dot_bf16(inverse.astype(BF16), root)
        correction = (jnp.where(diagonal, 1.5, 0.0) - 0.5 * product).astype(BF16)
        if iteration + 1 < ITERS:
            root = dot_bf16(root, correction).astype(BF16)
        if inverse is None:
            inverse = correction.astype(F32)
        else:
            inverse = dot_bf16(correction, inverse.astype(BF16))
    flipped = inverse.T
    halfway = jnp.sum(flipped * projected, axis=0, keepdims=True)
    weight = jnp.sum(inverse * halfway, axis=1, keepdims=True)
    weight = jnp.broadcast_to(weight, (total, 128)).T[0:1, :] / bound
    out[0] = (jnp.sqrt((total - 1.0) / bound) * flipped + weight).astype(BF16)


def transforms(hx_rows, obs_rows, scale_rows, count, wraps):
    total, own = hx_rows.shape[1:]
    half = own // 2
    held = hx_rows.shape[0]
    shift = 0 if wraps else 1
    flops = count * (2 * total * total * 2 * own + 18 * total**3)
    return pl.pallas_call(
        transform_kernel,
        grid=(count,),
        in_specs=[
            pl.BlockSpec((1, total, half), lambda a: ((a + shift + held - 1) % held, 0, 1)),
            pl.BlockSpec((1, total, own), lambda a: (a + shift, 0, 0)),
            pl.BlockSpec((1, total, half), lambda a: ((a + shift + 1) % held, 0, 0)),
            pl.BlockSpec((1, 1, 2 * own), lambda a: (a, 0, 0)),
            pl.BlockSpec((1, 1, 2 * own), lambda a: (a, 0, 0)),
        ],
        out_specs=pl.BlockSpec((1, total, total), lambda a: (a, 0, 0)),
        out_shape=jax.ShapeDtypeStruct((count, total, total), BF16),
        scratch_shapes=[pltpu.VMEM((total, 2 * own), BF16), pltpu.VMEM((total, 2 * own), BF16)],
        compiler_params=params(1),
        cost_estimate=pl.CostEstimate(
            flops=flops, bytes_accessed=4 * count * total * total * 2, transcendentals=0
        ),
    )(hx_rows, hx_rows, hx_rows, obs_rows, scale_rows)


def centre(state, pert, means):
    for a in range(state.shape[0]):
        values = state[a].astype(F32)
        mean = jnp.sum(values, axis=0, keepdims=True) * (1.0 / state.shape[1])
        means[a] = mean
        pert[a] = (values - mean).astype(BF16)


def transport(tiles, here, ahead, behind, low):
    count, depth = len(tiles), len(tiles[0])
    size = tiles[0][0].shape[1]
    shift = size // 2
    for _ in range(STEPS):
        first = [pltpu.roll(column[0], shift, 1) for column in tiles]
        last = [pltpu.roll(column[depth - 1], shift, 1) for column in tiles]
        moved = []
        for a in range(count):
            column = []
            for k in range(depth):
                if k + 1 < depth:
                    after = tiles[a][k + 1]
                else:
                    after = jnp.where(low, first[a], first[(a + 1) % count])
                if k > 0:
                    prior = tiles[a][k - 1]
                else:
                    prior = jnp.where(low, last[(a + count - 1) % count], last[a])
                column.append(here * tiles[a][k] + ahead * after + behind * prior)
            moved.append(column)
        tiles = moved
    return tiles


def forecast_kernel(state, transform, speed, out, pert, means, fields):
    count, block, size = out.shape
    lanes = speed.shape[1]

    @pl.when(pl.program_id(0) == 0)
    def _():
        centre(state, pert, means)

    for a in range(count):
        fields[a] = (dot_bf16(transform[a], pert[a]) + means[a]).astype(BF16)
    chunk = 16
    c = jnp.broadcast_to(speed[...], (chunk, lanes))
    here, ahead, behind = 1.0 - c * c, 0.5 * (c * c - c), 0.5 * (c * c + c)
    low = lax.broadcasted_iota(jnp.int32, (chunk, lanes), 1) < lanes // 2

    def rows_at(step, carry):
        rows = pl.ds(pl.multiple_of(step * chunk, chunk), chunk)
        tiles = [
            [fields[a, rows, k * lanes : (k + 1) * lanes].astype(F32) for k in range(size // lanes)]
            for a in range(count)
        ]
        tiles = transport(tiles, here, ahead, behind, low)
        for a in range(count):
            for k in range(size // lanes):
                out[a, rows, k * lanes : (k + 1) * lanes] = tiles[a][k].astype(BF16)
        return carry

    lax.fori_loop(0, block // chunk, rows_at, 0)


def forecasts(state, transform, speed):
    count, total, size = state.shape
    block = min(total, 256)
    return pl.pallas_call(
        forecast_kernel,
        grid=(total // block,),
        in_specs=[
            pl.BlockSpec((count, total, size), lambda i: (0, 0, 0)),
            pl.BlockSpec((count, block, total), lambda i: (0, i, 0)),
            pl.BlockSpec(speed.shape, lambda i: (0, 0)),
        ],
        out_specs=pl.BlockSpec((count, block, size), lambda i: (0, i, 0)),
        out_shape=jax.ShapeDtypeStruct((count, total, size), BF16),
        scratch_shapes=[
            pltpu.VMEM((count, total, size), BF16),
            pltpu.VMEM((count, 1, size), F32),
            pltpu.VMEM((count, block, size), BF16),
        ],
        compiler_params=params(1),
    )(state, transform, speed)


def analysis_kernel(state, transform, out, pert, means):
    centre(state, pert, means)
    out[0] = (dot_bf16(transform[0], pert[0]) + means[0]).astype(BF16)


def analyses(state, transform):
    count, total, size = state.shape
    return pl.pallas_call(
        analysis_kernel,
        grid=(count,),
        in_specs=[
            pl.BlockSpec((1, total, size), lambda a: (a, 0, 0)),
            pl.BlockSpec((1, total, total), lambda a: (a, 0, 0)),
        ],
        out_specs=pl.BlockSpec((1, total, size), lambda a: (a, 0, 0)),
        out_shape=jax.ShapeDtypeStruct((count, total, size), BF16),
        scratch_shapes=[pltpu.VMEM((1, total, size), BF16), pltpu.VMEM((1, 1, size), F32)],
        compiler_params=params(1),
    )(state, transform)


def shared_transport(analysis, speed, width, jump):
    count, total, size = analysis.shape
    lanes = speed.shape[1]
    cells = lanes // width
    tiles = size // lanes
    fields = widened(analysis, jump).reshape(count + 2, total, tiles, width, cells)
    fields = fields.transpose(1, 0, 3, 2, 4).reshape(total, -1, cells).astype(F32)
    c = speed[0, :cells]
    for _ in range(STEPS):
        prior, here, after = fields[:, :-2], fields[:, 1:-1], fields[:, 2:]
        fields = (1.0 - c * c) * here + 0.5 * (c * c - c) * after + 0.5 * (c * c + c) * prior
    spare = tiles * width - STEPS
    fields = fields[:, spare : fields.shape[1] - spare].astype(BF16)
    fields = fields.reshape(total, count, width, tiles, cells)
    return fields.transpose(1, 0, 3, 2, 4).reshape(count, total, size)


def widened(blocks, jump):
    count = lax.axis_size("sub")
    forward = [(i, (i + jump) % count) for i in range(count)]
    backward = [(target, source) for source, target in forward]
    low = lax.ppermute(blocks[-1:], "sub", forward)
    high = lax.ppermute(blocks[:1], "sub", backward)
    return jnp.concatenate([low, blocks, high], axis=0)


def advance(member_state, hx_values, obs_value, obs_var, courant):
    slabs, local, cells_a, cols = member_state.shape
    patches, own = hx_values.shape[3:]
    owners = lax.axis_size("mem")
    lines = lax.axis_size("sub")
    width = patches // owners
    count = slabs * width
    groups = lines // count
    total = local * owners
    cells_b = cols // patches
    lane_cells = width * cells_b
    place = lax.axis_index("sub") % count
    slab, part = place // width, place % width

    index_groups = None
    if groups > 1:
        held = count * owners
        index_groups = [list(range(g * held, (g + 1) * held)) for g in range(groups)]

    def exchange(blocks):
        return lax.all_to_all(
            blocks,
            ("sub", "mem"),
            split_axis=0,
            concat_axis=0,
            tiled=True,
            axis_index_groups=index_groups,
        )

    hx_rows = exchange(pack_obs(hx_values, width).reshape(count * owners, local, own))
    hx_rows = hx_rows.reshape(count, total, own)

    stats = jnp.stack([obs_value[:, 0], obs_var[:, 0]], axis=2)
    stats = lax.all_gather(stats, "sub", axis=0)
    stats = lax.dynamic_slice(stats, (0, slab, part, 0, 0), (lines, 1, 1, 2, own))
    stats = stats.reshape(lines, 2, own).astype(F32)
    half = own // 2
    stats = jnp.concatenate(
        [jnp.roll(stats, 1, 0)[:, :, half:], stats, jnp.roll(stats, -1, 0)[:, :, :half]], axis=2
    )
    if groups > 1:
        first = lax.axis_index("sub") // count * count
        stats = lax.dynamic_slice_in_dim(stats, first, count, axis=0)
    taper = (jnp.arange(half, dtype=F32) + 1.0) / (half + 1.0)
    local_weight = jnp.concatenate([taper, jnp.ones((own,), F32), taper[::-1]])
    obs_rows = stats[:, 0:1]
    scale_rows = local_weight / stats[:, 1:2]

    state = exchange(pack_state(member_state, width, owners).reshape(count * owners, local, -1))
    state = state.reshape(count, total, -1)

    held_rows = hx_rows if groups == 1 else widened(hx_rows, count)
    transform = transforms(held_rows, obs_rows, scale_rows, count, groups == 1)

    column = (lax.axis_index("mem") * width + part) * cells_b
    speed = lax.dynamic_slice(courant, (slab, column), (1, cells_b))
    speed = jnp.concatenate([speed] * width, axis=1)
    if groups == 1 and width == 2:
        fields = forecasts(state, transform, speed)
    else:
        fields = shared_transport(analyses(state, transform), speed, width, count)
    back = exchange(fields.reshape(count * owners, local, -1))
    return unpack_state(back.reshape(slabs, width, owners, local, -1), cells_a)


def solution(mesh):
    in_specs = (
        P(None, "mem", "sub", None),
        P(None, "mem", "sub", None, None),
        P(None, "sub", "mem", None),
        P(None, "sub", "mem", None),
        P(),
    )
    out_specs = P(None, "mem", "sub", None)
    return jax.shard_map(advance, mesh=mesh, in_specs=in_specs, out_specs=out_specs, check_vma=False)
```

```python
import jax
import jax.numpy as jnp
from jax import lax
from jax.experimental import pallas as pl
from jax.experimental.pallas import tpu as pltpu
from jax.sharding import PartitionSpec as P

ITERS = 4
STEPS = 4
F32 = jnp.float32
BF16 = jnp.bfloat16
VMEM_LIMIT = 48 * 1024 * 1024
ANY = pl.BlockSpec(memory_space=pl.ANY)


def params(count):
    return pltpu.CompilerParams(
        dimension_semantics=("arbitrary",) * count, vmem_limit_bytes=VMEM_LIMIT
    )


def split(value, size):
    return value >> (size.bit_length() - 1), value & (size - 1)


def iota(rows, cols, dim):
    return lax.broadcasted_iota(jnp.int32, (rows, cols), dim)


def dot_bf16(left, right):
    return jnp.dot(left, right, preferred_element_type=F32)


def moved(left, right):
    return dot_bf16(left, right).astype(BF16)


def ones_at(condition):
    return jnp.where(condition, 1.0, 0.0).astype(BF16)


def start_all(copies):
    for copy in copies:
        copy.start()
    return copies


def wait_all(copies):
    for copy in copies:
        copy.wait()


def place(count):
    return lax.axis_index("sub") & (count - 1), lax.axis_index("mem")


def partners(count, owners):
    column, member = place(count)
    return [
        (r, column ^ (r // owners), member ^ (r % owners)) for r in range(count * owners)
    ]


def send_out(packed, outs, sems):
    count, owners = packed.shape[:2]
    wait_all(
        start_all(
            [
                pltpu.make_async_copy(packed.at[column, member], outs[r], sems.at[r])
                for r, column, member in partners(count, owners)
            ]
        )
    )


def pack_obs_kernel(rows, *rest):
    *outs, order, packed, sems = rest
    _, block, _, patches, own = rows.shape
    owners = packed.shape[1]
    width = patches // owners
    slab, group = pl.program_id(0), pl.program_id(1)
    size = block * patches

    @pl.when((slab == 0) & (group == 0))
    def _():
        rest, member = split(iota(size, size, 0), block)
        part, owner = split(rest, owners)
        order[...] = ones_at(iota(size, size, 1) == member * patches + owner * width + part)

    flat = moved(order[...], rows[...].reshape(size, own))
    here = pl.ds(pl.multiple_of(group * block, block), block)
    packed[pl.ds(slab * width, width), :, here, :] = flat.reshape(width, owners, block, own)

    @pl.when((slab == pl.num_programs(0) - 1) & (group == pl.num_programs(1) - 1))
    def _():
        send_out(packed, outs, sems)


def pack_obs(hx_values, owners):
    slabs, local, _, patches, own = hx_values.shape
    width = patches // owners
    count = slabs * width
    block = 16
    return pl.pallas_call(
        pack_obs_kernel,
        grid=(slabs, local // block),
        in_specs=[pl.BlockSpec((1, block, 1, patches, own), lambda s, g: (s, g, 0, 0, 0))],
        out_specs=[ANY] * (count * owners),
        out_shape=[jax.ShapeDtypeStruct((local, own), BF16)] * (count * owners),
        scratch_shapes=[
            pltpu.VMEM((block * patches, block * patches), BF16),
            pltpu.VMEM((count, owners, local, own), BF16),
            pltpu.SemaphoreType.DMA((count * owners,)),
        ],
        compiler_params=params(2),
        name="pack_obs",
    )(hx_values)


def swapped(width, lanes):
    size = width * lanes
    outer, cell = split(iota(size, size, 1), lanes // width)
    first, second = split(outer, width)
    return ones_at(iota(size, size, 0) == (second * width + first) * (lanes // width) + cell)


def transposed(outer, inner):
    size = outer * inner
    first, second = split(iota(size, size, 0), inner)
    return ones_at(iota(size, size, 1) == second * outer + first)


def pack_state_kernel(cells, _, *rest):
    *outs, order, swap, packed, sems = rest
    owners, _, size = packed.shape[1:]
    block, cells_a, cols = cells.shape[1:]
    lanes = cols // owners
    tiles = size // lanes
    width = cells_a // tiles
    slab, group = pl.program_id(0), pl.program_id(1)

    @pl.when((slab == 0) & (group == 0))
    def _():
        order[...] = transposed(cells_a, block)
        swap[...] = swapped(width, lanes)

    rows = moved(order[...], cells[...].reshape(block * cells_a, cols))
    parts = []
    for owner in range(owners):
        for tile in range(tiles):
            pieces = [
                rows[
                    (half * tiles + tile) * block : (half * tiles + tile + 1) * block,
                    owner * lanes : (owner + 1) * lanes,
                ]
                for half in range(width)
            ]
            parts.append(jnp.concatenate(pieces, axis=1))
    mixed = moved(jnp.concatenate(parts, axis=0), swap[...])
    here = pl.ds(pl.multiple_of(group * block, block), block)
    for owner in range(owners):
        for tile in range(tiles):
            at = (owner * tiles + tile) * block
            for part in range(width):
                packed[slab * width + part, owner, here, tile * lanes : (tile + 1) * lanes] = mixed[
                    at : at + block, part * lanes : (part + 1) * lanes
                ]

    @pl.when((slab == pl.num_programs(0) - 1) & (group == pl.num_programs(1) - 1))
    def _():
        send_out(packed, outs, sems)


def pack_state(member_state, width, owners, after):
    slabs, local, cells_a, cols = member_state.shape
    lanes = cols // owners
    size = cells_a * lanes // width
    count = slabs * width
    block = 32
    return pl.pallas_call(
        pack_state_kernel,
        grid=(slabs, local // block),
        in_specs=[pl.BlockSpec((1, block, cells_a, cols), lambda s, g: (s, g, 0, 0)), ANY],
        out_specs=[ANY] * (count * owners),
        out_shape=[jax.ShapeDtypeStruct((local, size), BF16)] * (count * owners),
        scratch_shapes=[
            pltpu.VMEM((block * cells_a, block * cells_a), BF16),
            pltpu.VMEM((width * lanes, width * lanes), BF16),
            pltpu.VMEM((count, owners, local, size), BF16),
            pltpu.SemaphoreType.DMA((count * owners,)),
        ],
        compiler_params=params(2),
        name="pack_state",
    )(member_state, after)


def unpack_state_kernel(*refs, held):
    blocks = refs[:held]
    out, order, swap, packed, sems = refs[held:]
    count, owners, _, size = packed.shape
    block, cells_a, cols = out.shape[1:]
    lanes = cols // owners
    tiles = size // lanes
    width = cells_a // tiles
    slab, group = pl.program_id(0), pl.program_id(1)

    @pl.when((slab == 0) & (group == 0))
    def _():
        copies = start_all(
            [
                pltpu.make_async_copy(blocks[r], packed.at[column, member], sems.at[r])
                for r, column, member in partners(count, owners)
            ]
        )
        order[...] = transposed(block, cells_a)
        swap[...] = swapped(width, lanes)
        wait_all(copies)

    here = pl.ds(pl.multiple_of(group * block, block), block)
    parts = []
    for owner in range(owners):
        for tile in range(tiles):
            pieces = [
                packed[slab * width + part, owner, here, tile * lanes : (tile + 1) * lanes]
                for part in range(width)
            ]
            parts.append(jnp.concatenate(pieces, axis=1))
    mixed = moved(jnp.concatenate(parts, axis=0), swap[...])
    columns = []
    for owner in range(owners):
        rows = []
        for cell in range(cells_a):
            half, tile = cell // tiles, cell % tiles
            at = (owner * tiles + tile) * block
            rows.append(mixed[at : at + block, half * lanes : (half + 1) * lanes])
        columns.append(jnp.concatenate(rows, axis=0))
    rows = moved(order[...], jnp.concatenate(columns, axis=1))
    out[...] = rows.reshape(out.shape)


def unpack_state(blocks, slabs, width, cells_a):
    local, size = blocks[0].shape
    held = len(blocks)
    owners = held // (slabs * width)
    lanes = size * width // cells_a
    cols = owners * lanes
    block = 32

    def kernel(*refs):
        unpack_state_kernel(*refs, held=held)

    return pl.pallas_call(
        kernel,
        grid=(slabs, local // block),
        in_specs=[ANY] * held,
        out_specs=pl.BlockSpec((1, block, cells_a, cols), lambda s, g: (s, g, 0, 0)),
        out_shape=jax.ShapeDtypeStruct((slabs, local, cells_a, cols), BF16),
        scratch_shapes=[
            pltpu.VMEM((block * cells_a, block * cells_a), BF16),
            pltpu.VMEM((width * lanes, width * lanes), BF16),
            pltpu.VMEM((slabs * width, owners, local, size), BF16),
            pltpu.SemaphoreType.DMA((held,)),
        ],
        compiler_params=params(2),
        name="unpack_state",
    )(*blocks)


def gather_kernel(*refs, held, owners):
    blocks, (out, sems) = refs[:held], refs[held:]
    local = out.shape[1] // owners
    wait_all(
        start_all(
            [
                pltpu.make_async_copy(
                    blocks[r],
                    out.at[patch, pl.ds((r % owners) * local, local)],
                    sems.at[r],
                )
                for r, patch, _ in partners(held // owners, owners)
            ]
        )
    )


def gathered(blocks, count):
    local, size = blocks[0].shape
    held = len(blocks)
    owners = held // count

    def kernel(*refs):
        gather_kernel(*refs, held=held, owners=owners)

    return pl.pallas_call(
        kernel,
        in_specs=[ANY] * held,
        out_specs=ANY,
        out_shape=jax.ShapeDtypeStruct((count, owners * local, size), BF16),
        scratch_shapes=[pltpu.SemaphoreType.DMA((held,))],
        compiler_params=pltpu.CompilerParams(vmem_limit_bytes=VMEM_LIMIT),
        name="gather",
    )(*blocks)


def scatter_kernel(rows, *refs, owners):
    *outs, sems = refs
    local = rows.shape[1] // owners
    wait_all(
        start_all(
            [
                pltpu.make_async_copy(
                    rows.at[patch, pl.ds((r % owners) * local, local)], outs[r], sems.at[r]
                )
                for r, patch, _ in partners(rows.shape[0], owners)
            ]
        )
    )


def scattered(rows, owners):
    count, total, size = rows.shape
    held = count * owners

    def kernel(*refs):
        scatter_kernel(*refs, owners=owners)

    return pl.pallas_call(
        kernel,
        in_specs=[ANY],
        out_specs=[ANY] * held,
        out_shape=[jax.ShapeDtypeStruct((total // owners, size), BF16)] * held,
        scratch_shapes=[pltpu.SemaphoreType.DMA((held,))],
        compiler_params=pltpu.CompilerParams(vmem_limit_bytes=VMEM_LIMIT),
        name="scatter",
    )(rows)


def transform_kernel(before, middle, after, obs, scale, out, pert, weighted):
    total = middle.shape[1]
    half = before.shape[2]
    projected = jnp.zeros((total, 1), F32)
    start = 0
    for part in (before, middle, after):
        span = part.shape[2]
        for at in range(0, span, half):
            cols = slice(start, start + half)
            values = part[0, :, at : at + half].astype(F32)
            mean = jnp.sum(values, axis=0, keepdims=True) * (1.0 / total)
            centred = values - mean
            pert[:, cols] = centred.astype(BF16)
            scaled = (centred * scale[0, :, cols]).astype(BF16)
            weighted[:, cols] = scaled
            innovation = obs[0, :, cols] - mean
            projected += jnp.sum(scaled.astype(F32) * innovation, axis=1, keepdims=True)
            start += half
    diagonal = iota(total, total, 0) == iota(total, total, 1)
    gram = lax.dot_general(
        weighted[...], pert[...], (((1,), (1,)), ((), ())), preferred_element_type=F32
    )
    system = jnp.where(diagonal, total - 1.0, 0.0) + gram
    bound = jnp.max(jnp.sum(jnp.abs(system), axis=1, keepdims=True), axis=0, keepdims=True)
    root = (system / bound).astype(BF16)
    inverse = None
    for iteration in range(ITERS):
        product = root.astype(F32) if inverse is None else dot_bf16(inverse.astype(BF16), root)
        correction = (jnp.where(diagonal, 1.5, 0.0) - 0.5 * product).astype(BF16)
        if iteration + 1 < ITERS:
            root = moved(root, correction)
        if inverse is None:
            inverse = correction.astype(F32)
        else:
            inverse = dot_bf16(correction, inverse.astype(BF16))
    flipped = inverse.T
    halfway = jnp.sum(flipped * projected, axis=0, keepdims=True)
    weight = jnp.sum(inverse * halfway, axis=1, keepdims=True)
    weight = jnp.broadcast_to(weight, (total, 128)).T[0:1, :] / bound
    out[0] = (jnp.sqrt((total - 1.0) / bound) * flipped + weight).astype(BF16)


def transforms(hx_rows, obs_rows, scale_rows, count, wraps):
    held, total, own = hx_rows.shape
    half = own // 2
    shift = 0 if wraps else 1
    flops = count * (2 * total * total * 2 * own + 18 * total**3)
    return pl.pallas_call(
        transform_kernel,
        grid=(count,),
        in_specs=[
            pl.BlockSpec((1, total, half), lambda a: ((a + shift + held - 1) % held, 0, 1)),
            pl.BlockSpec((1, total, own), lambda a: (a + shift, 0, 0)),
            pl.BlockSpec((1, total, half), lambda a: ((a + shift + 1) % held, 0, 0)),
            pl.BlockSpec((1, 1, 2 * own), lambda a: (a, 0, 0)),
            pl.BlockSpec((1, 1, 2 * own), lambda a: (a, 0, 0)),
        ],
        out_specs=pl.BlockSpec((1, total, total), lambda a: (a, 0, 0)),
        out_shape=jax.ShapeDtypeStruct((count, total, total), BF16),
        scratch_shapes=[pltpu.VMEM((total, 2 * own), BF16), pltpu.VMEM((total, 2 * own), BF16)],
        compiler_params=params(1),
        cost_estimate=pl.CostEstimate(
            flops=flops, bytes_accessed=4 * count * total * total * 2, transcendentals=0
        ),
        name="transform",
    )(hx_rows, hx_rows, hx_rows, obs_rows, scale_rows)


def centred(values):
    values = values.astype(F32)
    mean = jnp.sum(values, axis=0, keepdims=True) * (1.0 / values.shape[0])
    return mean, (values - mean).astype(BF16)


def transport(tiles, here, ahead, behind, low):
    count, depth = len(tiles), len(tiles[0])
    shift = tiles[0][0].shape[1] // 2
    for _ in range(STEPS):
        first = [pltpu.roll(column[0], shift, 1) for column in tiles]
        last = [pltpu.roll(column[depth - 1], shift, 1) for column in tiles]
        later = []
        for a in range(count):
            column = []
            for k in range(depth):
                if k + 1 < depth:
                    after = tiles[a][k + 1]
                else:
                    after = jnp.where(low, first[a], first[(a + 1) % count])
                if k > 0:
                    prior = tiles[a][k - 1]
                else:
                    prior = jnp.where(low, last[(a + count - 1) % count], last[a])
                column.append(here * tiles[a][k] + ahead * after + behind * prior)
            later.append(column)
        tiles = later
    return tiles


def forecast_kernel(*refs, held, first, owners):
    blocks, (transform, speed) = refs[:held], refs[held : held + 2]
    outs = refs[held + 2 : -5]
    state, fields, results, in_sems, out_sems = refs[-5:]
    count, total, size = state.shape
    local = total // owners
    lanes = speed.shape[1]
    blocks_from = partners(count, owners)
    copies = start_all(
        [
            pltpu.make_async_copy(
                blocks[r],
                state.at[r // owners, pl.ds((r % owners) * local, local)],
                in_sems.at[r],
            )
            for r in range(held)
        ]
    )
    rows = results.shape[1]
    for near in range(count):
        wait_all(copies[near * owners : (near + 1) * owners])
        patch = blocks_from[near * owners][1]
        mean, pert = centred(state[near])
        fields[patch] = (dot_bf16(transform[patch], pert) + mean).astype(BF16).astype(F32)
    chunk = 16
    c = jnp.broadcast_to(speed[...], (8, lanes))
    here, ahead, behind = 1.0 - c * c, 0.5 * (c * c - c), 0.5 * (c * c + c)
    low = iota(8, lanes, 1) < lanes // 2

    def rows_at(step, carry):
        parts = []
        for half in range(chunk // 8):
            at = pl.ds(pl.multiple_of(step * chunk + half * 8, 8), 8)
            tiles = [
                [fields[a, at, k * lanes : (k + 1) * lanes] for k in range(size // lanes)]
                for a in range(count)
            ]
            parts.append(transport(tiles, here, ahead, behind, low))
        at = pl.ds(pl.multiple_of(step * chunk, chunk), chunk)
        for a in range(count):
            for k in range(size // lanes):
                value = jnp.concatenate([part[a][k] for part in parts], axis=0)
                results[a, at, k * lanes : (k + 1) * lanes] = value.astype(BF16)
        return carry

    sent = []
    for block in range(rows // local):
        lax.fori_loop(block * local // chunk, (block + 1) * local // chunk, rows_at, 0)
        for near in range(count):
            patch = blocks_from[near * owners][1]
            number = near * (rows // local) + block
            sent.append(
                pltpu.make_async_copy(
                    results.at[patch, pl.ds(block * local, local)],
                    outs[number],
                    out_sems.at[number],
                )
            )
            sent[-1].start()
    wait_all(sent)


def forecasts(blocks, transform, speed, owners, first, last):
    count, total, _ = transform.shape
    local, size = blocks[0].shape
    held = len(blocks)
    rows = (last - first) * local

    def kernel(*refs):
        forecast_kernel(*refs, held=held, first=first, owners=owners)

    return pl.pallas_call(
        kernel,
        grid=(1,),
        in_specs=[ANY] * held
        + [
            pl.BlockSpec((count, rows, total), lambda i: (0, first * local // rows, 0)),
            pl.BlockSpec(speed.shape, lambda i: (0, 0)),
        ],
        out_specs=[ANY] * (count * (last - first)),
        out_shape=[jax.ShapeDtypeStruct((local, size), BF16)] * (count * (last - first)),
        scratch_shapes=[
            pltpu.VMEM((count, total, size), BF16),
            pltpu.VMEM((count, rows, size), F32),
            pltpu.VMEM((count, rows, size), BF16),
            pltpu.SemaphoreType.DMA((held,)),
            pltpu.SemaphoreType.DMA((count * (last - first),)),
        ],
        compiler_params=params(1),
        cost_estimate=pl.CostEstimate(
            flops=2 * count * rows * total * size,
            bytes_accessed=4 * held * local * size,
            transcendentals=0,
        ),
        name="forecast",
    )(*blocks, transform, speed)


def analysis_kernel(state, transform, out):
    mean, pert = centred(state[0])
    out[0] = (dot_bf16(transform[0], pert) + mean).astype(BF16)


def analyses(state, transform):
    count, total, size = state.shape
    return pl.pallas_call(
        analysis_kernel,
        grid=(count,),
        in_specs=[
            pl.BlockSpec((1, total, size), lambda a: (a, 0, 0)),
            pl.BlockSpec((1, total, total), lambda a: (a, 0, 0)),
        ],
        out_specs=pl.BlockSpec((1, total, size), lambda a: (a, 0, 0)),
        out_shape=jax.ShapeDtypeStruct((count, total, size), BF16),
        compiler_params=params(1),
        name="analysis",
    )(state, transform)


def shared_transport(analysis, speed, width, jump):
    count, total, size = analysis.shape
    lanes = speed.shape[1]
    cells = lanes // width
    tiles = size // lanes
    fields = widened(analysis, jump).reshape(count + 2, total, tiles, width, cells)
    fields = fields.transpose(1, 0, 3, 2, 4).reshape(total, -1, cells).astype(F32)
    c = speed[0, :cells]
    for _ in range(STEPS):
        prior, here, after = fields[:, :-2], fields[:, 1:-1], fields[:, 2:]
        fields = (1.0 - c * c) * here + 0.5 * (c * c - c) * after + 0.5 * (c * c + c) * prior
    spare = tiles * width - STEPS
    fields = fields[:, spare : fields.shape[1] - spare].astype(BF16)
    fields = fields.reshape(total, count, width, tiles, cells)
    return fields.transpose(1, 0, 3, 2, 4).reshape(count, total, size)


def widened(blocks, jump):
    count = lax.axis_size("sub")
    forward = [(i, (i + jump) % count) for i in range(count)]
    backward = [(target, source) for source, target in forward]
    low = lax.ppermute(blocks[-1:], "sub", forward)
    high = lax.ppermute(blocks[:1], "sub", backward)
    return jnp.concatenate([low, blocks, high], axis=0)


def exchange(blocks, numbers, owners):
    lines = lax.axis_size("sub")
    order = sorted(range(len(blocks)), key=lambda i: -(numbers[i] % owners >= owners // 2))
    received = list(blocks)
    for i in order:
        column, member = numbers[i] // owners, numbers[i] % owners
        if numbers[i] == 0:
            continue
        pairs = [
            (s * owners + m, (s ^ column) * owners + (m ^ member))
            for s in range(lines)
            for m in range(owners)
        ]
        received[i] = lax.ppermute(blocks[i], ("sub", "mem"), pairs)
    return received


def advance(member_state, hx_values, obs_value, obs_var, courant):
    slabs, local, cells_a, cols = member_state.shape
    patches, own = hx_values.shape[3:]
    owners = lax.axis_size("mem")
    lines = lax.axis_size("sub")
    width = patches // owners
    count = slabs * width
    groups = lines // count
    cells_b = cols // patches
    column, member = place(count)
    slab, part = column // width, column % width
    numbers = list(range(count * owners))

    hx_blocks = exchange(pack_obs(hx_values, owners), numbers, owners)

    stats = jnp.stack([obs_value[:, 0], obs_var[:, 0]], axis=2)
    stats = lax.all_gather(stats, "sub", axis=0)
    stats = lax.dynamic_slice(stats, (0, slab, part, 0, 0), (lines, 1, 1, 2, own))
    stats = stats.reshape(lines, 2, own).astype(F32)
    half = own // 2
    stats = jnp.concatenate(
        [jnp.roll(stats, 1, 0)[:, :, half:], stats, jnp.roll(stats, -1, 0)[:, :, :half]], axis=2
    )
    if groups > 1:
        first = lax.axis_index("sub") // count * count
        stats = lax.dynamic_slice_in_dim(stats, first, count, axis=0)
    taper = (jnp.arange(half, dtype=F32) + 1.0) / (half + 1.0)
    local_weight = jnp.concatenate([taper, jnp.ones((own,), F32), taper[::-1]])
    obs_rows = stats[:, 0:1]
    scale_rows = local_weight / stats[:, 1:2]

    packed = pack_state(member_state, width, owners, hx_blocks[owners - 1])
    blocks = exchange(packed, numbers, owners)

    hx_rows = gathered(hx_blocks, count)
    if groups > 1:
        hx_rows = widened(hx_rows, count)
    transform = transforms(hx_rows, obs_rows, scale_rows, count, groups == 1)

    line = (member * width + part) * cells_b
    speed = lax.dynamic_slice(courant, (slab, line), (1, cells_b))
    speed = jnp.concatenate([speed] * width, axis=1)
    if groups == 1 and width == 2:
        middle = owners // 2
        back = [None] * (count * owners)
        for first, last in ((middle, owners), (0, middle)):
            chosen = [r * owners + i for r in range(count) for i in range(first, last)]
            fields = forecasts(blocks, transform, speed, owners, first, last)
            for r, block in zip(chosen, exchange(fields, chosen, owners)):
                back[r] = block
    else:
        fields = shared_transport(
            analyses(gathered(blocks, count), transform), speed, width, count
        )
        back = exchange(scattered(fields, owners), numbers, owners)
    return unpack_state(back, slabs, width, cells_a)


def solution(mesh):
    in_specs = (
        P(None, "mem", "sub", None),
        P(None, "mem", "sub", None, None),
        P(None, "sub", "mem", None),
        P(None, "sub", "mem", None),
        P(),
    )
    out_specs = P(None, "mem", "sub", None)
    return jax.shard_map(advance, mesh=mesh, in_specs=in_specs, out_specs=out_specs, check_vma=False)
```

```python
import jax
import jax.numpy as jnp
from jax import lax
from jax.experimental import pallas as pl
from jax.experimental.pallas import tpu as pltpu
from jax.sharding import PartitionSpec as P

ITERS = 4
STEPS = 4
F32 = jnp.float32
BF16 = jnp.bfloat16
VMEM_LIMIT = 48 * 1024 * 1024


def params(count):
    return pltpu.CompilerParams(
        dimension_semantics=("arbitrary",) * count, vmem_limit_bytes=VMEM_LIMIT
    )


def split(value, size):
    return value >> (size.bit_length() - 1), value & (size - 1)


def iota(rows, cols, dim):
    return lax.broadcasted_iota(jnp.int32, (rows, cols), dim)


def dot_bf16(left, right):
    return jnp.dot(left, right, preferred_element_type=F32)


def moved(left, right):
    return dot_bf16(left, right).astype(BF16)


def ones_at(condition):
    return jnp.where(condition, 1.0, 0.0).astype(BF16)


def pack_obs_kernel(rows, out, order):
    _, width, owners, block, own = out.shape
    size = order.shape[0]
    patches = width * owners

    @pl.when((pl.program_id(0) == 0) & (pl.program_id(1) == 0))
    def _():
        rest, member = split(iota(size, size, 0), block)
        part, owner = split(rest, owners)
        order[...] = ones_at(iota(size, size, 1) == member * patches + owner * width + part)

    out[...] = moved(order[...], rows[...].reshape(size, own)).reshape(out.shape)


def pack_obs(hx_values, width):
    slabs, local, _, patches, own = hx_values.shape
    owners = patches // width
    block = 16
    return pl.pallas_call(
        pack_obs_kernel,
        grid=(slabs, local // block),
        in_specs=[pl.BlockSpec((1, block, 1, patches, own), lambda s, g: (s, g, 0, 0, 0))],
        out_specs=pl.BlockSpec((1, width, owners, block, own), lambda s, g: (s, 0, 0, g, 0)),
        out_shape=jax.ShapeDtypeStruct((slabs, width, owners, local, own), BF16),
        scratch_shapes=[pltpu.VMEM((block * patches, block * patches), BF16)],
        compiler_params=params(2),
        name="pack_obs",
    )(hx_values)


def swapped(width, lanes):
    size = width * lanes
    outer, cell = split(iota(size, size, 1), lanes // width)
    first, second = split(outer, width)
    return ones_at(iota(size, size, 0) == (second * width + first) * (lanes // width) + cell)


def transposed(outer, inner):
    size = outer * inner
    first, second = split(iota(size, size, 0), inner)
    return ones_at(iota(size, size, 1) == second * outer + first)


def pack_state_kernel(cells, out, order, swap):
    _, width, owners, block, size = out.shape
    lanes = cells.shape[3] // owners
    tiles = size // lanes

    @pl.when((pl.program_id(0) == 0) & (pl.program_id(1) == 0))
    def _():
        order[...] = transposed(cells.shape[2], block)
        swap[...] = swapped(width, lanes)

    rows = moved(order[...], cells[...].reshape(order.shape[0], cells.shape[3]))
    parts = []
    for owner in range(owners):
        for tile in range(tiles):
            pieces = [
                rows[
                    (half * tiles + tile) * block : (half * tiles + tile + 1) * block,
                    owner * lanes : (owner + 1) * lanes,
                ]
                for half in range(width)
            ]
            parts.append(jnp.concatenate(pieces, axis=1))
    mixed = moved(jnp.concatenate(parts, axis=0), swap[...])
    for owner in range(owners):
        for tile in range(tiles):
            at = (owner * tiles + tile) * block
            for part in range(width):
                out[0, part, owner, :, tile * lanes : (tile + 1) * lanes] = mixed[
                    at : at + block, part * lanes : (part + 1) * lanes
                ]


def pack_state(member_state, width, owners):
    slabs, local, cells_a, cols = member_state.shape
    lanes = cols // owners
    size = cells_a * lanes // width
    block = 32
    return pl.pallas_call(
        pack_state_kernel,
        grid=(slabs, local // block),
        in_specs=[
            pl.BlockSpec((1, block, cells_a, cols), lambda s, g: (s, g, 0, 0)),
        ],
        out_specs=pl.BlockSpec((1, width, owners, block, size), lambda s, g: (s, 0, 0, g, 0)),
        out_shape=jax.ShapeDtypeStruct((slabs, width, owners, local, size), BF16),
        scratch_shapes=[
            pltpu.VMEM((block * cells_a, block * cells_a), BF16),
            pltpu.VMEM((width * lanes, width * lanes), BF16),
        ],
        compiler_params=params(2),
        name="pack_state",
    )(member_state)


def unpack_state_kernel(packed, out, order, swap):
    _, width, owners, block, size = packed.shape
    cells_a = out.shape[2]
    tiles = cells_a // width
    lanes = size // tiles

    @pl.when((pl.program_id(0) == 0) & (pl.program_id(1) == 0))
    def _():
        order[...] = transposed(block, cells_a)
        swap[...] = swapped(width, lanes)

    parts = []
    for owner in range(owners):
        for tile in range(tiles):
            pieces = [
                packed[0, part, owner, :, tile * lanes : (tile + 1) * lanes]
                for part in range(width)
            ]
            parts.append(jnp.concatenate(pieces, axis=1))
    mixed = moved(jnp.concatenate(parts, axis=0), swap[...])
    columns = []
    for owner in range(owners):
        rows = []
        for cell in range(cells_a):
            half, tile = cell // tiles, cell % tiles
            at = (owner * tiles + tile) * block
            rows.append(mixed[at : at + block, half * lanes : (half + 1) * lanes])
        columns.append(jnp.concatenate(rows, axis=0))
    rows = moved(order[...], jnp.concatenate(columns, axis=1))
    out[...] = rows.reshape(out.shape)


def unpack_state(packed, cells_a):
    slabs, width, owners, local, size = packed.shape
    lanes = size * width // cells_a
    cols = owners * lanes
    block = 32
    return pl.pallas_call(
        unpack_state_kernel,
        grid=(slabs, local // block),
        in_specs=[
            pl.BlockSpec((1, width, owners, block, size), lambda s, g: (s, 0, 0, g, 0)),
        ],
        out_specs=pl.BlockSpec((1, block, cells_a, cols), lambda s, g: (s, g, 0, 0)),
        out_shape=jax.ShapeDtypeStruct((slabs, local, cells_a, cols), BF16),
        scratch_shapes=[
            pltpu.VMEM((block * cells_a, block * cells_a), BF16),
            pltpu.VMEM((width * lanes, width * lanes), BF16),
        ],
        compiler_params=params(2),
        name="unpack_state",
    )(packed)


def transform_kernel(before, middle, after, obs, scale, out, pert, weighted):
    total = middle.shape[1]
    half = before.shape[2]
    projected = jnp.zeros((total, 1), F32)
    start = 0
    for part in (before, middle, after):
        span = part.shape[2]
        for at in range(0, span, half):
            cols = slice(start, start + half)
            values = part[0, :, at : at + half].astype(F32)
            mean = jnp.sum(values, axis=0, keepdims=True) * (1.0 / total)
            centred = values - mean
            pert[:, cols] = centred.astype(BF16)
            scaled = (centred * scale[0, :, cols]).astype(BF16)
            weighted[:, cols] = scaled
            innovation = obs[0, :, cols] - mean
            projected += jnp.sum(scaled.astype(F32) * innovation, axis=1, keepdims=True)
            start += half
    diagonal = iota(total, total, 0) == iota(total, total, 1)
    gram = lax.dot_general(
        weighted[...], pert[...], (((1,), (1,)), ((), ())), preferred_element_type=F32
    )
    system = jnp.where(diagonal, total - 1.0, 0.0) + gram
    bound = jnp.max(jnp.sum(jnp.abs(system), axis=1, keepdims=True), axis=0, keepdims=True)
    root = (system / bound).astype(BF16)
    inverse = None
    for iteration in range(ITERS):
        product = root.astype(F32) if inverse is None else dot_bf16(inverse.astype(BF16), root)
        correction = (jnp.where(diagonal, 1.5, 0.0) - 0.5 * product).astype(BF16)
        if iteration + 1 < ITERS:
            root = moved(root, correction)
        if inverse is None:
            inverse = correction.astype(F32)
        else:
            inverse = dot_bf16(correction, inverse.astype(BF16))
    flipped = inverse.T
    halfway = jnp.sum(flipped * projected, axis=0, keepdims=True)
    weight = jnp.sum(inverse * halfway, axis=1, keepdims=True)
    weight = jnp.broadcast_to(weight, (total, 128)).T[0:1, :] / bound
    out[0] = (jnp.sqrt((total - 1.0) / bound) * flipped + weight).astype(BF16)


def transforms(hx_rows, obs_rows, scale_rows, count, wraps):
    held, total, own = hx_rows.shape
    half = own // 2
    shift = 0 if wraps else 1
    flops = count * (2 * total * total * 2 * own + 18 * total**3)
    return pl.pallas_call(
        transform_kernel,
        grid=(count,),
        in_specs=[
            pl.BlockSpec((1, total, half), lambda a: ((a + shift + held - 1) % held, 0, 1)),
            pl.BlockSpec((1, total, own), lambda a: (a + shift, 0, 0)),
            pl.BlockSpec((1, total, half), lambda a: ((a + shift + 1) % held, 0, 0)),
            pl.BlockSpec((1, 1, 2 * own), lambda a: (a, 0, 0)),
            pl.BlockSpec((1, 1, 2 * own), lambda a: (a, 0, 0)),
        ],
        out_specs=pl.BlockSpec((1, total, total), lambda a: (a, 0, 0)),
        out_shape=jax.ShapeDtypeStruct((count, total, total), BF16),
        scratch_shapes=[pltpu.VMEM((total, 2 * own), BF16), pltpu.VMEM((total, 2 * own), BF16)],
        compiler_params=params(1),
        cost_estimate=pl.CostEstimate(
            flops=flops, bytes_accessed=4 * count * total * total * 2, transcendentals=0
        ),
        name="transform",
    )(hx_rows, hx_rows, hx_rows, obs_rows, scale_rows)


def centred(values):
    values = values.astype(F32)
    mean = jnp.sum(values, axis=0, keepdims=True) * (1.0 / values.shape[0])
    return mean, (values - mean).astype(BF16)


def stencil(c):
    step = [0.5 * (c * c + c), 1.0 - c * c, 0.5 * (c * c - c)]
    taps = step
    for _ in range(STEPS - 1):
        longer = [jnp.zeros_like(c)] * (len(taps) + 2)
        for i, tap in enumerate(taps):
            for j, weight in enumerate(step):
                longer[i + j] = longer[i + j] + tap * weight
        taps = longer
    return taps


def transport(tiles, taps, low):
    count, depth = len(tiles), len(tiles[0])
    shift = tiles[0][0].shape[1] // 2
    turned = [[pltpu.roll(tile, shift, 1) for tile in column] for column in tiles]
    results = []
    for a in range(count):
        before = [jnp.where(low, u, v) for u, v in zip(turned[(a - 1) % count], turned[a])]
        after = [jnp.where(low, u, v) for u, v in zip(turned[a], turned[(a + 1) % count])]
        line = before + tiles[a] + after
        start = depth - STEPS
        results.append(
            [sum(taps[t] * line[start + k + t] for t in range(len(taps))) for k in range(depth)]
        )
    return results


def forecast_kernel(state, transform, speed, out, pert, means, fields):
    count, block, size = out.shape
    lanes = speed.shape[1]

    @pl.when(pl.program_id(0) == 0)
    def _():
        for a in range(count):
            means[a], pert[a] = centred(state[a])

    for a in range(count):
        values = dot_bf16(transform[a], pert[a]) + means[a]
        fields[a] = values.astype(BF16).astype(F32)
    chunk = 16
    taps = stencil(jnp.broadcast_to(speed[...], (8, lanes)))
    low = iota(8, lanes, 1) < lanes // 2

    def rows_at(step, carry):
        parts = []
        for half in range(chunk // 8):
            at = pl.ds(pl.multiple_of(step * chunk + half * 8, 8), 8)
            tiles = [
                [fields[a, at, k * lanes : (k + 1) * lanes] for k in range(size // lanes)]
                for a in range(count)
            ]
            parts.append(transport(tiles, taps, low))
        at = pl.ds(pl.multiple_of(step * chunk, chunk), chunk)
        for a in range(count):
            for k in range(size // lanes):
                value = jnp.concatenate([part[a][k] for part in parts], axis=0)
                out[a, at, k * lanes : (k + 1) * lanes] = value.astype(BF16)
        return carry

    lax.fori_loop(0, block // chunk, rows_at, 0)


def forecasts(state, transform, speed):
    count, total, size = state.shape
    block = min(total, 256)
    return pl.pallas_call(
        forecast_kernel,
        grid=(total // block,),
        in_specs=[
            pl.BlockSpec((count, total, size), lambda i: (0, 0, 0)),
            pl.BlockSpec((count, block, total), lambda i: (0, i, 0)),
            pl.BlockSpec(speed.shape, lambda i: (0, 0)),
        ],
        out_specs=pl.BlockSpec((count, block, size), lambda i: (0, i, 0)),
        out_shape=jax.ShapeDtypeStruct((count, total, size), BF16),
        scratch_shapes=[
            pltpu.VMEM((count, total, size), BF16),
            pltpu.VMEM((count, 1, size), F32),
            pltpu.VMEM((count, block, size), F32),
        ],
        compiler_params=params(1),
        name="forecast",
    )(state, transform, speed)


def analysis_kernel(state, transform, out):
    mean, pert = centred(state[0])
    out[0] = (dot_bf16(transform[0], pert) + mean).astype(BF16)


def analyses(state, transform):
    count, total, size = state.shape
    return pl.pallas_call(
        analysis_kernel,
        grid=(count,),
        in_specs=[
            pl.BlockSpec((1, total, size), lambda a: (a, 0, 0)),
            pl.BlockSpec((1, total, total), lambda a: (a, 0, 0)),
        ],
        out_specs=pl.BlockSpec((1, total, size), lambda a: (a, 0, 0)),
        out_shape=jax.ShapeDtypeStruct((count, total, size), BF16),
        compiler_params=params(1),
        name="analysis",
    )(state, transform)


def shared_transport(analysis, speed, width, jump):
    count, total, size = analysis.shape
    lanes = speed.shape[1]
    cells = lanes // width
    tiles = size // lanes
    fields = widened(analysis, jump).reshape(count + 2, total, tiles, width, cells)
    fields = fields.transpose(1, 0, 3, 2, 4).reshape(total, -1, cells).astype(F32)
    c = speed[0, :cells]
    for _ in range(STEPS):
        prior, here, after = fields[:, :-2], fields[:, 1:-1], fields[:, 2:]
        fields = (1.0 - c * c) * here + 0.5 * (c * c - c) * after + 0.5 * (c * c + c) * prior
    spare = tiles * width - STEPS
    fields = fields[:, spare : fields.shape[1] - spare].astype(BF16)
    fields = fields.reshape(total, count, width, tiles, cells)
    return fields.transpose(1, 0, 3, 2, 4).reshape(count, total, size)


def widened(blocks, jump):
    count = lax.axis_size("sub")
    forward = [(i, (i + jump) % count) for i in range(count)]
    backward = [(target, source) for source, target in forward]
    low = lax.ppermute(blocks[-1:], "sub", forward)
    high = lax.ppermute(blocks[:1], "sub", backward)
    return jnp.concatenate([low, blocks, high], axis=0)


def advance(member_state, hx_values, obs_value, obs_var, courant):
    slabs, local, cells_a, cols = member_state.shape
    patches, own = hx_values.shape[3:]
    owners = lax.axis_size("mem")
    lines = lax.axis_size("sub")
    width = patches // owners
    count = slabs * width
    groups = lines // count
    total = local * owners
    cells_b = cols // patches
    lane_cells = width * cells_b
    place = lax.axis_index("sub") % count
    slab, part = place // width, place % width

    index_groups = None
    if groups > 1:
        held = count * owners
        index_groups = [list(range(g * held, (g + 1) * held)) for g in range(groups)]

    def exchange(blocks):
        return lax.all_to_all(
            blocks,
            ("sub", "mem"),
            split_axis=0,
            concat_axis=0,
            tiled=True,
            axis_index_groups=index_groups,
        )

    hx_rows = exchange(pack_obs(hx_values, width).reshape(count * owners, local, own))
    hx_rows = hx_rows.reshape(count, total, own)

    stats = jnp.stack([obs_value[:, 0], obs_var[:, 0]], axis=2)
    stats = lax.all_gather(stats, "sub", axis=0)
    stats = lax.dynamic_slice(stats, (0, slab, part, 0, 0), (lines, 1, 1, 2, own))
    stats = stats.reshape(lines, 2, own).astype(F32)
    half = own // 2
    stats = jnp.concatenate(
        [jnp.roll(stats, 1, 0)[:, :, half:], stats, jnp.roll(stats, -1, 0)[:, :, :half]], axis=2
    )
    if groups > 1:
        first = lax.axis_index("sub") // count * count
        stats = lax.dynamic_slice_in_dim(stats, first, count, axis=0)
    taper = (jnp.arange(half, dtype=F32) + 1.0) / (half + 1.0)
    local_weight = jnp.concatenate([taper, jnp.ones((own,), F32), taper[::-1]])
    obs_rows = stats[:, 0:1]
    scale_rows = local_weight / stats[:, 1:2]

    state = exchange(pack_state(member_state, width, owners).reshape(count * owners, local, -1))
    state = state.reshape(count, total, -1)

    held_rows = hx_rows if groups == 1 else widened(hx_rows, count)
    transform = transforms(held_rows, obs_rows, scale_rows, count, groups == 1)

    column = (lax.axis_index("mem") * width + part) * cells_b
    speed = lax.dynamic_slice(courant, (slab, column), (1, cells_b))
    speed = jnp.concatenate([speed] * width, axis=1)
    if groups == 1 and width == 2 and cells_a // width >= STEPS:
        fields = forecasts(state, transform, speed)
    else:
        fields = shared_transport(analyses(state, transform), speed, width, count)
    back = exchange(fields.reshape(count * owners, local, -1))
    return unpack_state(back.reshape(slabs, width, owners, local, -1), cells_a)


def solution(mesh):
    in_specs = (
        P(None, "mem", "sub", None),
        P(None, "mem", "sub", None, None),
        P(None, "sub", "mem", None),
        P(None, "sub", "mem", None),
        P(),
    )
    out_specs = P(None, "mem", "sub", None)
    return jax.shard_map(advance, mesh=mesh, in_specs=in_specs, out_specs=out_specs, check_vma=False)
```

```python
import jax
import jax.numpy as jnp
from jax import lax
from jax.experimental import pallas as pl
from jax.experimental.pallas import tpu as pltpu
from jax.sharding import PartitionSpec as P

ITERS = 4
STEPS = 4
PAIR = 2
SPARE = 16
F32 = jnp.float32
BF16 = jnp.bfloat16
VMEM_LIMIT = 60 * 1024 * 1024


def params(count):
    return pltpu.CompilerParams(
        dimension_semantics=("arbitrary",) * count, vmem_limit_bytes=VMEM_LIMIT
    )


def split(value, size):
    return value >> (size.bit_length() - 1), value & (size - 1)


def iota(rows, cols, dim):
    return lax.broadcasted_iota(jnp.int32, (rows, cols), dim)


def dot_bf16(left, right):
    return jnp.dot(left, right, preferred_element_type=F32)


def moved(left, right):
    return dot_bf16(left, right).astype(BF16)


def ones_at(condition):
    return jnp.where(condition, 1.0, 0.0).astype(BF16)


def own_layer():
    return lax.axis_index("mem") >> 1


def own_bit():
    return lax.axis_index("mem") & 1


def pack_obs_kernel(rows, *refs, layers, width, given):
    stats, outs, order = refs[:given], refs[given:-1], refs[-1]
    local, patches, own = rows.shape[1], rows.shape[3], rows.shape[4]
    size = order.shape[0]
    block = size // patches

    @pl.when(pl.program_id(0) == 0)
    def _():
        rest, member = split(iota(size, size, 0), block)
        rest, layer = split(rest, layers)
        part, bit = split(rest, PAIR)
        owner = (layer ^ own_layer()) * PAIR + bit
        order[...] = ones_at(iota(size, size, 1) == member * patches + owner * width + part)

    for at in range(0, local, block):
        flat = moved(order[...], rows[0, at : at + block].reshape(size, own))
        flat = flat.reshape(width * PAIR, layers, block, own)
        for layer in range(layers):
            if stats:
                start = layer * local + at
                outs[0][0, :, start : start + block, :] = flat[:, layer]
            else:
                outs[layer][0, :, at : at + block, :] = flat[:, layer]
    if stats:
        value, variance = (ref[0, 0].astype(F32) for ref in stats)
        line = iota(SPARE, own, 0)
        for part in range(width):
            spare = jnp.where(line == 0, value[part : part + 1], variance[part : part + 1])
            for bit in range(PAIR):
                outs[0][0, part * PAIR + bit, layers * local :, :] = spare.astype(BF16)


def pack_obs(hx_values, layers, piece, stats):
    slabs, members, _, patches, own = hx_values.shape
    width = patches // (layers * PAIR)
    local = members // 2
    block = 16

    def kernel(*refs):
        pack_obs_kernel(*refs, layers=layers, width=width, given=len(stats))

    held = width * PAIR
    shapes = [(held, local, own)] * layers
    if stats:
        shapes = [(held, layers * local + SPARE, own)]
    return pl.pallas_call(
        kernel,
        grid=(slabs,),
        in_specs=[pl.BlockSpec((1, local, 1, patches, own), lambda s: (s, piece, 0, 0, 0))]
        + [pl.BlockSpec((1, 1, width, own), lambda s: (s, 0, 0, 0))] * len(stats),
        out_specs=[pl.BlockSpec((1, *shape), lambda s: (s, 0, 0, 0)) for shape in shapes],
        out_shape=[jax.ShapeDtypeStruct((slabs, *shape), BF16) for shape in shapes],
        scratch_shapes=[pltpu.VMEM((block * patches, block * patches), BF16)],
        compiler_params=params(1),
        name="pack_obs",
    )(hx_values, *stats)


def swapped(width, lanes):
    size = width * lanes
    outer, cell = split(iota(size, size, 1), lanes // width)
    first, second = split(outer, width)
    return ones_at(iota(size, size, 0) == (second * width + first) * (lanes // width) + cell)


def transposed(outer, inner):
    size = outer * inner
    first, second = split(iota(size, size, 0), inner)
    return ones_at(iota(size, size, 1) == second * outer + first)


def pack_state_kernel(cells, out, order, swap):
    _, width, _, layers, block, size = out.shape
    cells_a, cols = cells.shape[2:]
    lanes = cols // (layers * PAIR)
    tiles = size // lanes

    @pl.when((pl.program_id(0) == 0) & (pl.program_id(1) == 0))
    def _():
        order[...] = transposed(cells_a, block)
        swap[...] = swapped(width, lanes)

    rows = moved(order[...], cells[...].reshape(block * cells_a, cols))
    parts = []
    for owner in range(layers * PAIR):
        for tile in range(tiles):
            pieces = [
                rows[
                    (half * tiles + tile) * block : (half * tiles + tile + 1) * block,
                    owner * lanes : (owner + 1) * lanes,
                ]
                for half in range(width)
            ]
            parts.append(jnp.concatenate(pieces, axis=1))
    mixed = moved(jnp.concatenate(parts, axis=0), swap[...])
    for owner in range(layers * PAIR):
        layer = own_layer() ^ (owner // PAIR)
        for tile in range(tiles):
            at = (owner * tiles + tile) * block
            for part in range(width):
                out[0, part, owner % PAIR, layer, :, tile * lanes : (tile + 1) * lanes] = mixed[
                    at : at + block, part * lanes : (part + 1) * lanes
                ]


def pack_state(member_state, layers, width):
    slabs, local, cells_a, cols = member_state.shape
    lanes = cols // (layers * PAIR)
    size = cells_a * lanes // width
    block = 32
    return pl.pallas_call(
        pack_state_kernel,
        grid=(slabs, local // block),
        in_specs=[pl.BlockSpec((1, block, cells_a, cols), lambda s, g: (s, g, 0, 0))],
        out_specs=pl.BlockSpec(
            (1, width, PAIR, layers, block, size), lambda s, g: (s, 0, 0, 0, g, 0)
        ),
        out_shape=jax.ShapeDtypeStruct((slabs, width, PAIR, layers, local, size), BF16),
        scratch_shapes=[
            pltpu.VMEM((block * cells_a, block * cells_a), BF16),
            pltpu.VMEM((width * lanes, width * lanes), BF16),
        ],
        compiler_params=params(2),
        name="pack_state",
    )(member_state)


def unpack_state_kernel(*refs, layers, width):
    blocks = refs[:layers]
    out, order, swap = refs[-3:]
    block, cells_a, cols = out.shape[1:]
    size = blocks[0].shape[2]
    lanes = cols // (layers * PAIR)
    tiles = size // lanes

    @pl.when(pl.program_id(0) == 0)
    def _():
        order[...] = transposed(block, cells_a)
        swap[...] = swapped(width, lanes)

    for layer in range(layers):
        parts = []
        for bit in range(PAIR):
            for tile in range(tiles):
                pieces = [
                    blocks[layer][part * PAIR + bit, :, tile * lanes : (tile + 1) * lanes]
                    for part in range(width)
                ]
                parts.append(jnp.concatenate(pieces, axis=1))
        mixed = moved(jnp.concatenate(parts, axis=0), swap[...])
        columns = []
        for bit in range(PAIR):
            rows = []
            for cell in range(cells_a):
                half, tile = cell // tiles, cell % tiles
                at = (bit * tiles + tile) * block
                rows.append(mixed[at : at + block, half * lanes : (half + 1) * lanes])
            columns.append(jnp.concatenate(rows, axis=0))
        rows = moved(order[...], jnp.concatenate(columns, axis=1))
        span = PAIR * lanes
        at = pl.multiple_of((own_layer() ^ layer) * span, span)
        out[0, :, :, pl.ds(at, span)] = rows.reshape(block, cells_a, span)


def unpack_state(blocks, specs, shape, piece, before):
    slabs, local, cells_a, cols = shape
    block = local // 2
    layers = len(blocks)
    size = blocks[0].shape[2]
    lanes = cols // (layers * PAIR)
    width = cells_a * lanes // size

    def kernel(*refs):
        unpack_state_kernel(*refs, layers=layers, width=width)

    kept = [] if before is None else [before]
    return pl.pallas_call(
        kernel,
        grid=(slabs,),
        in_specs=specs + [pl.BlockSpec(memory_space=pl.ANY)] * len(kept),
        out_specs=pl.BlockSpec((1, block, cells_a, cols), lambda s: (s, piece, 0, 0)),
        out_shape=jax.ShapeDtypeStruct(shape, BF16),
        scratch_shapes=[
            pltpu.VMEM((block * cells_a, block * cells_a), BF16),
            pltpu.VMEM((width * lanes, width * lanes), BF16),
        ],
        input_output_aliases={layers: 0} if kept else {},
        compiler_params=params(1),
        name="unpack_state",
    )(*blocks, *kept)


def transform_kernel(spread, *refs, layers, count, shift):
    seconds = refs[:layers]
    out, pert, weighted = refs[layers:]
    total = out.shape[1]
    own = spread.shape[2]
    half = own // 2
    local = total // (layers * PAIR * 2)
    held = spread.shape[0] // PAIR
    a = pl.program_id(0) + shift
    taper = (iota(1, half, 1).astype(F32) + 1.0) / (half + 1.0)
    fall = (half - iota(1, half, 1).astype(F32)) / (half + 1.0)
    level = jnp.ones((1, half), F32)
    sources = [
        (lax.rem(a + held - 1, held), half, taper),
        (a, 0, level),
        (a, half, level),
        (lax.rem(a + 1, held), 0, fall),
    ]
    projected = jnp.zeros((total, 1), F32)
    for number, (patch, start, weight) in enumerate(sources):
        cols = slice(start, start + half)
        pieces = []
        for layer in range(layers):
            for bit in range(PAIR):
                block = patch * PAIR + bit
                pieces.append(spread[block, layer * local : (layer + 1) * local, cols])
                pieces.append(seconds[layer][block, 0:local, cols])
        values = jnp.concatenate(pieces, axis=0).astype(F32)
        at = layers * local
        stats = seconds[0][patch * PAIR + own_bit(), at : at + SPARE, cols].astype(F32)
        mean = jnp.sum(values, axis=0, keepdims=True) * (1.0 / total)
        centre = values - mean
        place = slice(number * half, (number + 1) * half)
        pert[:, place] = centre.astype(BF16)
        scaled = (centre * (weight / stats[1:2])).astype(BF16)
        weighted[:, place] = scaled
        innovation = stats[0:1] - mean
        projected += jnp.sum(scaled.astype(F32) * innovation, axis=1, keepdims=True)
    diagonal = iota(total, total, 0) == iota(total, total, 1)
    gram = lax.dot_general(
        weighted[...], pert[...], (((1,), (1,)), ((), ())), preferred_element_type=F32
    )
    system = jnp.where(diagonal, total - 1.0, 0.0) + gram
    bound = jnp.max(jnp.sum(jnp.abs(system), axis=1, keepdims=True), axis=0, keepdims=True)
    root = (system / bound).astype(BF16)
    inverse = None
    for iteration in range(ITERS):
        product = root.astype(F32) if inverse is None else dot_bf16(inverse.astype(BF16), root)
        correction = (jnp.where(diagonal, 1.5, 0.0) - 0.5 * product).astype(BF16)
        if iteration + 1 < ITERS:
            root = moved(root, correction)
        if inverse is None:
            inverse = correction.astype(F32)
        else:
            inverse = dot_bf16(correction, inverse.astype(BF16))
    flipped = inverse.T
    halfway = jnp.sum(flipped * projected, axis=0, keepdims=True)
    weight = jnp.sum(inverse * halfway, axis=1, keepdims=True)
    weight = jnp.broadcast_to(weight, (total, 128)).T[0:1, :] / bound
    out[0] = (jnp.sqrt((total - 1.0) / bound) * flipped + weight).astype(BF16)


def transforms(spread, seconds, count):
    layers = len(seconds)
    held, rows, own = spread.shape
    total = rows * PAIR * 2
    shift = (held // PAIR - count) // 2
    flops = count * (2 * total * total * 2 * own + 18 * total**3)

    def kernel(*refs):
        transform_kernel(*refs, layers=layers, count=count, shift=shift)

    return pl.pallas_call(
        kernel,
        grid=(count,),
        in_specs=[
            pl.BlockSpec(array.shape, lambda a: (0, 0, 0)) for array in (spread, *seconds)
        ],
        out_specs=pl.BlockSpec((1, total, total), lambda a: (a, 0, 0)),
        out_shape=jax.ShapeDtypeStruct((count, total, total), BF16),
        scratch_shapes=[pltpu.VMEM((total, 2 * own), BF16), pltpu.VMEM((total, 2 * own), BF16)],
        compiler_params=params(1),
        cost_estimate=pl.CostEstimate(
            flops=flops, bytes_accessed=4 * count * total * total * 2, transcendentals=0
        ),
        name="transform",
    )(spread, *seconds)


def centred(values):
    values = values.astype(F32)
    mean = jnp.sum(values, axis=0, keepdims=True) * (1.0 / values.shape[0])
    return mean, (values - mean).astype(BF16)


def stencil(c):
    step = [0.5 * (c * c + c), 1.0 - c * c, 0.5 * (c * c - c)]
    taps = step
    for _ in range(STEPS - 1):
        longer = [jnp.zeros_like(c)] * (len(taps) + 2)
        for i, tap in enumerate(taps):
            for j, weight in enumerate(step):
                longer[i + j] = longer[i + j] + tap * weight
        taps = longer
    return taps


def transport(tiles, taps, low):
    count, depth = len(tiles), len(tiles[0])
    shift = tiles[0][0].shape[1] // 2
    turned = [[pltpu.roll(tile, shift, 1) for tile in column] for column in tiles]
    results = []
    for a in range(count):
        before = [jnp.where(low, u, v) for u, v in zip(turned[(a - 1) % count], turned[a])]
        after = [jnp.where(low, u, v) for u, v in zip(turned[a], turned[(a + 1) % count])]
        line = before + tiles[a] + after
        start = depth - STEPS
        results.append(
            [sum(taps[t] * line[start + k + t] for t in range(len(taps))) for k in range(depth)]
        )
    return results


def forecast_kernel(*refs, layers, spread):
    blocks, (transform, courant) = refs[:layers], refs[layers : layers + 2]
    outs, fields = refs[layers + 2 : -1], refs[-1]
    count, rows, size = fields.shape
    total = transform.shape[4]
    local = rows // (layers * PAIR)
    a = pl.program_id(0)
    values = jnp.concatenate(
        [block[...].reshape(total // layers, size) for block in blocks], axis=0
    )
    mean, pert = centred(values)
    update = dot_bf16(transform[...].reshape(rows, total), pert)
    fields[a] = (update + mean).astype(BF16).astype(F32)

    @pl.when(a == count - 1)
    def _():
        lanes = courant.shape[1] // (layers * PAIR)
        column = lax.axis_index("sub") & (count - 1)
        slab, part = column // 2, column % 2
        low = iota(8, lanes, 1) < lanes // 2
        at = pl.ds(pl.multiple_of(lax.axis_index("mem") * lanes, lanes), lanes)
        speeds = courant[:, at]
        speed = speeds[0:1]
        for other in range(1, speeds.shape[0]):
            speed = jnp.where(slab == other, speeds[other : other + 1], speed)
        speed = jnp.broadcast_to(speed, (8, lanes))
        speed = jnp.where(low == (part == 0), speed, pltpu.roll(speed, lanes // 2, 1))
        taps = stencil(speed)
        chunk = 16
        steps = local // chunk
        for layer in range(layers):

            def rows_at(step, carry):
                bit, inside = step // steps, step % steps
                start = (layer * PAIR + bit) * local + inside * chunk
                parts = []
                for half in range(chunk // 8):
                    at = pl.ds(pl.multiple_of(start + half * 8, 8), 8)
                    tiles = [
                        [fields[a, at, k * lanes : (k + 1) * lanes] for k in range(size // lanes)]
                        for a in range(count)
                    ]
                    parts.append(transport(tiles, taps, low))
                to = inside * chunk + (layer * local if spread else 0)
                at = pl.ds(pl.multiple_of(to, chunk), chunk)
                out = outs[0] if spread else outs[layer]
                for a in range(count):
                    for k in range(size // lanes):
                        value = jnp.concatenate([part[a][k] for part in parts], axis=0)
                        out[a * PAIR + bit, at, k * lanes : (k + 1) * lanes] = value.astype(BF16)
                return carry

            lax.fori_loop(0, PAIR * steps, rows_at, 0)


def forecasts(own_blocks, blocks, transform, courant, piece):
    held, layers, local, size = own_blocks.shape
    count = held // PAIR
    total = transform.shape[2]
    half = local // 2
    transform = transform.reshape(count, layers * PAIR, 2, half, total)
    shapes = [(held, half, size)] * layers
    if piece == 1:
        shapes = [(held, layers * half, size)]

    def kernel(*refs):
        forecast_kernel(*refs, layers=layers, spread=piece == 1)

    return pl.pallas_call(
        kernel,
        grid=(count,),
        in_specs=[
            pl.BlockSpec((PAIR, 1, local, size), lambda a: (a, 0, 0, 0)),
            *[pl.BlockSpec((PAIR, local, size), lambda a: (a, 0, 0)) for _ in blocks],
            pl.BlockSpec(
                (1, layers * PAIR, 1, half, total), lambda a: (a, 0, piece, 0, 0)
            ),
            pl.BlockSpec(courant.shape, lambda a: (0, 0)),
        ],
        out_specs=[pl.BlockSpec(shape, lambda a: (0, 0, 0)) for shape in shapes],
        out_shape=[jax.ShapeDtypeStruct(shape, BF16) for shape in shapes],
        scratch_shapes=[pltpu.VMEM((count, total // 2, size), F32)],
        compiler_params=params(1),
        cost_estimate=pl.CostEstimate(
            flops=count * total * total * size, bytes_accessed=4 * total * size * count, transcendentals=0
        ),
        name="forecast",
    )(own_blocks, *blocks, transform, courant)


def analysis_kernel(state, transform, out):
    mean, pert = centred(state[0])
    out[0] = (dot_bf16(transform[0], pert) + mean).astype(BF16)


def analyses(state, transform):
    count, total, size = state.shape
    return pl.pallas_call(
        analysis_kernel,
        grid=(count,),
        in_specs=[
            pl.BlockSpec((1, total, size), lambda a: (a, 0, 0)),
            pl.BlockSpec((1, total, total), lambda a: (a, 0, 0)),
        ],
        out_specs=pl.BlockSpec((1, total, size), lambda a: (a, 0, 0)),
        out_shape=jax.ShapeDtypeStruct((count, total, size), BF16),
        compiler_params=params(1),
        name="analysis",
    )(state, transform)


def shared_transport(analysis, speed, width, jump):
    count, total, size = analysis.shape
    lanes = speed.shape[1]
    cells = lanes // width
    tiles = size // lanes
    fields = widened(analysis, jump).reshape(count + 2, total, tiles, width, cells)
    fields = fields.transpose(1, 0, 3, 2, 4).reshape(total, -1, cells).astype(F32)
    c = speed[0, :cells]
    for _ in range(STEPS):
        prior, here, after = fields[:, :-2], fields[:, 1:-1], fields[:, 2:]
        fields = (1.0 - c * c) * here + 0.5 * (c * c - c) * after + 0.5 * (c * c + c) * prior
    spare = tiles * width - STEPS
    fields = fields[:, spare : fields.shape[1] - spare].astype(BF16)
    fields = fields.reshape(total, count, width, tiles, cells)
    return fields.transpose(1, 0, 3, 2, 4).reshape(count, total, size)


def widened(blocks, jump):
    count = lax.axis_size("sub")
    forward = [(i, (i + jump) % count) for i in range(count)]
    backward = [(target, source) for source, target in forward]
    span = blocks.shape[0] // jump
    low = lax.ppermute(blocks[-span:], "sub", forward)
    high = lax.ppermute(blocks[:span], "sub", backward)
    return jnp.concatenate([low, blocks, high], axis=0)


def advance(member_state, hx_values, obs_value, obs_var, courant):
    slabs, local, cells_a, cols = member_state.shape
    patches, own = hx_values.shape[3:]
    owners = lax.axis_size("mem")
    lines = lax.axis_size("sub")
    layers = owners // PAIR
    width = patches // owners
    count = slabs * width
    held = count * PAIR
    half = local // 2
    shared = lines > count
    cells_b = cols // patches
    far_first = range(layers - 1, 0, -1)

    layer_groups = [
        [s * owners + layer * PAIR + bit for s in range(g, g + count) for bit in range(PAIR)]
        for g in range(0, lines, count)
        for layer in range(layers)
    ]

    def within(blocks):
        return lax.all_to_all(
            blocks,
            ("sub", "mem"),
            split_axis=0,
            concat_axis=0,
            tiled=True,
            axis_index_groups=layer_groups,
        )

    def across(blocks):
        received = list(blocks)
        for layer in far_first:
            pairs = [
                (s * owners + m, s * owners + (m ^ (layer * PAIR)))
                for s in range(lines)
                for m in range(owners)
            ]
            received[layer] = lax.ppermute(blocks[layer], ("sub", "mem"), pairs)
        return received

    def layered(blocks, rows):
        return [blocks[:, layer * rows : (layer + 1) * rows] for layer in range(layers)]

    first = pack_obs(hx_values, layers, 0, ())
    first = across([block.reshape(held, half, own) for block in first])
    (second,) = pack_obs(hx_values, layers, 1, (obs_value, obs_var))
    second = within(second.reshape(held, -1, own))
    seconds = [second] + across(layered(second, half))[1:]
    state = pack_state(member_state, layers, width)
    size = state.shape[5]
    state = within(state.reshape(held, layers * local, size))
    states = across(layered(state, local))
    first = within(jnp.concatenate(first, axis=1))
    observed = [first, *seconds]
    if shared:
        observed = [widened(array, count) for array in observed]
    transform = transforms(observed[0], observed[1:], count)

    if not shared and width == 2 and cells_a // width >= STEPS:
        state = state.reshape(held, layers, local, size)
        back = forecasts(state, states[1:], transform, courant, 0)
        (last,) = forecasts(state, states[1:], transform, courant, 1)
    else:
        column = lax.axis_index("sub") % count
        line = (lax.axis_index("mem") * width + column % width) * cells_b
        speed = lax.dynamic_slice(courant, (column // width, line), (1, cells_b))
        speed = jnp.concatenate([speed] * width, axis=1)
        states = [block.reshape(count, PAIR * local, size) for block in states]
        analysis = analyses(jnp.concatenate(states, axis=1), transform)
        fields = shared_transport(analysis, speed, width, count)
        fields = fields.reshape(count, layers, PAIR, 2, half, size)
        fields = fields.transpose(3, 0, 2, 1, 4, 5).reshape(2, held, layers, half, size)
        back = [fields[0, :, layer] for layer in range(layers)]
        last = fields[1].reshape(held, layers * half, size)
    back = within(jnp.concatenate(across(back), axis=1))
    last = within(last)
    lasts = across(layered(last, half))

    def spec(layer):
        return pl.BlockSpec((width * PAIR, half, size), lambda s: (s, layer, 0))

    shape = member_state.shape
    done = unpack_state([back] * layers, [spec(i) for i in range(layers)], shape, 0, None)
    return unpack_state([last, *lasts[1:]], [spec(0)] * layers, shape, 1, done)


def solution(mesh):
    in_specs = (
        P(None, "mem", "sub", None),
        P(None, "mem", "sub", None, None),
        P(None, "sub", "mem", None),
        P(None, "sub", "mem", None),
        P(),
    )
    out_specs = P(None, "mem", "sub", None)
    return jax.shard_map(advance, mesh=mesh, in_specs=in_specs, out_specs=out_specs, check_vma=False)
```

```python
import jax
import jax.numpy as jnp
from jax import lax
from jax.experimental import pallas as pl
from jax.experimental.pallas import tpu as pltpu
from jax.sharding import PartitionSpec as P

ITERS = 4
STEPS = 4
PAIR = 2
SPARE = 16
F32 = jnp.float32
BF16 = jnp.bfloat16
VMEM_LIMIT = 60 * 1024 * 1024
ANY = pl.BlockSpec(memory_space=pl.ANY)


def params(count):
    return pltpu.CompilerParams(
        dimension_semantics=("arbitrary",) * count, vmem_limit_bytes=VMEM_LIMIT
    )


def split(value, size):
    return value >> (size.bit_length() - 1), value & (size - 1)


def iota(rows, cols, dim):
    return lax.broadcasted_iota(jnp.int32, (rows, cols), dim)


def dot_bf16(left, right):
    return jnp.dot(left, right, preferred_element_type=F32)


def moved(left, right):
    return dot_bf16(left, right).astype(BF16)


def ones_at(condition):
    return jnp.where(condition, 1.0, 0.0).astype(BF16)


def own_layer():
    return lax.axis_index("mem") >> 1


def own_bit():
    return lax.axis_index("mem") & 1


def pack_obs_kernel(rows, *refs, layers, width, given):
    stats, outs, order = refs[:given], refs[given:-1], refs[-1]
    local, patches, own = rows.shape[1], rows.shape[3], rows.shape[4]
    size = order.shape[0]
    block = size // patches

    @pl.when(pl.program_id(0) == 0)
    def _():
        rest, member = split(iota(size, size, 0), block)
        rest, layer = split(rest, layers)
        part, bit = split(rest, PAIR)
        owner = (layer ^ own_layer()) * PAIR + bit
        order[...] = ones_at(iota(size, size, 1) == member * patches + owner * width + part)

    for at in range(0, local, block):
        flat = moved(order[...], rows[0, at : at + block].reshape(size, own))
        flat = flat.reshape(width * PAIR, layers, block, own)
        for layer in range(layers):
            if stats:
                start = layer * local + at
                outs[0][0, :, start : start + block, :] = flat[:, layer]
            else:
                outs[layer][0, :, at : at + block, :] = flat[:, layer]
    if stats:
        value, variance = (ref[0, 0].astype(F32) for ref in stats)
        line = iota(SPARE, own, 0)
        for part in range(width):
            spare = jnp.where(line == 0, value[part : part + 1], variance[part : part + 1])
            for bit in range(PAIR):
                outs[0][0, part * PAIR + bit, layers * local :, :] = spare.astype(BF16)


def pack_obs(hx_values, layers, piece, stats, after):
    slabs, members, _, patches, own = hx_values.shape
    width = patches // (layers * PAIR)
    local = members // 2
    block = 16

    def kernel(*refs):
        kept = refs[: 1 + len(stats)] + refs[1 + len(stats) + len(after) :]
        pack_obs_kernel(*kept, layers=layers, width=width, given=len(stats))

    held = width * PAIR
    shapes = [(held, local, own)] * layers
    if stats:
        shapes = [(held, layers * local + SPARE, own)]
    return pl.pallas_call(
        kernel,
        grid=(slabs,),
        in_specs=[pl.BlockSpec((1, local, 1, patches, own), lambda s: (s, piece, 0, 0, 0))]
        + [pl.BlockSpec((1, 1, width, own), lambda s: (s, 0, 0, 0))] * len(stats)
        + [ANY] * len(after),
        out_specs=[pl.BlockSpec((1, *shape), lambda s: (s, 0, 0, 0)) for shape in shapes],
        out_shape=[jax.ShapeDtypeStruct((slabs, *shape), BF16) for shape in shapes],
        scratch_shapes=[pltpu.VMEM((block * patches, block * patches), BF16)],
        compiler_params=params(1),
        name="pack_obs",
    )(hx_values, *stats, *after)


def swapped(width, lanes):
    size = width * lanes
    outer, cell = split(iota(size, size, 1), lanes // width)
    first, second = split(outer, width)
    return ones_at(iota(size, size, 0) == (second * width + first) * (lanes // width) + cell)


def transposed(outer, inner):
    size = outer * inner
    first, second = split(iota(size, size, 0), inner)
    return ones_at(iota(size, size, 1) == second * outer + first)


def pack_state_kernel(cells, out, order, swap):
    _, width, _, layers, block, size = out.shape
    cells_a, cols = cells.shape[2:]
    lanes = cols // (layers * PAIR)
    tiles = size // lanes

    @pl.when((pl.program_id(0) == 0) & (pl.program_id(1) == 0))
    def _():
        order[...] = transposed(cells_a, block)
        swap[...] = swapped(width, lanes)

    rows = moved(order[...], cells[...].reshape(block * cells_a, cols))
    parts = []
    for owner in range(layers * PAIR):
        for tile in range(tiles):
            pieces = [
                rows[
                    (half * tiles + tile) * block : (half * tiles + tile + 1) * block,
                    owner * lanes : (owner + 1) * lanes,
                ]
                for half in range(width)
            ]
            parts.append(jnp.concatenate(pieces, axis=1))
    mixed = moved(jnp.concatenate(parts, axis=0), swap[...])
    for owner in range(layers * PAIR):
        layer = own_layer() ^ (owner // PAIR)
        for tile in range(tiles):
            at = (owner * tiles + tile) * block
            for part in range(width):
                out[0, part, owner % PAIR, layer, :, tile * lanes : (tile + 1) * lanes] = mixed[
                    at : at + block, part * lanes : (part + 1) * lanes
                ]


def pack_state(member_state, layers, width, after):
    slabs, local, cells_a, cols = member_state.shape
    lanes = cols // (layers * PAIR)
    size = cells_a * lanes // width
    block = 32

    def kernel(*refs):
        pack_state_kernel(refs[0], *refs[1 + len(after) :])

    return pl.pallas_call(
        kernel,
        grid=(slabs, local // block),
        in_specs=[pl.BlockSpec((1, block, cells_a, cols), lambda s, g: (s, g, 0, 0))]
        + [ANY] * len(after),
        out_specs=pl.BlockSpec(
            (1, width, PAIR, layers, block, size), lambda s, g: (s, 0, 0, 0, g, 0)
        ),
        out_shape=jax.ShapeDtypeStruct((slabs, width, PAIR, layers, local, size), BF16),
        scratch_shapes=[
            pltpu.VMEM((block * cells_a, block * cells_a), BF16),
            pltpu.VMEM((width * lanes, width * lanes), BF16),
        ],
        compiler_params=params(2),
        name="pack_state",
    )(member_state, *after)


def unpack_state_kernel(packed, out, order, swap):
    _, width, owners, block, size = packed.shape
    cells_a = out.shape[2]
    tiles = cells_a // width
    lanes = size // tiles

    @pl.when((pl.program_id(0) == 0) & (pl.program_id(1) == 0))
    def _():
        order[...] = transposed(block, cells_a)
        swap[...] = swapped(width, lanes)

    parts = []
    for owner in range(owners):
        for tile in range(tiles):
            pieces = [
                packed[0, part, owner, :, tile * lanes : (tile + 1) * lanes]
                for part in range(width)
            ]
            parts.append(jnp.concatenate(pieces, axis=1))
    mixed = moved(jnp.concatenate(parts, axis=0), swap[...])
    columns = []
    for owner in range(owners):
        rows = []
        for cell in range(cells_a):
            half, tile = cell // tiles, cell % tiles
            at = (owner * tiles + tile) * block
            rows.append(mixed[at : at + block, half * lanes : (half + 1) * lanes])
        columns.append(jnp.concatenate(rows, axis=0))
    rows = moved(order[...], jnp.concatenate(columns, axis=1))
    out[...] = rows.reshape(out.shape)


def unpack_state(packed, cells_a):
    slabs, width, owners, local, size = packed.shape
    lanes = size * width // cells_a
    cols = owners * lanes
    block = 32
    return pl.pallas_call(
        unpack_state_kernel,
        grid=(slabs, local // block),
        in_specs=[
            pl.BlockSpec((1, width, owners, block, size), lambda s, g: (s, 0, 0, g, 0)),
        ],
        out_specs=pl.BlockSpec((1, block, cells_a, cols), lambda s, g: (s, g, 0, 0)),
        out_shape=jax.ShapeDtypeStruct((slabs, local, cells_a, cols), BF16),
        scratch_shapes=[
            pltpu.VMEM((block * cells_a, block * cells_a), BF16),
            pltpu.VMEM((width * lanes, width * lanes), BF16),
        ],
        compiler_params=params(2),
        name="unpack_state",
    )(packed)


def join_kernel(*refs, layers):
    out, sems = refs[-2:]
    rows = out.shape[1] // layers
    copies = [
        pltpu.make_async_copy(
            refs[layer], out.at[:, pl.ds(layer * rows, rows), :], sems.at[layer]
        )
        for layer in range(layers)
    ]
    for copy in copies:
        copy.start()
    for copy in copies:
        copy.wait()


def join(blocks, after):
    layers = len(blocks)
    held, rows, size = blocks[0].shape

    def kernel(*refs):
        join_kernel(*refs, layers=layers)

    return pl.pallas_call(
        kernel,
        in_specs=[ANY] * (layers + len(after)),
        out_specs=ANY,
        out_shape=jax.ShapeDtypeStruct((held, layers * rows, size), BF16),
        scratch_shapes=[pltpu.SemaphoreType.DMA((layers,))],
        compiler_params=pltpu.CompilerParams(vmem_limit_bytes=VMEM_LIMIT),
        name="join",
    )(*blocks, *after)


def transform_kernel(spread, *refs, layers, count, shift):
    seconds = refs[:layers]
    out, pert, weighted = refs[layers:]
    total = out.shape[1]
    own = spread.shape[2]
    half = own // 2
    local = total // (layers * PAIR * 2)
    held = spread.shape[0] // PAIR
    a = pl.program_id(0) + shift
    taper = (iota(1, half, 1).astype(F32) + 1.0) / (half + 1.0)
    fall = (half - iota(1, half, 1).astype(F32)) / (half + 1.0)
    level = jnp.ones((1, half), F32)
    sources = [
        (lax.rem(a + held - 1, held), half, taper),
        (a, 0, level),
        (a, half, level),
        (lax.rem(a + 1, held), 0, fall),
    ]
    projected = jnp.zeros((total, 1), F32)
    for number, (patch, start, weight) in enumerate(sources):
        cols = slice(start, start + half)
        pieces = []
        for layer in range(layers):
            for bit in range(PAIR):
                block = patch * PAIR + bit
                pieces.append(spread[block, layer * local : (layer + 1) * local, cols])
                pieces.append(seconds[layer][block, 0:local, cols])
        values = jnp.concatenate(pieces, axis=0).astype(F32)
        at = layers * local
        stats = seconds[0][patch * PAIR + own_bit(), at : at + SPARE, cols].astype(F32)
        mean = jnp.sum(values, axis=0, keepdims=True) * (1.0 / total)
        centre = values - mean
        place = slice(number * half, (number + 1) * half)
        pert[:, place] = centre.astype(BF16)
        scaled = (centre * (weight / stats[1:2])).astype(BF16)
        weighted[:, place] = scaled
        innovation = stats[0:1] - mean
        projected += jnp.sum(scaled.astype(F32) * innovation, axis=1, keepdims=True)
    diagonal = iota(total, total, 0) == iota(total, total, 1)
    gram = lax.dot_general(
        weighted[...], pert[...], (((1,), (1,)), ((), ())), preferred_element_type=F32
    )
    system = jnp.where(diagonal, total - 1.0, 0.0) + gram
    bound = jnp.max(jnp.sum(jnp.abs(system), axis=1, keepdims=True), axis=0, keepdims=True)
    root = (system / bound).astype(BF16)
    inverse = None
    for iteration in range(ITERS):
        product = root.astype(F32) if inverse is None else dot_bf16(inverse.astype(BF16), root)
        correction = (jnp.where(diagonal, 1.5, 0.0) - 0.5 * product).astype(BF16)
        if iteration + 1 < ITERS:
            root = moved(root, correction)
        if inverse is None:
            inverse = correction.astype(F32)
        else:
            inverse = dot_bf16(correction, inverse.astype(BF16))
    flipped = inverse.T
    halfway = jnp.sum(flipped * projected, axis=0, keepdims=True)
    weight = jnp.sum(inverse * halfway, axis=1, keepdims=True)
    weight = jnp.broadcast_to(weight, (total, 128)).T[0:1, :] / bound
    out[0] = (jnp.sqrt((total - 1.0) / bound) * flipped + weight).astype(BF16)


def transforms(spread, seconds, count):
    layers = len(seconds)
    held, rows, own = spread.shape
    total = rows * PAIR * 2
    shift = (held // PAIR - count) // 2
    flops = count * (2 * total * total * 2 * own + 18 * total**3)

    def kernel(*refs):
        transform_kernel(*refs, layers=layers, count=count, shift=shift)

    return pl.pallas_call(
        kernel,
        grid=(count,),
        in_specs=[
            pl.BlockSpec(array.shape, lambda a: (0, 0, 0)) for array in (spread, *seconds)
        ],
        out_specs=pl.BlockSpec((1, total, total), lambda a: (a, 0, 0)),
        out_shape=jax.ShapeDtypeStruct((count, total, total), BF16),
        scratch_shapes=[pltpu.VMEM((total, 2 * own), BF16), pltpu.VMEM((total, 2 * own), BF16)],
        compiler_params=params(1),
        cost_estimate=pl.CostEstimate(
            flops=flops, bytes_accessed=4 * count * total * total * 2, transcendentals=0
        ),
        name="transform",
    )(spread, *seconds)


def centred(values):
    values = values.astype(F32)
    mean = jnp.sum(values, axis=0, keepdims=True) * (1.0 / values.shape[0])
    return mean, (values - mean).astype(BF16)


def stencil(c):
    step = [0.5 * (c * c + c), 1.0 - c * c, 0.5 * (c * c - c)]
    taps = step
    for _ in range(STEPS - 1):
        longer = [jnp.zeros_like(c)] * (len(taps) + 2)
        for i, tap in enumerate(taps):
            for j, weight in enumerate(step):
                longer[i + j] = longer[i + j] + tap * weight
        taps = longer
    return taps


def transport(tiles, taps, low):
    count, depth = len(tiles), len(tiles[0])
    shift = tiles[0][0].shape[1] // 2
    turned = [[pltpu.roll(tile, shift, 1) for tile in column] for column in tiles]
    results = []
    for a in range(count):
        before = [jnp.where(low, u, v) for u, v in zip(turned[(a - 1) % count], turned[a])]
        after = [jnp.where(low, u, v) for u, v in zip(turned[a], turned[(a + 1) % count])]
        line = before + tiles[a] + after
        start = depth - STEPS
        results.append(
            [sum(taps[t] * line[start + k + t] for t in range(len(taps))) for k in range(depth)]
        )
    return results


def forecast_kernel(*refs, layers):
    blocks, (transform, courant) = refs[:layers], refs[layers : layers + 2]
    out, fields = refs[-2:]
    count, total, size = fields.shape
    local = total // (layers * PAIR)
    a = pl.program_id(0)
    values = jnp.concatenate(
        [block[...].reshape(total // layers, size) for block in blocks], axis=0
    )
    mean, pert = centred(values)
    update = dot_bf16(transform[0], pert)
    fields[a] = (update + mean).astype(BF16).astype(F32)

    @pl.when(a == count - 1)
    def _():
        lanes = courant.shape[1] // (layers * PAIR)
        column = lax.axis_index("sub") & (count - 1)
        slab, part = column // 2, column % 2
        low = iota(8, lanes, 1) < lanes // 2
        at = pl.ds(pl.multiple_of(lax.axis_index("mem") * lanes, lanes), lanes)
        speeds = courant[:, at]
        speed = speeds[0:1]
        for other in range(1, speeds.shape[0]):
            speed = jnp.where(slab == other, speeds[other : other + 1], speed)
        speed = jnp.broadcast_to(speed, (8, lanes))
        speed = jnp.where(low == (part == 0), speed, pltpu.roll(speed, lanes // 2, 1))
        taps = stencil(speed)
        chunk = 16
        steps = local // chunk
        for layer in range(layers):

            def rows_at(step, carry):
                bit, inside = step // steps, step % steps
                start = (layer * PAIR + bit) * local + inside * chunk
                parts = []
                for half in range(chunk // 8):
                    at = pl.ds(pl.multiple_of(start + half * 8, 8), 8)
                    tiles = [
                        [fields[a, at, k * lanes : (k + 1) * lanes] for k in range(size // lanes)]
                        for a in range(count)
                    ]
                    parts.append(transport(tiles, taps, low))
                at = pl.ds(pl.multiple_of(inside * chunk, chunk), chunk)
                owner = (own_layer() ^ layer) * PAIR + bit
                for a in range(count):
                    for k in range(size // lanes):
                        value = jnp.concatenate([part[a][k] for part in parts], axis=0)
                        out[a, owner, at, k * lanes : (k + 1) * lanes] = value.astype(BF16)
                return carry

            lax.fori_loop(0, PAIR * steps, rows_at, 0)


def forecasts(own_blocks, blocks, transform, courant):
    held, layers, local, size = own_blocks.shape
    count, total, _ = transform.shape
    owners = layers * PAIR

    def kernel(*refs):
        forecast_kernel(*refs, layers=layers)

    return pl.pallas_call(
        kernel,
        grid=(count,),
        in_specs=[
            pl.BlockSpec((PAIR, 1, local, size), lambda a: (a, 0, 0, 0)),
            *[pl.BlockSpec((PAIR, local, size), lambda a: (a, 0, 0)) for _ in blocks],
            pl.BlockSpec((1, total, total), lambda a: (a, 0, 0)),
            pl.BlockSpec(courant.shape, lambda a: (0, 0)),
        ],
        out_specs=pl.BlockSpec((count, owners, local, size), lambda a: (0, 0, 0, 0)),
        out_shape=jax.ShapeDtypeStruct((count, owners, local, size), BF16),
        scratch_shapes=[pltpu.VMEM((count, total, size), F32)],
        compiler_params=params(1),
        name="forecast",
    )(own_blocks, *blocks, transform, courant)


def analysis_kernel(state, transform, out):
    mean, pert = centred(state[0])
    out[0] = (dot_bf16(transform[0], pert) + mean).astype(BF16)


def analyses(state, transform):
    count, total, size = state.shape
    return pl.pallas_call(
        analysis_kernel,
        grid=(count,),
        in_specs=[
            pl.BlockSpec((1, total, size), lambda a: (a, 0, 0)),
            pl.BlockSpec((1, total, total), lambda a: (a, 0, 0)),
        ],
        out_specs=pl.BlockSpec((1, total, size), lambda a: (a, 0, 0)),
        out_shape=jax.ShapeDtypeStruct((count, total, size), BF16),
        compiler_params=params(1),
        name="analysis",
    )(state, transform)


def shared_transport(analysis, speed, width, jump):
    count, total, size = analysis.shape
    lanes = speed.shape[1]
    cells = lanes // width
    tiles = size // lanes
    fields = widened(analysis, jump).reshape(count + 2, total, tiles, width, cells)
    fields = fields.transpose(1, 0, 3, 2, 4).reshape(total, -1, cells).astype(F32)
    c = speed[0, :cells]
    for _ in range(STEPS):
        prior, here, after = fields[:, :-2], fields[:, 1:-1], fields[:, 2:]
        fields = (1.0 - c * c) * here + 0.5 * (c * c - c) * after + 0.5 * (c * c + c) * prior
    spare = tiles * width - STEPS
    fields = fields[:, spare : fields.shape[1] - spare].astype(BF16)
    fields = fields.reshape(total, count, width, tiles, cells)
    return fields.transpose(1, 0, 3, 2, 4).reshape(count, total, size)


def widened(blocks, jump):
    count = lax.axis_size("sub")
    forward = [(i, (i + jump) % count) for i in range(count)]
    backward = [(target, source) for source, target in forward]
    span = blocks.shape[0] // jump
    low = lax.ppermute(blocks[-span:], "sub", forward)
    high = lax.ppermute(blocks[:span], "sub", backward)
    return jnp.concatenate([low, blocks, high], axis=0)


def advance(member_state, hx_values, obs_value, obs_var, courant):
    slabs, local, cells_a, cols = member_state.shape
    patches, own = hx_values.shape[3:]
    owners = lax.axis_size("mem")
    lines = lax.axis_size("sub")
    layers = owners // PAIR
    width = patches // owners
    count = slabs * width
    held = count * PAIR
    half = local // 2
    shared = lines > count
    cells_b = cols // patches
    far_first = range(layers - 1, 0, -1)

    layer_groups = [
        [s * owners + layer * PAIR + bit for s in range(g, g + count) for bit in range(PAIR)]
        for g in range(0, lines, count)
        for layer in range(layers)
    ]

    def within(blocks):
        return lax.all_to_all(
            blocks,
            ("sub", "mem"),
            split_axis=0,
            concat_axis=0,
            tiled=True,
            axis_index_groups=layer_groups,
        )

    def across(blocks):
        received = list(blocks)
        for layer in far_first:
            pairs = [
                (s * owners + m, s * owners + (m ^ (layer * PAIR)))
                for s in range(lines)
                for m in range(owners)
            ]
            received[layer] = lax.ppermute(blocks[layer], ("sub", "mem"), pairs)
        return received

    def layered(blocks, rows):
        return [blocks[:, layer * rows : (layer + 1) * rows] for layer in range(layers)]

    packed = pack_obs(hx_values, layers, 0, (), ())
    first = across([block.reshape(held, half, own) for block in packed])
    (second,) = pack_obs(hx_values, layers, 1, (obs_value, obs_var), packed[:1])
    second = within(second.reshape(held, -1, own))
    seconds = [second] + across(layered(second, half))[1:]
    state = pack_state(member_state, layers, width, first[1:2] + first[-1:])
    size = state.shape[5]
    state = within(state.reshape(held, layers * local, size))
    states = across(layered(state, local))
    first = within(join(first, [state]))
    observed = [first, *seconds]
    if shared:
        observed = [widened(array, count) for array in observed]
    transform = transforms(observed[0], observed[1:], count)

    if not shared and width == 2 and cells_a // width >= STEPS:
        state = state.reshape(held, layers, local, size)
        fields = forecasts(state, states[1:], transform, courant)
    else:
        column = lax.axis_index("sub") % count
        line = (lax.axis_index("mem") * width + column % width) * cells_b
        speed = lax.dynamic_slice(courant, (column // width, line), (1, cells_b))
        speed = jnp.concatenate([speed] * width, axis=1)
        states = [block.reshape(count, PAIR * local, size) for block in states]
        analysis = analyses(jnp.concatenate(states, axis=1), transform)
        fields = shared_transport(analysis, speed, width, count)
        fields = fields.reshape(count, layers, PAIR * local, size)
        place = jnp.arange(layers) ^ own_layer()
        fields = jnp.take(fields, place, axis=1)

    groups = None
    if shared:
        span = count * owners
        groups = [list(range(g, g + span)) for g in range(0, lines * owners, span)]
    back = lax.all_to_all(
        fields.reshape(count * owners, local, size),
        ("sub", "mem"),
        split_axis=0,
        concat_axis=0,
        tiled=True,
        axis_index_groups=groups,
    )
    return unpack_state(back.reshape(slabs, width, owners, local, size), cells_a)


def solution(mesh):
    in_specs = (
        P(None, "mem", "sub", None),
        P(None, "mem", "sub", None, None),
        P(None, "sub", "mem", None),
        P(None, "sub", "mem", None),
        P(),
    )
    out_specs = P(None, "mem", "sub", None)
    return jax.shard_map(advance, mesh=mesh, in_specs=in_specs, out_specs=out_specs, check_vma=False)
```

```python
import jax
import jax.numpy as jnp
from jax import lax
from jax.experimental import pallas as pl
from jax.experimental.pallas import tpu as pltpu
from jax.sharding import PartitionSpec as P

ITERS = 4
STEPS = 4
PAIR = 2
SPARE = 16
F32 = jnp.float32
BF16 = jnp.bfloat16
VMEM_LIMIT = 60 * 1024 * 1024
ANY = pl.BlockSpec(memory_space=pl.ANY)


def params(count):
    return pltpu.CompilerParams(
        dimension_semantics=("arbitrary",) * count, vmem_limit_bytes=VMEM_LIMIT
    )


def split(value, size):
    return value >> (size.bit_length() - 1), value & (size - 1)


def iota(rows, cols, dim):
    return lax.broadcasted_iota(jnp.int32, (rows, cols), dim)


def dot_bf16(left, right):
    return jnp.dot(left, right, preferred_element_type=F32)


def moved(left, right):
    return dot_bf16(left, right).astype(BF16)


def ones_at(condition):
    return jnp.where(condition, 1.0, 0.0).astype(BF16)


def own_layer():
    return lax.axis_index("mem") >> 1


def own_bit():
    return lax.axis_index("mem") & 1


def pack_obs_kernel(rows, value, variance, *refs, layers):
    *firsts, second, order = refs
    _, local, _, patches, own = rows.shape
    half = local // 2
    width = value.shape[2]
    size = order.shape[0]
    block = size // patches

    @pl.when(pl.program_id(0) == 0)
    def _():
        rest, member = split(iota(size, size, 0), block)
        rest, layer = split(rest, layers)
        part, bit = split(rest, PAIR)
        owner = (layer ^ own_layer()) * PAIR + bit
        order[...] = ones_at(iota(size, size, 1) == member * patches + owner * width + part)

    for at in range(0, local, block):
        flat = moved(order[...], rows[0, at : at + block].reshape(size, own))
        flat = flat.reshape(width * PAIR, layers, block, own)
        for layer in range(layers):
            if at < half:
                firsts[layer][0, :, at : at + block, :] = flat[:, layer]
            else:
                start = layer * half + at - half
                second[0, :, start : start + block, :] = flat[:, layer]
    values, variances = (ref[0, 0].astype(F32) for ref in (value, variance))
    line = iota(SPARE, own, 0)
    for part in range(width):
        spare = jnp.where(line == 0, values[part : part + 1], variances[part : part + 1])
        for bit in range(PAIR):
            second[0, part * PAIR + bit, layers * half :, :] = spare.astype(BF16)


def pack_obs(hx_values, obs_value, obs_var, layers):
    slabs, local, _, patches, own = hx_values.shape
    width = patches // (layers * PAIR)
    block = 16

    def kernel(*refs):
        pack_obs_kernel(*refs, layers=layers)

    held = width * PAIR
    shapes = [(held, local // 2, own)] * layers + [(held, layers * local // 2 + SPARE, own)]
    return pl.pallas_call(
        kernel,
        grid=(slabs,),
        in_specs=[pl.BlockSpec((1, local, 1, patches, own), lambda s: (s, 0, 0, 0, 0))]
        + [pl.BlockSpec((1, 1, width, own), lambda s: (s, 0, 0, 0))] * 2,
        out_specs=[pl.BlockSpec((1, *shape), lambda s: (s, 0, 0, 0)) for shape in shapes],
        out_shape=[jax.ShapeDtypeStruct((slabs, *shape), BF16) for shape in shapes],
        scratch_shapes=[pltpu.VMEM((block * patches, block * patches), BF16)],
        compiler_params=params(1),
        name="pack_obs",
    )(hx_values, obs_value, obs_var)


def swapped(width, lanes):
    size = width * lanes
    outer, cell = split(iota(size, size, 1), lanes // width)
    first, second = split(outer, width)
    return ones_at(iota(size, size, 0) == (second * width + first) * (lanes // width) + cell)


def transposed(outer, inner):
    size = outer * inner
    first, second = split(iota(size, size, 0), inner)
    return ones_at(iota(size, size, 1) == second * outer + first)


def pack_state_kernel(cells, out, order, swap):
    _, width, _, layers, block, size = out.shape
    cells_a, cols = cells.shape[2:]
    lanes = cols // (layers * PAIR)
    tiles = size // lanes

    @pl.when((pl.program_id(0) == 0) & (pl.program_id(1) == 0))
    def _():
        order[...] = transposed(cells_a, block)
        swap[...] = swapped(width, lanes)

    rows = moved(order[...], cells[...].reshape(block * cells_a, cols))
    parts = []
    for owner in range(layers * PAIR):
        for tile in range(tiles):
            pieces = [
                rows[
                    (half * tiles + tile) * block : (half * tiles + tile + 1) * block,
                    owner * lanes : (owner + 1) * lanes,
                ]
                for half in range(width)
            ]
            parts.append(jnp.concatenate(pieces, axis=1))
    mixed = moved(jnp.concatenate(parts, axis=0), swap[...])
    for owner in range(layers * PAIR):
        layer = own_layer() ^ (owner // PAIR)
        for tile in range(tiles):
            at = (owner * tiles + tile) * block
            for part in range(width):
                out[0, part, owner % PAIR, layer, :, tile * lanes : (tile + 1) * lanes] = mixed[
                    at : at + block, part * lanes : (part + 1) * lanes
                ]


def pack_state(member_state, layers, width, after):
    slabs, local, cells_a, cols = member_state.shape
    lanes = cols // (layers * PAIR)
    size = cells_a * lanes // width
    block = 32

    def kernel(*refs):
        pack_state_kernel(refs[0], *refs[1 + len(after) :])

    return pl.pallas_call(
        kernel,
        grid=(slabs, local // block),
        in_specs=[pl.BlockSpec((1, block, cells_a, cols), lambda s, g: (s, g, 0, 0))]
        + [ANY] * len(after),
        out_specs=pl.BlockSpec(
            (1, width, PAIR, layers, block, size), lambda s, g: (s, 0, 0, 0, g, 0)
        ),
        out_shape=jax.ShapeDtypeStruct((slabs, width, PAIR, layers, local, size), BF16),
        scratch_shapes=[
            pltpu.VMEM((block * cells_a, block * cells_a), BF16),
            pltpu.VMEM((width * lanes, width * lanes), BF16),
        ],
        compiler_params=params(2),
        name="pack_state",
    )(member_state, *after)


def unpack_state_kernel(*refs, layers, width):
    blocks = refs[:layers]
    out, order, swap = refs[-3:]
    block, cells_a, cols = out.shape[1:]
    size = blocks[0].shape[2]
    lanes = cols // (layers * PAIR)
    tiles = size // lanes

    @pl.when(pl.program_id(0) == 0)
    def _():
        order[...] = transposed(block, cells_a)
        swap[...] = swapped(width, lanes)

    for layer in range(layers):
        parts = []
        for bit in range(PAIR):
            for tile in range(tiles):
                pieces = [
                    blocks[layer][part * PAIR + bit, :, tile * lanes : (tile + 1) * lanes]
                    for part in range(width)
                ]
                parts.append(jnp.concatenate(pieces, axis=1))
        mixed = moved(jnp.concatenate(parts, axis=0), swap[...])
        columns = []
        for bit in range(PAIR):
            rows = []
            for cell in range(cells_a):
                half, tile = cell // tiles, cell % tiles
                at = (bit * tiles + tile) * block
                rows.append(mixed[at : at + block, half * lanes : (half + 1) * lanes])
            columns.append(jnp.concatenate(rows, axis=0))
        rows = moved(order[...], jnp.concatenate(columns, axis=1))
        span = PAIR * lanes
        at = pl.multiple_of((own_layer() ^ layer) * span, span)
        out[0, :, :, pl.ds(at, span)] = rows.reshape(block, cells_a, span)


def unpack_state(blocks, specs, shape, piece, before):
    slabs, local, cells_a, cols = shape
    block = local // 2
    layers = len(blocks)
    size = blocks[0].shape[2]
    lanes = cols // (layers * PAIR)
    width = cells_a * lanes // size

    def kernel(*refs):
        unpack_state_kernel(*refs, layers=layers, width=width)

    kept = [] if before is None else [before]
    return pl.pallas_call(
        kernel,
        grid=(slabs,),
        in_specs=specs + [ANY] * len(kept),
        out_specs=pl.BlockSpec((1, block, cells_a, cols), lambda s: (s, piece, 0, 0)),
        out_shape=jax.ShapeDtypeStruct(shape, BF16),
        scratch_shapes=[
            pltpu.VMEM((block * cells_a, block * cells_a), BF16),
            pltpu.VMEM((width * lanes, width * lanes), BF16),
        ],
        input_output_aliases={layers: 0} if kept else {},
        compiler_params=params(1),
        name="unpack_state",
    )(*blocks, *kept)


def join(blocks, after):
    layers = len(blocks)
    held, rows, size = blocks[0].shape
    span = held // 2

    def kernel(*refs):
        for layer in range(layers):
            refs[-1][:, layer * rows : (layer + 1) * rows, :] = refs[layer][...]

    return pl.pallas_call(
        kernel,
        grid=(2,),
        in_specs=[pl.BlockSpec((span, rows, size), lambda i: (i, 0, 0))] * layers
        + [ANY] * len(after),
        out_specs=pl.BlockSpec((span, layers * rows, size), lambda i: (i, 0, 0)),
        out_shape=jax.ShapeDtypeStruct((held, layers * rows, size), BF16),
        compiler_params=params(1),
        name="join",
    )(*blocks, *after)


def gate(array, after):
    return pl.pallas_call(
        lambda *refs: None,
        in_specs=[ANY] * (1 + len(after)),
        out_specs=ANY,
        out_shape=jax.ShapeDtypeStruct(array.shape, array.dtype),
        input_output_aliases={0: 0},
        compiler_params=pltpu.CompilerParams(vmem_limit_bytes=VMEM_LIMIT),
        name="gate",
    )(array, *after)


def transform_kernel(spread, *refs, layers, count, shift):
    seconds = refs[:layers]
    out, pert, weighted = refs[layers:]
    total = out.shape[1]
    own = spread.shape[2]
    half = own // 2
    local = total // (layers * PAIR * 2)
    held = spread.shape[0] // PAIR
    a = pl.program_id(0) + shift
    taper = (iota(1, half, 1).astype(F32) + 1.0) / (half + 1.0)
    fall = (half - iota(1, half, 1).astype(F32)) / (half + 1.0)
    level = jnp.ones((1, half), F32)
    sources = [
        (lax.rem(a + held - 1, held), half, taper),
        (a, 0, level),
        (a, half, level),
        (lax.rem(a + 1, held), 0, fall),
    ]
    projected = jnp.zeros((total, 1), F32)
    for number, (patch, start, weight) in enumerate(sources):
        cols = slice(start, start + half)
        pieces = []
        for layer in range(layers):
            for bit in range(PAIR):
                block = patch * PAIR + bit
                pieces.append(spread[block, layer * local : (layer + 1) * local, cols])
                pieces.append(seconds[layer][block, 0:local, cols])
        values = jnp.concatenate(pieces, axis=0).astype(F32)
        at = layers * local
        stats = seconds[0][patch * PAIR + own_bit(), at : at + SPARE, cols].astype(F32)
        mean = jnp.sum(values, axis=0, keepdims=True) * (1.0 / total)
        centre = values - mean
        place = slice(number * half, (number + 1) * half)
        pert[:, place] = centre.astype(BF16)
        scaled = (centre * (weight / stats[1:2])).astype(BF16)
        weighted[:, place] = scaled
        innovation = stats[0:1] - mean
        projected += jnp.sum(scaled.astype(F32) * innovation, axis=1, keepdims=True)
    diagonal = iota(total, total, 0) == iota(total, total, 1)
    gram = lax.dot_general(
        weighted[...], pert[...], (((1,), (1,)), ((), ())), preferred_element_type=F32
    )
    system = jnp.where(diagonal, total - 1.0, 0.0) + gram
    bound = jnp.max(jnp.sum(jnp.abs(system), axis=1, keepdims=True), axis=0, keepdims=True)
    root = (system / bound).astype(BF16)
    inverse = None
    for iteration in range(ITERS):
        product = root.astype(F32) if inverse is None else dot_bf16(inverse.astype(BF16), root)
        correction = (jnp.where(diagonal, 1.5, 0.0) - 0.5 * product).astype(BF16)
        if iteration + 1 < ITERS:
            root = moved(root, correction)
        if inverse is None:
            inverse = correction.astype(F32)
        else:
            inverse = dot_bf16(correction, inverse.astype(BF16))
    flipped = inverse.T
    halfway = jnp.sum(flipped * projected, axis=0, keepdims=True)
    weight = jnp.sum(inverse * halfway, axis=1, keepdims=True)
    weight = jnp.broadcast_to(weight, (total, 128)).T[0:1, :] / bound
    out[0] = (jnp.sqrt((total - 1.0) / bound) * flipped + weight).astype(BF16)


def transforms(spread, seconds, count, after):
    layers = len(seconds)
    held, rows, own = spread.shape
    total = rows * PAIR * 2
    shift = (held // PAIR - count) // 2
    flops = count * (2 * total * total * 2 * own + 18 * total**3)

    def kernel(*refs):
        kept = refs[: 1 + layers] + refs[1 + layers + len(after) :]
        transform_kernel(*kept, layers=layers, count=count, shift=shift)

    return pl.pallas_call(
        kernel,
        grid=(count,),
        in_specs=[
            pl.BlockSpec(array.shape, lambda a: (0, 0, 0)) for array in (spread, *seconds)
        ]
        + [ANY] * len(after),
        out_specs=pl.BlockSpec((1, total, total), lambda a: (a, 0, 0)),
        out_shape=jax.ShapeDtypeStruct((count, total, total), BF16),
        scratch_shapes=[pltpu.VMEM((total, 2 * own), BF16), pltpu.VMEM((total, 2 * own), BF16)],
        compiler_params=params(1),
        cost_estimate=pl.CostEstimate(
            flops=flops, bytes_accessed=4 * count * total * total * 2, transcendentals=0
        ),
        name="transform",
    )(spread, *seconds, *after)


def centred(values):
    values = values.astype(F32)
    mean = jnp.sum(values, axis=0, keepdims=True) * (1.0 / values.shape[0])
    return mean, (values - mean).astype(BF16)


def stencil(c):
    step = [0.5 * (c * c + c), 1.0 - c * c, 0.5 * (c * c - c)]
    taps = step
    for _ in range(STEPS - 1):
        longer = [jnp.zeros_like(c)] * (len(taps) + 2)
        for i, tap in enumerate(taps):
            for j, weight in enumerate(step):
                longer[i + j] = longer[i + j] + tap * weight
        taps = longer
    return taps


def transport(tiles, taps, low):
    count, depth = len(tiles), len(tiles[0])
    shift = tiles[0][0].shape[1] // 2
    turned = [[pltpu.roll(tile, shift, 1) for tile in column] for column in tiles]
    results = []
    for a in range(count):
        before = [jnp.where(low, u, v) for u, v in zip(turned[(a - 1) % count], turned[a])]
        after = [jnp.where(low, u, v) for u, v in zip(turned[a], turned[(a + 1) % count])]
        line = before + tiles[a] + after
        start = depth - STEPS
        results.append(
            [sum(taps[t] * line[start + k + t] for t in range(len(taps))) for k in range(depth)]
        )
    return results


def forecast_kernel(*refs, layers, spread):
    blocks, (transform, courant) = refs[:layers], refs[layers : layers + 2]
    outs, fields = refs[layers + 2 : -1], refs[-1]
    count, rows, size = fields.shape
    total = transform.shape[4]
    local = rows // (layers * PAIR)
    a = pl.program_id(0)
    values = jnp.concatenate(
        [block[...].reshape(total // layers, size) for block in blocks], axis=0
    )
    mean, pert = centred(values)
    update = dot_bf16(transform[...].reshape(rows, total), pert)
    fields[a] = (update + mean).astype(BF16).astype(F32)

    @pl.when(a == count - 1)
    def _():
        lanes = courant.shape[1] // (layers * PAIR)
        column = lax.axis_index("sub") & (count - 1)
        slab, part = column // 2, column % 2
        low = iota(8, lanes, 1) < lanes // 2
        at = pl.ds(pl.multiple_of(lax.axis_index("mem") * lanes, lanes), lanes)
        speeds = courant[:, at]
        speed = speeds[0:1]
        for other in range(1, speeds.shape[0]):
            speed = jnp.where(slab == other, speeds[other : other + 1], speed)
        speed = jnp.broadcast_to(speed, (8, lanes))
        speed = jnp.where(low == (part == 0), speed, pltpu.roll(speed, lanes // 2, 1))
        taps = stencil(speed)
        chunk = 16
        steps = local // chunk
        for layer in range(layers):

            def rows_at(step, carry):
                bit, inside = step // steps, step % steps
                start = (layer * PAIR + bit) * local + inside * chunk
                parts = []
                for half in range(chunk // 8):
                    at = pl.ds(pl.multiple_of(start + half * 8, 8), 8)
                    tiles = [
                        [fields[a, at, k * lanes : (k + 1) * lanes] for k in range(size // lanes)]
                        for a in range(count)
                    ]
                    parts.append(transport(tiles, taps, low))
                to = inside * chunk + (layer * local if spread else 0)
                at = pl.ds(pl.multiple_of(to, chunk), chunk)
                out = outs[0] if spread else outs[layer]
                for a in range(count):
                    for k in range(size // lanes):
                        value = jnp.concatenate([part[a][k] for part in parts], axis=0)
                        out[a * PAIR + bit, at, k * lanes : (k + 1) * lanes] = value.astype(BF16)
                return carry

            lax.fori_loop(0, PAIR * steps, rows_at, 0)


def forecasts(own_blocks, blocks, transform, courant, piece, after):
    held, layers, local, size = own_blocks.shape
    count = held // PAIR
    total = transform.shape[2]
    half = local // 2
    transform = transform.reshape(count, layers * PAIR, 2, half, total)
    shapes = [(held, half, size)] * layers
    if piece == 1:
        shapes = [(held, layers * half, size)]

    def kernel(*refs):
        kept = refs[: layers + 2] + refs[layers + 2 + len(after) :]
        forecast_kernel(*kept, layers=layers, spread=piece == 1)

    return pl.pallas_call(
        kernel,
        grid=(count,),
        in_specs=[
            pl.BlockSpec((PAIR, 1, local, size), lambda a: (a, 0, 0, 0)),
            *[pl.BlockSpec((PAIR, local, size), lambda a: (a, 0, 0)) for _ in blocks],
            pl.BlockSpec(
                (1, layers * PAIR, 1, half, total), lambda a: (a, 0, piece, 0, 0)
            ),
            pl.BlockSpec(courant.shape, lambda a: (0, 0)),
            *[ANY] * len(after),
        ],
        out_specs=[pl.BlockSpec(shape, lambda a: (0, 0, 0)) for shape in shapes],
        out_shape=[jax.ShapeDtypeStruct(shape, BF16) for shape in shapes],
        scratch_shapes=[pltpu.VMEM((count, total // 2, size), F32)],
        compiler_params=params(1),
        cost_estimate=pl.CostEstimate(
            flops=count * total * total * size, bytes_accessed=4 * total * size * count, transcendentals=0
        ),
        name="forecast",
    )(own_blocks, *blocks, transform, courant, *after)


def analysis_kernel(state, transform, out):
    mean, pert = centred(state[0])
    out[0] = (dot_bf16(transform[0], pert) + mean).astype(BF16)


def analyses(state, transform):
    count, total, size = state.shape
    return pl.pallas_call(
        analysis_kernel,
        grid=(count,),
        in_specs=[
            pl.BlockSpec((1, total, size), lambda a: (a, 0, 0)),
            pl.BlockSpec((1, total, total), lambda a: (a, 0, 0)),
        ],
        out_specs=pl.BlockSpec((1, total, size), lambda a: (a, 0, 0)),
        out_shape=jax.ShapeDtypeStruct((count, total, size), BF16),
        compiler_params=params(1),
        name="analysis",
    )(state, transform)


def shared_transport(analysis, speed, width, jump):
    count, total, size = analysis.shape
    lanes = speed.shape[1]
    cells = lanes // width
    tiles = size // lanes
    fields = widened(analysis, jump).reshape(count + 2, total, tiles, width, cells)
    fields = fields.transpose(1, 0, 3, 2, 4).reshape(total, -1, cells).astype(F32)
    c = speed[0, :cells]
    for _ in range(STEPS):
        prior, here, after = fields[:, :-2], fields[:, 1:-1], fields[:, 2:]
        fields = (1.0 - c * c) * here + 0.5 * (c * c - c) * after + 0.5 * (c * c + c) * prior
    spare = tiles * width - STEPS
    fields = fields[:, spare : fields.shape[1] - spare].astype(BF16)
    fields = fields.reshape(total, count, width, tiles, cells)
    return fields.transpose(1, 0, 3, 2, 4).reshape(count, total, size)


def widened(blocks, jump):
    count = lax.axis_size("sub")
    forward = [(i, (i + jump) % count) for i in range(count)]
    backward = [(target, source) for source, target in forward]
    span = blocks.shape[0] // jump
    low = lax.ppermute(blocks[-span:], "sub", forward)
    high = lax.ppermute(blocks[:span], "sub", backward)
    return jnp.concatenate([low, blocks, high], axis=0)


def advance(member_state, hx_values, obs_value, obs_var, courant):
    slabs, local, cells_a, cols = member_state.shape
    patches, own = hx_values.shape[3:]
    owners = lax.axis_size("mem")
    lines = lax.axis_size("sub")
    layers = owners // PAIR
    width = patches // owners
    count = slabs * width
    held = count * PAIR
    half = local // 2
    shared = lines > count
    cells_b = cols // patches
    far_first = range(layers - 1, 0, -1)

    layer_groups = [
        [s * owners + layer * PAIR + bit for s in range(g, g + count) for bit in range(PAIR)]
        for g in range(0, lines, count)
        for layer in range(layers)
    ]

    def within(blocks):
        return lax.all_to_all(
            blocks,
            ("sub", "mem"),
            split_axis=0,
            concat_axis=0,
            tiled=True,
            axis_index_groups=layer_groups,
        )

    def across(blocks, before=None):
        received = list(blocks)
        blocks = list(blocks)
        for layer in far_first:
            if before is not None and layer >= layers // 2:
                blocks[layer] = gate(blocks[layer], [before[layer]])
            pairs = [
                (s * owners + m, s * owners + (m ^ (layer * PAIR)))
                for s in range(lines)
                for m in range(owners)
            ]
            received[layer] = lax.ppermute(blocks[layer], ("sub", "mem"), pairs)
        return received

    def layered(blocks, rows):
        return [blocks[:, layer * rows : (layer + 1) * rows] for layer in range(layers)]

    *firsts, second = pack_obs(hx_values, obs_value, obs_var, layers)
    firsts = across([block.reshape(held, half, own) for block in firsts])
    second = within(second.reshape(held, -1, own))
    seconds = across(layered(second, half), firsts)
    state = pack_state(member_state, layers, width, ())
    size = state.shape[5]
    state = gate(state.reshape(held, layers * local, size), [second, firsts[1]])
    state = within(state)
    states = across(layered(state, local), seconds)
    first = within(join(firsts, [state]))
    observed = [first, second, *seconds[1:]]
    if shared:
        observed = [widened(array, count) for array in observed]
    transform = transforms(observed[0], observed[1:], count, states[1:2])

    if not shared and width == 2 and cells_a // width >= STEPS:
        state = state.reshape(held, layers, local, size)
        back = forecasts(state, states[1:], transform, courant, 0, ())
        (last,) = forecasts(state, states[1:], transform, courant, 1, back[:1])
    else:
        column = lax.axis_index("sub") % count
        line = (lax.axis_index("mem") * width + column % width) * cells_b
        speed = lax.dynamic_slice(courant, (column // width, line), (1, cells_b))
        speed = jnp.concatenate([speed] * width, axis=1)
        states = [block.reshape(count, PAIR * local, size) for block in states]
        analysis = analyses(jnp.concatenate(states, axis=1), transform)
        fields = shared_transport(analysis, speed, width, count)
        fields = fields.reshape(count, layers, PAIR, 2, half, size)
        fields = fields.transpose(3, 0, 2, 1, 4, 5).reshape(2, held, layers, half, size)
        back = [fields[0, :, layer] for layer in range(layers)]
        last = fields[1].reshape(held, layers * half, size)
    back = across(back)
    last = within(last)
    lasts = across(layered(last, half), back)
    back = within(join(back, [last]))

    def spec(layer):
        return pl.BlockSpec((width * PAIR, half, size), lambda s: (s, layer, 0))

    shape = member_state.shape
    done = unpack_state([back] * layers, [spec(i) for i in range(layers)], shape, 0, None)
    return unpack_state([last, *lasts[1:]], [spec(0)] * layers, shape, 1, done)


def solution(mesh):
    in_specs = (
        P(None, "mem", "sub", None),
        P(None, "mem", "sub", None, None),
        P(None, "sub", "mem", None),
        P(None, "sub", "mem", None),
        P(),
    )
    out_specs = P(None, "mem", "sub", None)
    return jax.shard_map(advance, mesh=mesh, in_specs=in_specs, out_specs=out_specs, check_vma=False)
```

```python
import jax
import jax.numpy as jnp
from jax import lax
from jax.experimental import pallas as pl
from jax.experimental.pallas import tpu as pltpu
from jax.sharding import PartitionSpec as P

ITERS = 4
STEPS = 4
F32 = jnp.float32
BF16 = jnp.bfloat16
MIB = 1024 * 1024
WHOLE = pl.BlockSpec(memory_space=pltpu.VMEM)


def params(count, limit=40):
    return pltpu.CompilerParams(
        dimension_semantics=("arbitrary",) * count, vmem_limit_bytes=limit * MIB
    )


def split(value, size):
    return value >> (size.bit_length() - 1), value & (size - 1)


def iota(rows, cols, dim):
    return lax.broadcasted_iota(jnp.int32, (rows, cols), dim)


def dot_bf16(left, right):
    return jnp.dot(left, right, preferred_element_type=F32)


def moved(left, right):
    return dot_bf16(left, right).astype(BF16)


def ones_at(condition):
    return jnp.where(condition, 1.0, 0.0).astype(BF16)


def pack_obs_kernel(rows, out, order):
    _, width, owners, block, own = out.shape
    size = order.shape[0]
    patches = width * owners

    @pl.when((pl.program_id(0) == 0) & (pl.program_id(1) == 0))
    def _():
        rest, member = split(iota(size, size, 0), block)
        part, owner = split(rest, owners)
        order[...] = ones_at(iota(size, size, 1) == member * patches + owner * width + part)

    out[...] = moved(order[...], rows[...].reshape(size, own)).reshape(out.shape)


def pack_obs(hx_values, width):
    slabs, local, _, patches, own = hx_values.shape
    owners = patches // width
    block = 16
    return pl.pallas_call(
        pack_obs_kernel,
        grid=(slabs, local // block),
        in_specs=[pl.BlockSpec((1, block, 1, patches, own), lambda s, g: (s, g, 0, 0, 0))],
        out_specs=pl.BlockSpec((1, width, owners, block, own), lambda s, g: (s, 0, 0, g, 0)),
        out_shape=jax.ShapeDtypeStruct((slabs, width, owners, local, own), BF16),
        scratch_shapes=[pltpu.VMEM((block * patches, block * patches), BF16)],
        compiler_params=params(2, 60),
        name="pack_obs",
    )(hx_values)


def swapped(width, lanes):
    size = width * lanes
    outer, cell = split(iota(size, size, 1), lanes // width)
    first, second = split(outer, width)
    return ones_at(iota(size, size, 0) == (second * width + first) * (lanes // width) + cell)


def transposed(outer, inner):
    size = outer * inner
    first, second = split(iota(size, size, 0), inner)
    return ones_at(iota(size, size, 1) == second * outer + first)


def pack_state_kernel(cells, out, order, swap):
    _, width, owners, block, size = out.shape
    lanes = cells.shape[3] // owners
    tiles = size // lanes

    @pl.when((pl.program_id(0) == 0) & (pl.program_id(1) == 0))
    def _():
        order[...] = transposed(cells.shape[2], block)
        swap[...] = swapped(width, lanes)

    rows = moved(order[...], cells[...].reshape(order.shape[0], cells.shape[3]))
    parts = []
    for owner in range(owners):
        for tile in range(tiles):
            pieces = [
                rows[
                    (half * tiles + tile) * block : (half * tiles + tile + 1) * block,
                    owner * lanes : (owner + 1) * lanes,
                ]
                for half in range(width)
            ]
            parts.append(jnp.concatenate(pieces, axis=1))
    mixed = moved(jnp.concatenate(parts, axis=0), swap[...])
    for owner in range(owners):
        for tile in range(tiles):
            at = (owner * tiles + tile) * block
            for part in range(width):
                out[0, part, owner, :, tile * lanes : (tile + 1) * lanes] = mixed[
                    at : at + block, part * lanes : (part + 1) * lanes
                ]


def pack_state(member_state, width, owners):
    slabs, local, cells_a, cols = member_state.shape
    lanes = cols // owners
    size = cells_a * lanes // width
    block = 32
    return pl.pallas_call(
        pack_state_kernel,
        grid=(slabs, local // block),
        in_specs=[
            pl.BlockSpec((1, block, cells_a, cols), lambda s, g: (s, g, 0, 0)),
        ],
        out_specs=pl.BlockSpec((1, width, owners, block, size), lambda s, g: (s, 0, 0, g, 0)),
        out_shape=jax.ShapeDtypeStruct((slabs, width, owners, local, size), BF16),
        scratch_shapes=[
            pltpu.VMEM((block * cells_a, block * cells_a), BF16),
            pltpu.VMEM((width * lanes, width * lanes), BF16),
        ],
        compiler_params=params(2, 60),
        name="pack_state",
    )(member_state)


def unpack_state_kernel(packed, out, order, swap):
    _, width, owners, _, size = packed.shape
    block, cells_a = out.shape[1:3]
    slab, group = pl.program_id(0), pl.program_id(1)
    here = pl.ds(pl.multiple_of(group * block, block), block)
    tiles = cells_a // width
    lanes = size // tiles

    @pl.when((pl.program_id(0) == 0) & (pl.program_id(1) == 0))
    def _():
        order[...] = transposed(block, cells_a)
        swap[...] = swapped(width, lanes)

    parts = []
    for owner in range(owners):
        for tile in range(tiles):
            pieces = [
                packed[slab, part, owner, here, tile * lanes : (tile + 1) * lanes]
                for part in range(width)
            ]
            parts.append(jnp.concatenate(pieces, axis=1))
    mixed = moved(jnp.concatenate(parts, axis=0), swap[...])
    columns = []
    for owner in range(owners):
        rows = []
        for cell in range(cells_a):
            half, tile = cell // tiles, cell % tiles
            at = (owner * tiles + tile) * block
            rows.append(mixed[at : at + block, half * lanes : (half + 1) * lanes])
        columns.append(jnp.concatenate(rows, axis=0))
    rows = moved(order[...], jnp.concatenate(columns, axis=1))
    out[...] = rows.reshape(out.shape)


def unpack_state(packed, cells_a):
    slabs, width, owners, local, size = packed.shape
    lanes = size * width // cells_a
    cols = owners * lanes
    block = 32
    return pl.pallas_call(
        unpack_state_kernel,
        grid=(slabs, local // block),
        in_specs=[WHOLE],
        out_specs=pl.BlockSpec((1, block, cells_a, cols), lambda s, g: (s, g, 0, 0)),
        out_shape=jax.ShapeDtypeStruct((slabs, local, cells_a, cols), BF16),
        scratch_shapes=[
            pltpu.VMEM((block * cells_a, block * cells_a), BF16),
            pltpu.VMEM((width * lanes, width * lanes), BF16),
        ],
        compiler_params=params(2),
        name="unpack_state",
    )(packed)


def transform_kernel(before, middle, after, obs, scale, out, rest, pert, weighted):
    total = middle.shape[1]
    half = before.shape[2]
    projected = jnp.zeros((total, 1), F32)
    start = 0
    for part in (before, middle, after):
        span = part.shape[2]
        for at in range(0, span, half):
            cols = slice(start, start + half)
            values = part[0, :, at : at + half].astype(F32)
            mean = jnp.sum(values, axis=0, keepdims=True) * (1.0 / total)
            centred = values - mean
            pert[:, cols] = centred.astype(BF16)
            scaled = (centred * scale[0, :, cols]).astype(BF16)
            weighted[:, cols] = scaled
            innovation = obs[0, :, cols] - mean
            projected += jnp.sum(scaled.astype(F32) * innovation, axis=1, keepdims=True)
            start += half
    diagonal = iota(total, total, 0) == iota(total, total, 1)
    gram = lax.dot_general(
        weighted[...], pert[...], (((1,), (1,)), ((), ())), preferred_element_type=F32
    )
    system = jnp.where(diagonal, total - 1.0, 0.0) + gram
    bound = jnp.max(jnp.sum(jnp.abs(system), axis=1, keepdims=True), axis=0, keepdims=True)
    root = (system / bound).astype(BF16)
    inverse = None
    for iteration in range(ITERS):
        product = root.astype(F32) if inverse is None else dot_bf16(inverse.astype(BF16), root)
        correction = (jnp.where(diagonal, 1.5, 0.0) - 0.5 * product).astype(BF16)
        if iteration + 1 < ITERS:
            root = moved(root, correction)
        if inverse is None:
            inverse = correction.astype(F32)
        else:
            inverse = dot_bf16(correction, inverse.astype(BF16))
    flipped = inverse.T
    halfway = jnp.sum(flipped * projected, axis=0, keepdims=True)
    weight = jnp.sum(inverse * halfway, axis=1, keepdims=True)
    weight = jnp.broadcast_to(weight, (total, 128)).T[0:1, :] / bound
    result = (jnp.sqrt((total - 1.0) / bound) * flipped + weight).astype(BF16)
    out[0] = result
    sums = jnp.sum(result.astype(F32), axis=1, keepdims=True)
    rest[0] = jnp.broadcast_to(1.0 - sums, (total, 128))


def transforms(hx_rows, obs_rows, scale_rows, count, wraps):
    held, total, own = hx_rows.shape
    half = own // 2
    shift = 0 if wraps else 1
    flops = count * (2 * total * total * 2 * own + 18 * total**3)
    return pl.pallas_call(
        transform_kernel,
        grid=(count,),
        in_specs=[
            pl.BlockSpec((1, total, half), lambda a: ((a + shift + held - 1) % held, 0, 1)),
            pl.BlockSpec((1, total, own), lambda a: (a + shift, 0, 0)),
            pl.BlockSpec((1, total, half), lambda a: ((a + shift + 1) % held, 0, 0)),
            pl.BlockSpec((1, 1, 2 * own), lambda a: (a, 0, 0)),
            pl.BlockSpec((1, 1, 2 * own), lambda a: (a, 0, 0)),
        ],
        out_specs=[
            pl.BlockSpec((1, total, total), lambda a: (a, 0, 0)),
            pl.BlockSpec((1, total, 128), lambda a: (a, 0, 0)),
        ],
        out_shape=[
            jax.ShapeDtypeStruct((count, total, total), BF16),
            jax.ShapeDtypeStruct((count, total, 128), F32),
        ],
        scratch_shapes=[pltpu.VMEM((total, 2 * own), BF16), pltpu.VMEM((total, 2 * own), BF16)],
        compiler_params=params(1),
        cost_estimate=pl.CostEstimate(
            flops=flops, bytes_accessed=4 * count * total * total * 2, transcendentals=0
        ),
        name="transform",
    )(hx_rows, hx_rows, hx_rows, obs_rows, scale_rows)


def centred(values):
    values = values.astype(F32)
    mean = jnp.sum(values, axis=0, keepdims=True) * (1.0 / values.shape[0])
    return mean, (values - mean).astype(BF16)


def stencil(c):
    step = [0.5 * (c * c + c), 1.0 - c * c, 0.5 * (c * c - c)]
    taps = step
    for _ in range(STEPS - 1):
        longer = [jnp.zeros_like(c)] * (len(taps) + 2)
        for i, tap in enumerate(taps):
            for j, weight in enumerate(step):
                longer[i + j] = longer[i + j] + tap * weight
        taps = longer
    return taps


def transport(tiles, taps, low):
    count, depth = len(tiles), len(tiles[0])
    shift = tiles[0][0].shape[1] // 2
    turned = [[pltpu.roll(tile, shift, 1) for tile in column] for column in tiles]
    results = []
    for a in range(count):
        before = [jnp.where(low, u, v) for u, v in zip(turned[(a - 1) % count], turned[a])]
        after = [jnp.where(low, u, v) for u, v in zip(turned[a], turned[(a + 1) % count])]
        line = before + tiles[a] + after
        start = depth - STEPS
        results.append(
            [sum(taps[t] * line[start + k + t] for t in range(len(taps))) for k in range(depth)]
        )
    return results


def forecast_kernel(state, transform, rest, speed, out, fields):
    count, total, size = out.shape
    lanes = speed.shape[1]
    for a in range(count):
        mean = jnp.sum(state[a].astype(F32), axis=0, keepdims=True) * (1.0 / total)
        values = dot_bf16(transform[a], state[a])
        for k in range(size // lanes):
            part = slice(k * lanes, (k + 1) * lanes)
            analysis = values[:, part] + rest[a] * mean[:, part]
            fields[a, :, part] = analysis.astype(BF16).astype(F32)
    chunk = 16
    taps = stencil(jnp.broadcast_to(speed[...], (8, lanes)))
    low = iota(8, lanes, 1) < lanes // 2

    def rows_at(step, carry):
        parts = []
        for half in range(chunk // 8):
            at = pl.ds(pl.multiple_of(step * chunk + half * 8, 8), 8)
            tiles = [
                [fields[a, at, k * lanes : (k + 1) * lanes] for k in range(size // lanes)]
                for a in range(count)
            ]
            parts.append(transport(tiles, taps, low))
        at = pl.ds(pl.multiple_of(step * chunk, chunk), chunk)
        for a in range(count):
            for k in range(size // lanes):
                value = jnp.concatenate([part[a][k] for part in parts], axis=0)
                out[a, at, k * lanes : (k + 1) * lanes] = value.astype(BF16)
        return carry

    lax.fori_loop(0, total // chunk, rows_at, 0)


def forecasts(state, transform, rest, speed):
    count, total, size = state.shape
    return pl.pallas_call(
        forecast_kernel,
        in_specs=[WHOLE] * 4,
        out_specs=WHOLE,
        out_shape=jax.ShapeDtypeStruct((count, total, size), BF16),
        scratch_shapes=[pltpu.VMEM((count, total, size), F32)],
        compiler_params=pltpu.CompilerParams(vmem_limit_bytes=40 * MIB),
        name="forecast",
    )(state, transform, rest, speed)


def analysis_kernel(state, transform, out):
    mean, pert = centred(state[0])
    out[0] = (dot_bf16(transform[0], pert) + mean).astype(BF16)


def analyses(state, transform):
    count, total, size = state.shape
    return pl.pallas_call(
        analysis_kernel,
        grid=(count,),
        in_specs=[
            pl.BlockSpec((1, total, size), lambda a: (a, 0, 0)),
            pl.BlockSpec((1, total, total), lambda a: (a, 0, 0)),
        ],
        out_specs=pl.BlockSpec((1, total, size), lambda a: (a, 0, 0)),
        out_shape=jax.ShapeDtypeStruct((count, total, size), BF16),
        compiler_params=params(1),
        name="analysis",
    )(state, transform)


def shared_transport(analysis, speed, width, jump):
    count, total, size = analysis.shape
    lanes = speed.shape[1]
    cells = lanes // width
    tiles = size // lanes
    fields = widened(analysis, jump).reshape(count + 2, total, tiles, width, cells)
    fields = fields.transpose(1, 0, 3, 2, 4).reshape(total, -1, cells).astype(F32)
    c = speed[0, :cells]
    for _ in range(STEPS):
        prior, here, after = fields[:, :-2], fields[:, 1:-1], fields[:, 2:]
        fields = (1.0 - c * c) * here + 0.5 * (c * c - c) * after + 0.5 * (c * c + c) * prior
    spare = tiles * width - STEPS
    fields = fields[:, spare : fields.shape[1] - spare].astype(BF16)
    fields = fields.reshape(total, count, width, tiles, cells)
    return fields.transpose(1, 0, 3, 2, 4).reshape(count, total, size)


def widened(blocks, jump):
    count = lax.axis_size("sub")
    forward = [(i, (i + jump) % count) for i in range(count)]
    backward = [(target, source) for source, target in forward]
    low = lax.ppermute(blocks[-1:], "sub", forward)
    high = lax.ppermute(blocks[:1], "sub", backward)
    return jnp.concatenate([low, blocks, high], axis=0)


def advance(member_state, hx_values, obs_value, obs_var, courant):
    slabs, local, cells_a, cols = member_state.shape
    patches, own = hx_values.shape[3:]
    owners = lax.axis_size("mem")
    lines = lax.axis_size("sub")
    width = patches // owners
    count = slabs * width
    groups = lines // count
    total = local * owners
    cells_b = cols // patches
    lane_cells = width * cells_b
    place = lax.axis_index("sub") % count
    slab, part = place // width, place % width

    index_groups = None
    if groups > 1:
        held = count * owners
        index_groups = [list(range(g * held, (g + 1) * held)) for g in range(groups)]

    def exchange(blocks):
        return lax.all_to_all(
            blocks,
            ("sub", "mem"),
            split_axis=0,
            concat_axis=0,
            tiled=True,
            axis_index_groups=index_groups,
        )

    hx_rows = exchange(pack_obs(hx_values, width).reshape(count * owners, local, own))
    hx_rows = hx_rows.reshape(count, total, own)

    stats = jnp.stack([obs_value[:, 0], obs_var[:, 0]], axis=2)
    stats = lax.all_gather(stats, "sub", axis=0)
    stats = lax.dynamic_slice(stats, (0, slab, part, 0, 0), (lines, 1, 1, 2, own))
    stats = stats.reshape(lines, 2, own).astype(F32)
    half = own // 2
    stats = jnp.concatenate(
        [jnp.roll(stats, 1, 0)[:, :, half:], stats, jnp.roll(stats, -1, 0)[:, :, :half]], axis=2
    )
    if groups > 1:
        first = lax.axis_index("sub") // count * count
        stats = lax.dynamic_slice_in_dim(stats, first, count, axis=0)
    taper = (jnp.arange(half, dtype=F32) + 1.0) / (half + 1.0)
    local_weight = jnp.concatenate([taper, jnp.ones((own,), F32), taper[::-1]])
    obs_rows = stats[:, 0:1]
    scale_rows = local_weight / stats[:, 1:2]

    state = exchange(pack_state(member_state, width, owners).reshape(count * owners, local, -1))
    state = state.reshape(count, total, -1)

    held_rows = hx_rows if groups == 1 else widened(hx_rows, count)
    transform, rest = transforms(held_rows, obs_rows, scale_rows, count, groups == 1)

    column = (lax.axis_index("mem") * width + part) * cells_b
    speed = lax.dynamic_slice(courant, (slab, column), (1, cells_b))
    speed = jnp.concatenate([speed] * width, axis=1)
    if groups == 1 and 2 * cells_b == 128 and width == 2 and cells_a // width >= STEPS:
        fields = forecasts(state, transform, rest, speed)
    else:
        fields = shared_transport(analyses(state, transform), speed, width, count)
    back = exchange(fields.reshape(count * owners, local, -1))
    return unpack_state(back.reshape(slabs, width, owners, local, -1), cells_a)


def solution(mesh):
    in_specs = (
        P(None, "mem", "sub", None),
        P(None, "mem", "sub", None, None),
        P(None, "sub", "mem", None),
        P(None, "sub", "mem", None),
        P(),
    )
    out_specs = P(None, "mem", "sub", None)
    return jax.shard_map(advance, mesh=mesh, in_specs=in_specs, out_specs=out_specs, check_vma=False)
```

```python
import jax
import jax.numpy as jnp
from jax import lax
from jax.experimental import pallas as pl
from jax.experimental.pallas import tpu as pltpu
from jax.sharding import PartitionSpec as P

ITERS = 4
STEPS = 4
F32 = jnp.float32
BF16 = jnp.bfloat16
MIB = 1024 * 1024
WHOLE = pl.BlockSpec(memory_space=pltpu.VMEM)


def params(count, limit=40):
    return pltpu.CompilerParams(
        dimension_semantics=("arbitrary",) * count, vmem_limit_bytes=limit * MIB
    )


def split(value, size):
    return value >> (size.bit_length() - 1), value & (size - 1)


def iota(rows, cols, dim):
    return lax.broadcasted_iota(jnp.int32, (rows, cols), dim)


def dot_bf16(left, right):
    return jnp.dot(left, right, preferred_element_type=F32)


def moved(left, right):
    return dot_bf16(left, right).astype(BF16)


def ones_at(condition):
    return jnp.where(condition, 1.0, 0.0).astype(BF16)


def pack_obs_kernel(rows, out, order):
    _, local, _, patches, own = rows.shape
    owners = out.shape[2]
    width = patches // owners
    block = order.shape[1] // patches
    part = pl.program_id(1)
    lead = block * owners

    @pl.when((pl.program_id(0) == 0) & (part == 0))
    def _():
        rest, member = split(iota(*order.shape, 0), block)
        side, owner = split(rest, owners)
        order[...] = ones_at(iota(*order.shape, 1) == member * patches + owner * width + side)

    turn = order[pl.ds(pl.multiple_of(part * lead, lead), lead), :]
    for at in range(0, local, block):
        flat = moved(turn, rows[0, at : at + block].reshape(block * patches, own))
        out[0, 0, :, at : at + block, :] = flat.reshape(owners, block, own)


def pack_obs(hx_values, width):
    slabs, local, _, patches, own = hx_values.shape
    owners = patches // width
    block = 16
    return pl.pallas_call(
        pack_obs_kernel,
        grid=(slabs, width),
        in_specs=[pl.BlockSpec((1, local, 1, patches, own), lambda s, p: (s, 0, 0, 0, 0))],
        out_specs=pl.BlockSpec((1, 1, owners, local, own), lambda s, p: (s, p, 0, 0, 0)),
        out_shape=jax.ShapeDtypeStruct((slabs, width, owners, local, own), BF16),
        scratch_shapes=[pltpu.VMEM((block * patches, block * patches), BF16)],
        compiler_params=params(2, 60),
        name="pack_obs",
    )(hx_values)


def swapped(width, lanes):
    size = width * lanes
    outer, cell = split(iota(size, size, 1), lanes // width)
    first, second = split(outer, width)
    return ones_at(iota(size, size, 0) == (second * width + first) * (lanes // width) + cell)


def transposed(outer, inner):
    size = outer * inner
    first, second = split(iota(size, size, 0), inner)
    return ones_at(iota(size, size, 1) == second * outer + first)


def pack_state_kernel(cells, out, order, swap):
    _, width, owners, block, size = out.shape
    lanes = cells.shape[3] // owners
    tiles = size // lanes

    @pl.when((pl.program_id(0) == 0) & (pl.program_id(1) == 0))
    def _():
        order[...] = transposed(cells.shape[2], block)
        swap[...] = swapped(width, lanes)

    rows = moved(order[...], cells[...].reshape(order.shape[0], cells.shape[3]))
    parts = []
    for owner in range(owners):
        for tile in range(tiles):
            pieces = [
                rows[
                    (half * tiles + tile) * block : (half * tiles + tile + 1) * block,
                    owner * lanes : (owner + 1) * lanes,
                ]
                for half in range(width)
            ]
            parts.append(jnp.concatenate(pieces, axis=1))
    mixed = moved(jnp.concatenate(parts, axis=0), swap[...])
    for owner in range(owners):
        for tile in range(tiles):
            at = (owner * tiles + tile) * block
            for part in range(width):
                out[0, part, owner, :, tile * lanes : (tile + 1) * lanes] = mixed[
                    at : at + block, part * lanes : (part + 1) * lanes
                ]


def pack_state(member_state, width, owners):
    slabs, local, cells_a, cols = member_state.shape
    lanes = cols // owners
    size = cells_a * lanes // width
    block = 32
    return pl.pallas_call(
        pack_state_kernel,
        grid=(slabs, local // block),
        in_specs=[
            pl.BlockSpec((1, block, cells_a, cols), lambda s, g: (s, g, 0, 0)),
        ],
        out_specs=pl.BlockSpec((1, width, owners, block, size), lambda s, g: (s, 0, 0, g, 0)),
        out_shape=jax.ShapeDtypeStruct((slabs, width, owners, local, size), BF16),
        scratch_shapes=[
            pltpu.VMEM((block * cells_a, block * cells_a), BF16),
            pltpu.VMEM((width * lanes, width * lanes), BF16),
        ],
        compiler_params=params(2, 60),
        name="pack_state",
    )(member_state)


def unpack_state_kernel(packed, out, order, swap):
    _, width, owners, _, size = packed.shape
    block, cells_a = out.shape[1:3]
    slab, group = pl.program_id(0), pl.program_id(1)
    here = pl.ds(pl.multiple_of(group * block, block), block)
    tiles = cells_a // width
    lanes = size // tiles

    @pl.when((pl.program_id(0) == 0) & (pl.program_id(1) == 0))
    def _():
        order[...] = transposed(block, cells_a)
        swap[...] = swapped(width, lanes)

    parts = []
    for owner in range(owners):
        for tile in range(tiles):
            pieces = [
                packed[slab, part, owner, here, tile * lanes : (tile + 1) * lanes]
                for part in range(width)
            ]
            parts.append(jnp.concatenate(pieces, axis=1))
    mixed = moved(jnp.concatenate(parts, axis=0), swap[...])
    columns = []
    for owner in range(owners):
        rows = []
        for cell in range(cells_a):
            half, tile = cell // tiles, cell % tiles
            at = (owner * tiles + tile) * block
            rows.append(mixed[at : at + block, half * lanes : (half + 1) * lanes])
        columns.append(jnp.concatenate(rows, axis=0))
    rows = moved(order[...], jnp.concatenate(columns, axis=1))
    out[...] = rows.reshape(out.shape)


def unpack_state(packed, cells_a):
    slabs, width, owners, local, size = packed.shape
    lanes = size * width // cells_a
    cols = owners * lanes
    block = 32
    return pl.pallas_call(
        unpack_state_kernel,
        grid=(slabs, local // block),
        in_specs=[WHOLE],
        out_specs=pl.BlockSpec((1, block, cells_a, cols), lambda s, g: (s, g, 0, 0)),
        out_shape=jax.ShapeDtypeStruct((slabs, local, cells_a, cols), BF16),
        scratch_shapes=[
            pltpu.VMEM((block * cells_a, block * cells_a), BF16),
            pltpu.VMEM((width * lanes, width * lanes), BF16),
        ],
        compiler_params=params(2),
        name="unpack_state",
    )(packed)


def transform_kernel(before, middle, after, obs, scale, out, rest, pert, weighted):
    total = middle.shape[1]
    half = before.shape[2]
    projected = jnp.zeros((total, 1), F32)
    start = 0
    for part in (before, middle, after):
        span = part.shape[2]
        for at in range(0, span, half):
            cols = slice(start, start + half)
            values = part[0, :, at : at + half].astype(F32)
            mean = jnp.sum(values, axis=0, keepdims=True) * (1.0 / total)
            centred = values - mean
            pert[:, cols] = centred.astype(BF16)
            scaled = (centred * scale[0, :, cols]).astype(BF16)
            weighted[:, cols] = scaled
            innovation = obs[0, :, cols] - mean
            projected += jnp.sum(scaled.astype(F32) * innovation, axis=1, keepdims=True)
            start += half
    diagonal = iota(total, total, 0) == iota(total, total, 1)
    gram = lax.dot_general(
        weighted[...], pert[...], (((1,), (1,)), ((), ())), preferred_element_type=F32
    )
    system = jnp.where(diagonal, total - 1.0, 0.0) + gram
    bound = jnp.max(jnp.sum(jnp.abs(system), axis=1, keepdims=True), axis=0, keepdims=True)
    root = (system / bound).astype(BF16)
    inverse = None
    for iteration in range(ITERS):
        product = root.astype(F32) if inverse is None else dot_bf16(inverse.astype(BF16), root)
        correction = (jnp.where(diagonal, 1.5, 0.0) - 0.5 * product).astype(BF16)
        if iteration + 1 < ITERS:
            root = moved(root, correction)
        if inverse is None:
            inverse = correction.astype(F32)
        else:
            inverse = dot_bf16(correction, inverse.astype(BF16))
    flipped = inverse.T
    halfway = jnp.sum(flipped * projected, axis=0, keepdims=True)
    weight = jnp.sum(inverse * halfway, axis=1, keepdims=True)
    weight = jnp.broadcast_to(weight, (total, 128)).T[0:1, :] / bound
    result = (jnp.sqrt((total - 1.0) / bound) * flipped + weight).astype(BF16)
    out[0] = result
    sums = jnp.sum(result.astype(F32), axis=1, keepdims=True)
    rest[0] = jnp.broadcast_to(1.0 - sums, (total, 128))


def transforms(hx_rows, obs_rows, scale_rows, count, wraps):
    held, total, own = hx_rows.shape
    half = own // 2
    shift = 0 if wraps else 1
    flops = count * (2 * total * total * 2 * own + 18 * total**3)
    return pl.pallas_call(
        transform_kernel,
        grid=(count,),
        in_specs=[
            pl.BlockSpec((1, total, half), lambda a: ((a + shift + held - 1) % held, 0, 1)),
            pl.BlockSpec((1, total, own), lambda a: (a + shift, 0, 0)),
            pl.BlockSpec((1, total, half), lambda a: ((a + shift + 1) % held, 0, 0)),
            pl.BlockSpec((1, 1, 2 * own), lambda a: (a, 0, 0)),
            pl.BlockSpec((1, 1, 2 * own), lambda a: (a, 0, 0)),
        ],
        out_specs=[
            pl.BlockSpec((1, total, total), lambda a: (a, 0, 0)),
            pl.BlockSpec((1, total, 128), lambda a: (a, 0, 0)),
        ],
        out_shape=[
            jax.ShapeDtypeStruct((count, total, total), BF16),
            jax.ShapeDtypeStruct((count, total, 128), F32),
        ],
        scratch_shapes=[pltpu.VMEM((total, 2 * own), BF16), pltpu.VMEM((total, 2 * own), BF16)],
        compiler_params=params(1, 60),
        cost_estimate=pl.CostEstimate(
            flops=flops, bytes_accessed=4 * count * total * total * 2, transcendentals=0
        ),
        name="transform",
    )(hx_rows, hx_rows, hx_rows, obs_rows, scale_rows)


def centred(values):
    values = values.astype(F32)
    mean = jnp.sum(values, axis=0, keepdims=True) * (1.0 / values.shape[0])
    return mean, (values - mean).astype(BF16)


def stencil(c):
    step = [0.5 * (c * c + c), 1.0 - c * c, 0.5 * (c * c - c)]
    taps = step
    for _ in range(STEPS - 1):
        longer = [jnp.zeros_like(c)] * (len(taps) + 2)
        for i, tap in enumerate(taps):
            for j, weight in enumerate(step):
                longer[i + j] = longer[i + j] + tap * weight
        taps = longer
    return taps


def transport(tiles, taps, low):
    count, depth = len(tiles), len(tiles[0])
    shift = tiles[0][0].shape[1] // 2
    turned = [[pltpu.roll(tile, shift, 1) for tile in column] for column in tiles]
    results = []
    for a in range(count):
        before = [jnp.where(low, u, v) for u, v in zip(turned[(a - 1) % count], turned[a])]
        after = [jnp.where(low, u, v) for u, v in zip(turned[a], turned[(a + 1) % count])]
        line = before + tiles[a] + after
        start = depth - STEPS
        results.append(
            [sum(taps[t] * line[start + k + t] for t in range(len(taps))) for k in range(depth)]
        )
    return results


def forecast_kernel(state, transforms, rest, speed, out, transform, fields, sems):
    count, total, size = out.shape
    lanes = speed.shape[1]
    copies = [
        pltpu.make_async_copy(transforms.at[a], transform.at[a], sems.at[a]) for a in range(count)
    ]
    for copy in copies:
        copy.start()
    for a in range(count):
        mean = jnp.sum(state[a].astype(F32), axis=0, keepdims=True) * (1.0 / total)
        copies[a].wait()
        values = dot_bf16(transform[a], state[a])
        for k in range(size // lanes):
            part = slice(k * lanes, (k + 1) * lanes)
            analysis = values[:, part] + rest[a] * mean[:, part]
            fields[a, :, part] = analysis.astype(BF16).astype(F32)
    chunk = 16
    taps = stencil(jnp.broadcast_to(speed[...], (8, lanes)))
    low = iota(8, lanes, 1) < lanes // 2

    def rows_at(step, carry):
        parts = []
        for half in range(chunk // 8):
            at = pl.ds(pl.multiple_of(step * chunk + half * 8, 8), 8)
            tiles = [
                [fields[a, at, k * lanes : (k + 1) * lanes] for k in range(size // lanes)]
                for a in range(count)
            ]
            parts.append(transport(tiles, taps, low))
        at = pl.ds(pl.multiple_of(step * chunk, chunk), chunk)
        for a in range(count):
            for k in range(size // lanes):
                value = jnp.concatenate([part[a][k] for part in parts], axis=0)
                out[a, at, k * lanes : (k + 1) * lanes] = value.astype(BF16)
        return carry

    lax.fori_loop(0, total // chunk, rows_at, 0)


def forecasts(state, transform, rest, speed):
    count, total, size = state.shape
    return pl.pallas_call(
        forecast_kernel,
        in_specs=[WHOLE, pl.BlockSpec(memory_space=pl.ANY), WHOLE, WHOLE],
        out_specs=WHOLE,
        out_shape=jax.ShapeDtypeStruct((count, total, size), BF16),
        scratch_shapes=[
            pltpu.VMEM((count, total, total), BF16),
            pltpu.VMEM((count, total, size), F32),
            pltpu.SemaphoreType.DMA((count,)),
        ],
        compiler_params=pltpu.CompilerParams(vmem_limit_bytes=40 * MIB),
        name="forecast",
    )(state, transform, rest, speed)


def analysis_kernel(state, transform, out):
    mean, pert = centred(state[0])
    out[0] = (dot_bf16(transform[0], pert) + mean).astype(BF16)


def analyses(state, transform):
    count, total, size = state.shape
    return pl.pallas_call(
        analysis_kernel,
        grid=(count,),
        in_specs=[
            pl.BlockSpec((1, total, size), lambda a: (a, 0, 0)),
            pl.BlockSpec((1, total, total), lambda a: (a, 0, 0)),
        ],
        out_specs=pl.BlockSpec((1, total, size), lambda a: (a, 0, 0)),
        out_shape=jax.ShapeDtypeStruct((count, total, size), BF16),
        compiler_params=params(1),
        name="analysis",
    )(state, transform)


def shared_transport(analysis, speed, width, jump):
    count, total, size = analysis.shape
    lanes = speed.shape[1]
    cells = lanes // width
    tiles = size // lanes
    fields = widened(analysis, jump).reshape(count + 2, total, tiles, width, cells)
    fields = fields.transpose(1, 0, 3, 2, 4).reshape(total, -1, cells).astype(F32)
    c = speed[0, :cells]
    for _ in range(STEPS):
        prior, here, after = fields[:, :-2], fields[:, 1:-1], fields[:, 2:]
        fields = (1.0 - c * c) * here + 0.5 * (c * c - c) * after + 0.5 * (c * c + c) * prior
    spare = tiles * width - STEPS
    fields = fields[:, spare : fields.shape[1] - spare].astype(BF16)
    fields = fields.reshape(total, count, width, tiles, cells)
    return fields.transpose(1, 0, 3, 2, 4).reshape(count, total, size)


def widened(blocks, jump):
    count = lax.axis_size("sub")
    forward = [(i, (i + jump) % count) for i in range(count)]
    backward = [(target, source) for source, target in forward]
    low = lax.ppermute(blocks[-1:], "sub", forward)
    high = lax.ppermute(blocks[:1], "sub", backward)
    return jnp.concatenate([low, blocks, high], axis=0)


def advance(member_state, hx_values, obs_value, obs_var, courant):
    slabs, local, cells_a, cols = member_state.shape
    patches, own = hx_values.shape[3:]
    owners = lax.axis_size("mem")
    lines = lax.axis_size("sub")
    width = patches // owners
    count = slabs * width
    groups = lines // count
    total = local * owners
    cells_b = cols // patches
    lane_cells = width * cells_b
    place = lax.axis_index("sub") % count
    slab, part = place // width, place % width

    index_groups = None
    if groups > 1:
        held = count * owners
        index_groups = [list(range(g * held, (g + 1) * held)) for g in range(groups)]

    def exchange(blocks):
        return lax.all_to_all(
            blocks,
            ("sub", "mem"),
            split_axis=0,
            concat_axis=0,
            tiled=True,
            axis_index_groups=index_groups,
        )

    hx_rows = exchange(pack_obs(hx_values, width).reshape(count * owners, local, own))
    hx_rows = hx_rows.reshape(count, total, own)

    stats = jnp.stack([obs_value[:, 0], obs_var[:, 0]], axis=2)
    stats = lax.all_gather(stats, "sub", axis=0)
    stats = lax.dynamic_slice(stats, (0, slab, part, 0, 0), (lines, 1, 1, 2, own))
    stats = stats.reshape(lines, 2, own).astype(F32)
    half = own // 2
    stats = jnp.concatenate(
        [jnp.roll(stats, 1, 0)[:, :, half:], stats, jnp.roll(stats, -1, 0)[:, :, :half]], axis=2
    )
    if groups > 1:
        first = lax.axis_index("sub") // count * count
        stats = lax.dynamic_slice_in_dim(stats, first, count, axis=0)
    taper = (jnp.arange(half, dtype=F32) + 1.0) / (half + 1.0)
    local_weight = jnp.concatenate([taper, jnp.ones((own,), F32), taper[::-1]])
    obs_rows = stats[:, 0:1]
    scale_rows = local_weight / stats[:, 1:2]

    state = exchange(pack_state(member_state, width, owners).reshape(count * owners, local, -1))
    state = state.reshape(count, total, -1)

    held_rows = hx_rows if groups == 1 else widened(hx_rows, count)
    transform, rest = transforms(held_rows, obs_rows, scale_rows, count, groups == 1)

    column = (lax.axis_index("mem") * width + part) * cells_b
    speed = lax.dynamic_slice(courant, (slab, column), (1, cells_b))
    speed = jnp.concatenate([speed] * width, axis=1)
    if groups == 1 and 2 * cells_b == 128 and width == 2 and cells_a // width >= STEPS:
        fields = forecasts(state, transform, rest, speed)
    else:
        fields = shared_transport(analyses(state, transform), speed, width, count)
    back = exchange(fields.reshape(count * owners, local, -1))
    return unpack_state(back.reshape(slabs, width, owners, local, -1), cells_a)


def solution(mesh):
    in_specs = (
        P(None, "mem", "sub", None),
        P(None, "mem", "sub", None, None),
        P(None, "sub", "mem", None),
        P(None, "sub", "mem", None),
        P(),
    )
    out_specs = P(None, "mem", "sub", None)
    return jax.shard_map(advance, mesh=mesh, in_specs=in_specs, out_specs=out_specs, check_vma=False)
```

```python
import jax
import jax.numpy as jnp
from jax import lax
from jax.experimental import pallas as pl
from jax.experimental.pallas import tpu as pltpu
from jax.sharding import PartitionSpec as P

ITERS = 4
STEPS = 4
F32 = jnp.float32
BF16 = jnp.bfloat16
MIB = 1024 * 1024
WHOLE = pl.BlockSpec(memory_space=pltpu.VMEM)
ANY = pl.BlockSpec(memory_space=pl.ANY)


def params(count, limit=48):
    return pltpu.CompilerParams(
        dimension_semantics=("arbitrary",) * count, vmem_limit_bytes=limit * MIB
    )


def split(value, size):
    return value >> (size.bit_length() - 1), value & (size - 1)


def iota(rows, cols, dim):
    return lax.broadcasted_iota(jnp.int32, (rows, cols), dim)


def dot_bf16(left, right):
    return jnp.dot(left, right, preferred_element_type=F32)


def moved(left, right):
    return dot_bf16(left, right).astype(BF16)


def ones_at(condition):
    return jnp.where(condition, 1.0, 0.0).astype(BF16)


def pack_obs_kernel(rows, out, order, held, packed, in_sems, out_sems):
    slabs, width, owners, local, own = packed.shape
    patches = width * owners
    block = order.shape[0] // patches
    count = local // block
    copies = [
        pltpu.make_async_copy(
            rows.at[slab, pl.ds(at * block, block)],
            held.at[slab, pl.ds(at * block, block)],
            in_sems.at[slab * count + at],
        )
        for slab in range(slabs)
        for at in range(count)
    ]
    for copy in copies:
        copy.start()
    rest, member = split(iota(*order.shape, 0), block)
    side, owner = split(rest, owners)
    order[...] = ones_at(iota(*order.shape, 1) == member * patches + owner * width + side)
    sent = []
    for slab in range(slabs):
        for at in range(count):
            copies[slab * count + at].wait()
            here = slice(at * block, (at + 1) * block)
            flat = moved(order[...], held[slab, here].reshape(block * patches, own))
            packed[slab, :, :, here, :] = flat.reshape(width, owners, block, own)
        sent.append(pltpu.make_async_copy(packed.at[slab], out.at[slab], out_sems.at[slab]))
        sent[-1].start()
    for copy in sent:
        copy.wait()


def pack_obs(hx_values, width):
    slabs, local, _, patches, own = hx_values.shape
    owners = patches // width
    block = 16
    return pl.pallas_call(
        pack_obs_kernel,
        in_specs=[ANY],
        out_specs=ANY,
        out_shape=jax.ShapeDtypeStruct((slabs, width, owners, local, own), BF16),
        scratch_shapes=[
            pltpu.VMEM((block * patches, block * patches), BF16),
            pltpu.VMEM((slabs, local, patches, own), BF16),
            pltpu.VMEM((slabs, width, owners, local, own), BF16),
            pltpu.SemaphoreType.DMA((slabs * local // block,)),
            pltpu.SemaphoreType.DMA((slabs,)),
        ],
        compiler_params=pltpu.CompilerParams(vmem_limit_bytes=60 * MIB),
        name="pack_obs",
    )(hx_values.reshape(slabs, local, patches, own))


def swapped(width, lanes):
    size = width * lanes
    outer, cell = split(iota(size, size, 1), lanes // width)
    first, second = split(outer, width)
    return ones_at(iota(size, size, 0) == (second * width + first) * (lanes // width) + cell)


def transposed(outer, inner):
    size = outer * inner
    first, second = split(iota(size, size, 0), inner)
    return ones_at(iota(size, size, 1) == second * outer + first)


def pack_state_kernel(cells, out, order, swap):
    _, width, owners, block, size = out.shape
    lanes = cells.shape[3] // owners
    tiles = size // lanes

    @pl.when((pl.program_id(0) == 0) & (pl.program_id(1) == 0))
    def _():
        order[...] = transposed(cells.shape[2], block)
        swap[...] = swapped(width, lanes)

    rows = moved(order[...], cells[...].reshape(order.shape[0], cells.shape[3]))
    parts = []
    for owner in range(owners):
        for tile in range(tiles):
            pieces = [
                rows[
                    (half * tiles + tile) * block : (half * tiles + tile + 1) * block,
                    owner * lanes : (owner + 1) * lanes,
                ]
                for half in range(width)
            ]
            parts.append(jnp.concatenate(pieces, axis=1))
    mixed = moved(jnp.concatenate(parts, axis=0), swap[...])
    for owner in range(owners):
        for tile in range(tiles):
            at = (owner * tiles + tile) * block
            for part in range(width):
                out[0, part, owner, :, tile * lanes : (tile + 1) * lanes] = mixed[
                    at : at + block, part * lanes : (part + 1) * lanes
                ]


def pack_state(member_state, width, owners):
    slabs, local, cells_a, cols = member_state.shape
    lanes = cols // owners
    size = cells_a * lanes // width
    block = 32
    return pl.pallas_call(
        pack_state_kernel,
        grid=(slabs, local // block),
        in_specs=[
            pl.BlockSpec((1, block, cells_a, cols), lambda s, g: (s, g, 0, 0)),
        ],
        out_specs=pl.BlockSpec((1, width, owners, block, size), lambda s, g: (s, 0, 0, g, 0)),
        out_shape=jax.ShapeDtypeStruct((slabs, width, owners, local, size), BF16),
        scratch_shapes=[
            pltpu.VMEM((block * cells_a, block * cells_a), BF16),
            pltpu.VMEM((width * lanes, width * lanes), BF16),
        ],
        compiler_params=params(2, 60),
        name="pack_state",
    )(member_state)


def unpack_state_kernel(packed, out, held, sems):
    slabs, width, owners, local, size = packed.shape
    cells_a = out.shape[2]
    tiles = cells_a // width
    lanes = size // tiles
    count = sems.shape[0] // slabs
    block = local // count
    order = transposed(block, cells_a)
    swap = swapped(width, lanes)
    sent = []
    for slab in range(slabs):
        for at in range(count):
            here = slice(at * block, (at + 1) * block)
            parts = []
            for owner in range(owners):
                for tile in range(tiles):
                    pieces = [
                        packed[slab, part, owner, here, tile * lanes : (tile + 1) * lanes]
                        for part in range(width)
                    ]
                    parts.append(jnp.concatenate(pieces, axis=1))
            mixed = moved(jnp.concatenate(parts, axis=0), swap)
            columns = []
            for owner in range(owners):
                rows = []
                for cell in range(cells_a):
                    half, tile = cell // tiles, cell % tiles
                    start = (owner * tiles + tile) * block
                    rows.append(mixed[start : start + block, half * lanes : (half + 1) * lanes])
                columns.append(jnp.concatenate(rows, axis=0))
            rows = moved(order, jnp.concatenate(columns, axis=1))
            held[slab, here] = rows.reshape(block, cells_a, owners * lanes)
            sent.append(
                pltpu.make_async_copy(
                    held.at[slab, pl.ds(at * block, block)],
                    out.at[slab, pl.ds(at * block, block)],
                    sems.at[slab * count + at],
                )
            )
            sent[-1].start()
    for copy in sent:
        copy.wait()


def unpack_state(packed, cells_a):
    slabs, width, owners, local, size = packed.shape
    lanes = size * width // cells_a
    shape = (slabs, local, cells_a, owners * lanes)
    block = 32
    return pl.pallas_call(
        unpack_state_kernel,
        in_specs=[WHOLE],
        out_specs=ANY,
        out_shape=jax.ShapeDtypeStruct(shape, BF16),
        scratch_shapes=[
            pltpu.VMEM(shape, BF16),
            pltpu.SemaphoreType.DMA((slabs * local // block,)),
        ],
        compiler_params=pltpu.CompilerParams(vmem_limit_bytes=48 * MIB),
        name="unpack_state",
    )(packed)


def transform_kernel(before, middle, after, obs, scale, out, rest, pert, weighted):
    total = middle.shape[1]
    half = before.shape[2]
    projected = jnp.zeros((total, 1), F32)
    start = 0
    for part in (before, middle, after):
        span = part.shape[2]
        for at in range(0, span, half):
            cols = slice(start, start + half)
            values = part[0, :, at : at + half].astype(F32)
            mean = jnp.sum(values, axis=0, keepdims=True) * (1.0 / total)
            centred = values - mean
            pert[:, cols] = centred.astype(BF16)
            scaled = (centred * scale[0, :, cols]).astype(BF16)
            weighted[:, cols] = scaled
            innovation = obs[0, :, cols] - mean
            projected += jnp.sum(scaled.astype(F32) * innovation, axis=1, keepdims=True)
            start += half
    diagonal = iota(total, total, 0) == iota(total, total, 1)
    gram = lax.dot_general(
        weighted[...], pert[...], (((1,), (1,)), ((), ())), preferred_element_type=F32
    )
    system = jnp.where(diagonal, total - 1.0, 0.0) + gram
    bound = jnp.max(jnp.sum(jnp.abs(system), axis=1, keepdims=True), axis=0, keepdims=True)
    root = (system / bound).astype(BF16)
    inverse = None
    for iteration in range(ITERS):
        product = root.astype(F32) if inverse is None else dot_bf16(inverse.astype(BF16), root)
        correction = (jnp.where(diagonal, 1.5, 0.0) - 0.5 * product).astype(BF16)
        if iteration + 1 < ITERS:
            root = moved(root, correction)
        if inverse is None:
            inverse = correction.astype(F32)
        else:
            inverse = dot_bf16(correction, inverse.astype(BF16))
    flipped = inverse.T
    halfway = jnp.sum(flipped * projected, axis=0, keepdims=True)
    weight = jnp.sum(inverse * halfway, axis=1, keepdims=True)
    weight = jnp.broadcast_to(weight, (total, 128)).T[0:1, :] / bound
    result = (jnp.sqrt((total - 1.0) / bound) * flipped + weight).astype(BF16)
    out[0] = result
    sums = jnp.sum(result.astype(F32), axis=1, keepdims=True)
    rest[0] = jnp.broadcast_to(1.0 - sums, (total, 128))


def transforms(hx_rows, obs_rows, scale_rows, count, wraps):
    held, total, own = hx_rows.shape
    half = own // 2
    shift = 0 if wraps else 1
    flops = count * (2 * total * total * 2 * own + 18 * total**3)
    return pl.pallas_call(
        transform_kernel,
        grid=(count,),
        in_specs=[
            pl.BlockSpec((1, total, half), lambda a: ((a + shift + held - 1) % held, 0, 1)),
            pl.BlockSpec((1, total, own), lambda a: (a + shift, 0, 0)),
            pl.BlockSpec((1, total, half), lambda a: ((a + shift + 1) % held, 0, 0)),
            pl.BlockSpec((1, 1, 2 * own), lambda a: (a, 0, 0)),
            pl.BlockSpec((1, 1, 2 * own), lambda a: (a, 0, 0)),
        ],
        out_specs=[
            pl.BlockSpec((1, total, total), lambda a: (a, 0, 0)),
            pl.BlockSpec((1, total, 128), lambda a: (a, 0, 0)),
        ],
        out_shape=[
            jax.ShapeDtypeStruct((count, total, total), BF16),
            jax.ShapeDtypeStruct((count, total, 128), F32),
        ],
        scratch_shapes=[pltpu.VMEM((total, 2 * own), BF16), pltpu.VMEM((total, 2 * own), BF16)],
        compiler_params=params(1),
        cost_estimate=pl.CostEstimate(
            flops=flops, bytes_accessed=4 * count * total * total * 2, transcendentals=0
        ),
        name="transform",
    )(hx_rows, hx_rows, hx_rows, obs_rows, scale_rows)


def centred(values):
    values = values.astype(F32)
    mean = jnp.sum(values, axis=0, keepdims=True) * (1.0 / values.shape[0])
    return mean, (values - mean).astype(BF16)


def stencil(c):
    step = [0.5 * (c * c + c), 1.0 - c * c, 0.5 * (c * c - c)]
    taps = step
    for _ in range(STEPS - 1):
        longer = [jnp.zeros_like(c)] * (len(taps) + 2)
        for i, tap in enumerate(taps):
            for j, weight in enumerate(step):
                longer[i + j] = longer[i + j] + tap * weight
        taps = longer
    return taps


def transport(tiles, taps, low):
    count, depth = len(tiles), len(tiles[0])
    shift = tiles[0][0].shape[1] // 2
    turned = [[pltpu.roll(tile, shift, 1) for tile in column] for column in tiles]
    results = []
    for a in range(count):
        before = [jnp.where(low, u, v) for u, v in zip(turned[(a - 1) % count], turned[a])]
        after = [jnp.where(low, u, v) for u, v in zip(turned[a], turned[(a + 1) % count])]
        line = before + tiles[a] + after
        start = depth - STEPS
        results.append(
            [sum(taps[t] * line[start + k + t] for t in range(len(taps))) for k in range(depth)]
        )
    return results


def forecast_kernel(state, transforms, rests, speed, out, transform, rest, fields, sems):
    count, total, size = out.shape
    lanes = speed.shape[1]
    copies = [
        [
            pltpu.make_async_copy(source.at[a], target.at[a], sems.at[i, a])
            for i, (source, target) in enumerate(((transforms, transform), (rests, rest)))
        ]
        for a in range(count)
    ]
    for pair in copies:
        for copy in pair:
            copy.start()
    for a in range(count):
        mean = jnp.sum(state[a].astype(F32), axis=0, keepdims=True) * (1.0 / total)
        for copy in copies[a]:
            copy.wait()
        values = dot_bf16(transform[a], state[a])
        for k in range(size // lanes):
            part = slice(k * lanes, (k + 1) * lanes)
            analysis = values[:, part] + rest[a] * mean[:, part]
            fields[a, :, part] = analysis.astype(BF16).astype(F32)
    chunk = 16
    taps = stencil(jnp.broadcast_to(speed[...], (8, lanes)))
    low = iota(8, lanes, 1) < lanes // 2

    def rows_at(step, carry):
        parts = []
        for half in range(chunk // 8):
            at = pl.ds(pl.multiple_of(step * chunk + half * 8, 8), 8)
            tiles = [
                [fields[a, at, k * lanes : (k + 1) * lanes] for k in range(size // lanes)]
                for a in range(count)
            ]
            parts.append(transport(tiles, taps, low))
        at = pl.ds(pl.multiple_of(step * chunk, chunk), chunk)
        for a in range(count):
            for k in range(size // lanes):
                value = jnp.concatenate([part[a][k] for part in parts], axis=0)
                out[a, at, k * lanes : (k + 1) * lanes] = value.astype(BF16)
        return carry

    lax.fori_loop(0, total // chunk, rows_at, 0)


def forecasts(state, transform, rest, speed):
    count, total, size = state.shape
    return pl.pallas_call(
        forecast_kernel,
        in_specs=[WHOLE, ANY, ANY, WHOLE],
        out_specs=WHOLE,
        out_shape=jax.ShapeDtypeStruct((count, total, size), BF16),
        scratch_shapes=[
            pltpu.VMEM((count, total, total), BF16),
            pltpu.VMEM(rest.shape, F32),
            pltpu.VMEM((count, total, size), F32),
            pltpu.SemaphoreType.DMA((2, count)),
        ],
        compiler_params=pltpu.CompilerParams(vmem_limit_bytes=48 * MIB),
        name="forecast",
    )(state, transform, rest, speed)


def analysis_kernel(state, transform, out):
    mean, pert = centred(state[0])
    out[0] = (dot_bf16(transform[0], pert) + mean).astype(BF16)


def analyses(state, transform):
    count, total, size = state.shape
    return pl.pallas_call(
        analysis_kernel,
        grid=(count,),
        in_specs=[
            pl.BlockSpec((1, total, size), lambda a: (a, 0, 0)),
            pl.BlockSpec((1, total, total), lambda a: (a, 0, 0)),
        ],
        out_specs=pl.BlockSpec((1, total, size), lambda a: (a, 0, 0)),
        out_shape=jax.ShapeDtypeStruct((count, total, size), BF16),
        compiler_params=params(1),
        name="analysis",
    )(state, transform)


def shared_transport(analysis, speed, width, jump):
    count, total, size = analysis.shape
    lanes = speed.shape[1]
    cells = lanes // width
    tiles = size // lanes
    fields = widened(analysis, jump).reshape(count + 2, total, tiles, width, cells)
    fields = fields.transpose(1, 0, 3, 2, 4).reshape(total, -1, cells).astype(F32)
    c = speed[0, :cells]
    for _ in range(STEPS):
        prior, here, after = fields[:, :-2], fields[:, 1:-1], fields[:, 2:]
        fields = (1.0 - c * c) * here + 0.5 * (c * c - c) * after + 0.5 * (c * c + c) * prior
    spare = tiles * width - STEPS
    fields = fields[:, spare : fields.shape[1] - spare].astype(BF16)
    fields = fields.reshape(total, count, width, tiles, cells)
    return fields.transpose(1, 0, 3, 2, 4).reshape(count, total, size)


def widened(blocks, jump):
    count = lax.axis_size("sub")
    forward = [(i, (i + jump) % count) for i in range(count)]
    backward = [(target, source) for source, target in forward]
    low = lax.ppermute(blocks[-1:], "sub", forward)
    high = lax.ppermute(blocks[:1], "sub", backward)
    return jnp.concatenate([low, blocks, high], axis=0)


def advance(member_state, hx_values, obs_value, obs_var, courant):
    slabs, local, cells_a, cols = member_state.shape
    patches, own = hx_values.shape[3:]
    owners = lax.axis_size("mem")
    lines = lax.axis_size("sub")
    width = patches // owners
    count = slabs * width
    groups = lines // count
    total = local * owners
    cells_b = cols // patches
    lane_cells = width * cells_b
    place = lax.axis_index("sub") % count
    slab, part = place // width, place % width

    index_groups = None
    if groups > 1:
        held = count * owners
        index_groups = [list(range(g * held, (g + 1) * held)) for g in range(groups)]

    def exchange(blocks):
        return lax.all_to_all(
            blocks,
            ("sub", "mem"),
            split_axis=0,
            concat_axis=0,
            tiled=True,
            axis_index_groups=index_groups,
        )

    hx_rows = exchange(pack_obs(hx_values, width).reshape(count * owners, local, own))
    hx_rows = hx_rows.reshape(count, total, own)

    stats = jnp.stack([obs_value[:, 0], obs_var[:, 0]], axis=2)
    stats = lax.all_gather(stats, "sub", axis=0)
    stats = lax.dynamic_slice(stats, (0, slab, part, 0, 0), (lines, 1, 1, 2, own))
    stats = stats.reshape(lines, 2, own).astype(F32)
    half = own // 2
    stats = jnp.concatenate(
        [jnp.roll(stats, 1, 0)[:, :, half:], stats, jnp.roll(stats, -1, 0)[:, :, :half]], axis=2
    )
    if groups > 1:
        first = lax.axis_index("sub") // count * count
        stats = lax.dynamic_slice_in_dim(stats, first, count, axis=0)
    taper = (jnp.arange(half, dtype=F32) + 1.0) / (half + 1.0)
    local_weight = jnp.concatenate([taper, jnp.ones((own,), F32), taper[::-1]])
    obs_rows = stats[:, 0:1]
    scale_rows = local_weight / stats[:, 1:2]

    state = exchange(pack_state(member_state, width, owners).reshape(count * owners, local, -1))
    state = state.reshape(count, total, -1)

    held_rows = hx_rows if groups == 1 else widened(hx_rows, count)
    transform, rest = transforms(held_rows, obs_rows, scale_rows, count, groups == 1)

    column = (lax.axis_index("mem") * width + part) * cells_b
    speed = lax.dynamic_slice(courant, (slab, column), (1, cells_b))
    speed = jnp.concatenate([speed] * width, axis=1)
    if groups == 1 and 2 * cells_b == 128 and width == 2 and cells_a // width >= STEPS:
        fields = forecasts(state, transform, rest, speed)
    else:
        fields = shared_transport(analyses(state, transform), speed, width, count)
    back = exchange(fields.reshape(count * owners, local, -1))
    return unpack_state(back.reshape(slabs, width, owners, local, -1), cells_a)


def solution(mesh):
    in_specs = (
        P(None, "mem", "sub", None),
        P(None, "mem", "sub", None, None),
        P(None, "sub", "mem", None),
        P(None, "sub", "mem", None),
        P(),
    )
    out_specs = P(None, "mem", "sub", None)
    return jax.shard_map(advance, mesh=mesh, in_specs=in_specs, out_specs=out_specs, check_vma=False)
```

```python
import jax
import jax.numpy as jnp
from jax import lax
from jax.experimental import pallas as pl
from jax.experimental.pallas import tpu as pltpu
from jax.sharding import PartitionSpec as P

ITERS = 4
STEPS = 4
F32 = jnp.float32
BF16 = jnp.bfloat16
MIB = 1024 * 1024
WHOLE = pl.BlockSpec(memory_space=pltpu.VMEM)
ANY = pl.BlockSpec(memory_space=pl.ANY)


def params(count, limit=48):
    return pltpu.CompilerParams(
        dimension_semantics=("arbitrary",) * count, vmem_limit_bytes=limit * MIB
    )


def split(value, size):
    return value >> (size.bit_length() - 1), value & (size - 1)


def iota(rows, cols, dim):
    return lax.broadcasted_iota(jnp.int32, (rows, cols), dim)


def dot_bf16(left, right):
    return jnp.dot(left, right, preferred_element_type=F32)


def moved(left, right):
    return dot_bf16(left, right).astype(BF16)


def ones_at(condition):
    return jnp.where(condition, 1.0, 0.0).astype(BF16)


def pack_obs_kernel(rows, out, order, held, packed, in_sems, out_sems):
    slabs, width, owners, local, own = packed.shape
    patches = width * owners
    block = order.shape[0] // patches
    count = local // block
    copies = [
        pltpu.make_async_copy(
            rows.at[slab, pl.ds(at * block, block)],
            held.at[slab, pl.ds(at * block, block)],
            in_sems.at[slab * count + at],
        )
        for slab in range(slabs)
        for at in range(count)
    ]
    for copy in copies:
        copy.start()
    rest, member = split(iota(*order.shape, 0), block)
    side, owner = split(rest, owners)
    order[...] = ones_at(iota(*order.shape, 1) == member * patches + owner * width + side)
    sent = []
    for slab in range(slabs):
        for at in range(count):
            copies[slab * count + at].wait()
            here = slice(at * block, (at + 1) * block)
            flat = moved(order[...], held[slab, here].reshape(block * patches, own))
            packed[slab, :, :, here, :] = flat.reshape(width, owners, block, own)
        sent.append(pltpu.make_async_copy(packed.at[slab], out.at[slab], out_sems.at[slab]))
        sent[-1].start()
    for copy in sent:
        copy.wait()


def pack_obs(hx_values, width):
    slabs, local, _, patches, own = hx_values.shape
    owners = patches // width
    block = 16
    return pl.pallas_call(
        pack_obs_kernel,
        in_specs=[ANY],
        out_specs=ANY,
        out_shape=jax.ShapeDtypeStruct((slabs, width, owners, local, own), BF16),
        scratch_shapes=[
            pltpu.VMEM((block * patches, block * patches), BF16),
            pltpu.VMEM((slabs, local, patches, own), BF16),
            pltpu.VMEM((slabs, width, owners, local, own), BF16),
            pltpu.SemaphoreType.DMA((slabs * local // block,)),
            pltpu.SemaphoreType.DMA((slabs,)),
        ],
        compiler_params=pltpu.CompilerParams(vmem_limit_bytes=60 * MIB),
        name="pack_obs",
    )(hx_values.reshape(slabs, local, patches, own))


def swapped(width, lanes):
    size = width * lanes
    outer, cell = split(iota(size, size, 1), lanes // width)
    first, second = split(outer, width)
    return ones_at(iota(size, size, 0) == (second * width + first) * (lanes // width) + cell)


def transposed(outer, inner):
    size = outer * inner
    first, second = split(iota(size, size, 0), inner)
    return ones_at(iota(size, size, 1) == second * outer + first)


def pack_state_kernel(cells, out, order, swap):
    _, width, owners, block, size = out.shape
    lanes = cells.shape[3] // owners
    tiles = size // lanes

    @pl.when((pl.program_id(0) == 0) & (pl.program_id(1) == 0))
    def _():
        order[...] = transposed(cells.shape[2], block)
        swap[...] = swapped(width, lanes)

    rows = moved(order[...], cells[...].reshape(order.shape[0], cells.shape[3]))
    parts = []
    for owner in range(owners):
        for tile in range(tiles):
            pieces = [
                rows[
                    (half * tiles + tile) * block : (half * tiles + tile + 1) * block,
                    owner * lanes : (owner + 1) * lanes,
                ]
                for half in range(width)
            ]
            parts.append(jnp.concatenate(pieces, axis=1))
    mixed = moved(jnp.concatenate(parts, axis=0), swap[...])
    for owner in range(owners):
        for tile in range(tiles):
            at = (owner * tiles + tile) * block
            for part in range(width):
                out[0, part, owner, :, tile * lanes : (tile + 1) * lanes] = mixed[
                    at : at + block, part * lanes : (part + 1) * lanes
                ]


def pack_state(member_state, width, owners):
    slabs, local, cells_a, cols = member_state.shape
    lanes = cols // owners
    size = cells_a * lanes // width
    block = 32
    return pl.pallas_call(
        pack_state_kernel,
        grid=(slabs, local // block),
        in_specs=[
            pl.BlockSpec((1, block, cells_a, cols), lambda s, g: (s, g, 0, 0)),
        ],
        out_specs=pl.BlockSpec((1, width, owners, block, size), lambda s, g: (s, 0, 0, g, 0)),
        out_shape=jax.ShapeDtypeStruct((slabs, width, owners, local, size), BF16),
        scratch_shapes=[
            pltpu.VMEM((block * cells_a, block * cells_a), BF16),
            pltpu.VMEM((width * lanes, width * lanes), BF16),
        ],
        compiler_params=params(2, 63),
        name="pack_state",
    )(member_state)


def unpack_state_kernel(packed, out, held, sems):
    slabs, width, owners, local, size = packed.shape
    cells_a = out.shape[2]
    tiles = cells_a // width
    lanes = size // tiles
    count = sems.shape[0] // slabs
    block = local // count
    order = transposed(block, cells_a)
    swap = swapped(width, lanes)
    sent = []
    for slab in range(slabs):
        for at in range(count):
            here = slice(at * block, (at + 1) * block)
            parts = []
            for owner in range(owners):
                for tile in range(tiles):
                    pieces = [
                        packed[slab, part, owner, here, tile * lanes : (tile + 1) * lanes]
                        for part in range(width)
                    ]
                    parts.append(jnp.concatenate(pieces, axis=1))
            mixed = moved(jnp.concatenate(parts, axis=0), swap)
            columns = []
            for owner in range(owners):
                rows = []
                for cell in range(cells_a):
                    half, tile = cell // tiles, cell % tiles
                    start = (owner * tiles + tile) * block
                    rows.append(mixed[start : start + block, half * lanes : (half + 1) * lanes])
                columns.append(jnp.concatenate(rows, axis=0))
            rows = moved(order, jnp.concatenate(columns, axis=1))
            held[slab, here] = rows.reshape(block, cells_a, owners * lanes)
            sent.append(
                pltpu.make_async_copy(
                    held.at[slab, pl.ds(at * block, block)],
                    out.at[slab, pl.ds(at * block, block)],
                    sems.at[slab * count + at],
                )
            )
            sent[-1].start()
    for copy in sent:
        copy.wait()


def unpack_state(packed, cells_a):
    slabs, width, owners, local, size = packed.shape
    lanes = size * width // cells_a
    shape = (slabs, local, cells_a, owners * lanes)
    block = 32
    return pl.pallas_call(
        unpack_state_kernel,
        in_specs=[WHOLE],
        out_specs=ANY,
        out_shape=jax.ShapeDtypeStruct(shape, BF16),
        scratch_shapes=[
            pltpu.VMEM(shape, BF16),
            pltpu.SemaphoreType.DMA((slabs * local // block,)),
        ],
        compiler_params=pltpu.CompilerParams(vmem_limit_bytes=48 * MIB),
        name="unpack_state",
    )(packed)


def transform_kernel(before, middle, after, obs, scale, out, rest, pert, weighted):
    total = middle.shape[1]
    half = before.shape[2]
    projected = jnp.zeros((total, 1), F32)
    start = 0
    for part in (before, middle, after):
        span = part.shape[2]
        for at in range(0, span, half):
            cols = slice(start, start + half)
            values = part[0, :, at : at + half].astype(F32)
            mean = jnp.sum(values, axis=0, keepdims=True) * (1.0 / total)
            centred = values - mean
            pert[:, cols] = centred.astype(BF16)
            scaled = (centred * scale[0, :, cols]).astype(BF16)
            weighted[:, cols] = scaled
            innovation = obs[0, :, cols] - mean
            projected += jnp.sum(scaled.astype(F32) * innovation, axis=1, keepdims=True)
            start += half
    diagonal = iota(total, total, 0) == iota(total, total, 1)
    gram = lax.dot_general(
        weighted[...], pert[...], (((1,), (1,)), ((), ())), preferred_element_type=F32
    )
    system = jnp.where(diagonal, total - 1.0, 0.0) + gram
    bound = jnp.max(jnp.sum(jnp.abs(system), axis=1, keepdims=True), axis=0, keepdims=True)
    root = (system / bound).astype(BF16)
    inverse = None
    for iteration in range(ITERS):
        product = root.astype(F32) if inverse is None else dot_bf16(inverse.astype(BF16), root)
        correction = (jnp.where(diagonal, 1.5, 0.0) - 0.5 * product).astype(BF16)
        if iteration + 1 < ITERS:
            root = moved(root, correction)
        if inverse is None:
            inverse = correction.astype(F32)
        else:
            inverse = dot_bf16(correction, inverse.astype(BF16))
    flipped = inverse.T
    halfway = jnp.sum(flipped * projected, axis=0, keepdims=True)
    weight = jnp.sum(inverse * halfway, axis=1, keepdims=True)
    weight = jnp.broadcast_to(weight, (total, 128)).T[0:1, :] / bound
    result = (jnp.sqrt((total - 1.0) / bound) * flipped + weight).astype(BF16)
    out[0] = result
    sums = jnp.sum(result.astype(F32), axis=1, keepdims=True)
    rest[0] = jnp.broadcast_to(1.0 - sums, (total, 128))


def transforms(hx_rows, obs_rows, scale_rows, count, wraps):
    held, total, own = hx_rows.shape
    half = own // 2
    shift = 0 if wraps else 1
    flops = count * (2 * total * total * 2 * own + 18 * total**3)
    return pl.pallas_call(
        transform_kernel,
        grid=(count,),
        in_specs=[
            pl.BlockSpec((1, total, half), lambda a: ((a + shift + held - 1) % held, 0, 1)),
            pl.BlockSpec((1, total, own), lambda a: (a + shift, 0, 0)),
            pl.BlockSpec((1, total, half), lambda a: ((a + shift + 1) % held, 0, 0)),
            pl.BlockSpec((1, 1, 2 * own), lambda a: (a, 0, 0)),
            pl.BlockSpec((1, 1, 2 * own), lambda a: (a, 0, 0)),
        ],
        out_specs=[
            pl.BlockSpec((1, total, total), lambda a: (a, 0, 0)),
            pl.BlockSpec((1, total, 128), lambda a: (a, 0, 0)),
        ],
        out_shape=[
            jax.ShapeDtypeStruct((count, total, total), BF16),
            jax.ShapeDtypeStruct((count, total, 128), F32),
        ],
        scratch_shapes=[pltpu.VMEM((total, 2 * own), BF16), pltpu.VMEM((total, 2 * own), BF16)],
        compiler_params=params(1, 32),
        cost_estimate=pl.CostEstimate(
            flops=flops, bytes_accessed=4 * count * total * total * 2, transcendentals=0
        ),
        name="transform",
    )(hx_rows, hx_rows, hx_rows, obs_rows, scale_rows)


def centred(values):
    values = values.astype(F32)
    mean = jnp.sum(values, axis=0, keepdims=True) * (1.0 / values.shape[0])
    return mean, (values - mean).astype(BF16)


def stencil(c):
    step = [0.5 * (c * c + c), 1.0 - c * c, 0.5 * (c * c - c)]
    taps = step
    for _ in range(STEPS - 1):
        longer = [jnp.zeros_like(c)] * (len(taps) + 2)
        for i, tap in enumerate(taps):
            for j, weight in enumerate(step):
                longer[i + j] = longer[i + j] + tap * weight
        taps = longer
    return taps


def transport(tiles, taps, low):
    count, depth = len(tiles), len(tiles[0])
    shift = tiles[0][0].shape[1] // 2
    turned = [[pltpu.roll(tile, shift, 1) for tile in column] for column in tiles]
    results = []
    for a in range(count):
        before = [jnp.where(low, u, v) for u, v in zip(turned[(a - 1) % count], turned[a])]
        after = [jnp.where(low, u, v) for u, v in zip(turned[a], turned[(a + 1) % count])]
        line = before + tiles[a] + after
        start = depth - STEPS
        results.append(
            [sum(taps[t] * line[start + k + t] for t in range(len(taps))) for k in range(depth)]
        )
    return results


def forecast_kernel(state, transform, rest, speed, out, fields):
    count, total, size = out.shape
    lanes = speed.shape[1]
    for a in range(count):
        mean = jnp.sum(state[a].astype(F32), axis=0, keepdims=True) * (1.0 / total)
        values = dot_bf16(transform[a], state[a])
        for k in range(size // lanes):
            part = slice(k * lanes, (k + 1) * lanes)
            analysis = values[:, part] + rest[a] * mean[:, part]
            fields[a, :, part] = analysis.astype(BF16).astype(F32)
    chunk = 16
    taps = stencil(jnp.broadcast_to(speed[...], (8, lanes)))
    low = iota(8, lanes, 1) < lanes // 2

    def rows_at(step, carry):
        parts = []
        for half in range(chunk // 8):
            at = pl.ds(pl.multiple_of(step * chunk + half * 8, 8), 8)
            tiles = [
                [fields[a, at, k * lanes : (k + 1) * lanes] for k in range(size // lanes)]
                for a in range(count)
            ]
            parts.append(transport(tiles, taps, low))
        at = pl.ds(pl.multiple_of(step * chunk, chunk), chunk)
        for a in range(count):
            for k in range(size // lanes):
                value = jnp.concatenate([part[a][k] for part in parts], axis=0)
                out[a, at, k * lanes : (k + 1) * lanes] = value.astype(BF16)
        return carry

    lax.fori_loop(0, total // chunk, rows_at, 0)


def forecasts(state, transform, rest, speed):
    count, total, size = state.shape
    return pl.pallas_call(
        forecast_kernel,
        in_specs=[WHOLE] * 4,
        out_specs=WHOLE,
        out_shape=jax.ShapeDtypeStruct((count, total, size), BF16),
        scratch_shapes=[pltpu.VMEM((count, total, size), F32)],
        compiler_params=pltpu.CompilerParams(vmem_limit_bytes=20 * MIB),
        name="forecast",
    )(state, transform, rest, speed)


def analysis_kernel(state, transform, out):
    mean, pert = centred(state[0])
    out[0] = (dot_bf16(transform[0], pert) + mean).astype(BF16)


def analyses(state, transform):
    count, total, size = state.shape
    return pl.pallas_call(
        analysis_kernel,
        grid=(count,),
        in_specs=[
            pl.BlockSpec((1, total, size), lambda a: (a, 0, 0)),
            pl.BlockSpec((1, total, total), lambda a: (a, 0, 0)),
        ],
        out_specs=pl.BlockSpec((1, total, size), lambda a: (a, 0, 0)),
        out_shape=jax.ShapeDtypeStruct((count, total, size), BF16),
        compiler_params=params(1),
        name="analysis",
    )(state, transform)


def shared_transport(analysis, speed, width, jump):
    count, total, size = analysis.shape
    lanes = speed.shape[1]
    cells = lanes // width
    tiles = size // lanes
    fields = widened(analysis, jump).reshape(count + 2, total, tiles, width, cells)
    fields = fields.transpose(1, 0, 3, 2, 4).reshape(total, -1, cells).astype(F32)
    c = speed[0, :cells]
    for _ in range(STEPS):
        prior, here, after = fields[:, :-2], fields[:, 1:-1], fields[:, 2:]
        fields = (1.0 - c * c) * here + 0.5 * (c * c - c) * after + 0.5 * (c * c + c) * prior
    spare = tiles * width - STEPS
    fields = fields[:, spare : fields.shape[1] - spare].astype(BF16)
    fields = fields.reshape(total, count, width, tiles, cells)
    return fields.transpose(1, 0, 3, 2, 4).reshape(count, total, size)


def widened(blocks, jump):
    count = lax.axis_size("sub")
    forward = [(i, (i + jump) % count) for i in range(count)]
    backward = [(target, source) for source, target in forward]
    low = lax.ppermute(blocks[-1:], "sub", forward)
    high = lax.ppermute(blocks[:1], "sub", backward)
    return jnp.concatenate([low, blocks, high], axis=0)


def advance(member_state, hx_values, obs_value, obs_var, courant):
    slabs, local, cells_a, cols = member_state.shape
    patches, own = hx_values.shape[3:]
    owners = lax.axis_size("mem")
    lines = lax.axis_size("sub")
    width = patches // owners
    count = slabs * width
    groups = lines // count
    total = local * owners
    cells_b = cols // patches
    lane_cells = width * cells_b
    place = lax.axis_index("sub") % count
    slab, part = place // width, place % width

    index_groups = None
    if groups > 1:
        held = count * owners
        index_groups = [list(range(g * held, (g + 1) * held)) for g in range(groups)]

    def exchange(blocks):
        return lax.all_to_all(
            blocks,
            ("sub", "mem"),
            split_axis=0,
            concat_axis=0,
            tiled=True,
            axis_index_groups=index_groups,
        )

    hx_rows = exchange(pack_obs(hx_values, width).reshape(count * owners, local, own))
    hx_rows = hx_rows.reshape(count, total, own)

    stats = jnp.stack([obs_value[:, 0], obs_var[:, 0]], axis=2)
    stats = lax.all_gather(stats, "sub", axis=0)
    stats = lax.dynamic_slice(stats, (0, slab, part, 0, 0), (lines, 1, 1, 2, own))
    stats = stats.reshape(lines, 2, own).astype(F32)
    half = own // 2
    stats = jnp.concatenate(
        [jnp.roll(stats, 1, 0)[:, :, half:], stats, jnp.roll(stats, -1, 0)[:, :, :half]], axis=2
    )
    if groups > 1:
        first = lax.axis_index("sub") // count * count
        stats = lax.dynamic_slice_in_dim(stats, first, count, axis=0)
    taper = (jnp.arange(half, dtype=F32) + 1.0) / (half + 1.0)
    local_weight = jnp.concatenate([taper, jnp.ones((own,), F32), taper[::-1]])
    obs_rows = stats[:, 0:1]
    scale_rows = local_weight / stats[:, 1:2]

    state = exchange(pack_state(member_state, width, owners).reshape(count * owners, local, -1))
    state = state.reshape(count, total, -1)

    held_rows = hx_rows if groups == 1 else widened(hx_rows, count)
    transform, rest = transforms(held_rows, obs_rows, scale_rows, count, groups == 1)

    column = (lax.axis_index("mem") * width + part) * cells_b
    speed = lax.dynamic_slice(courant, (slab, column), (1, cells_b))
    speed = jnp.concatenate([speed] * width, axis=1)
    if groups == 1 and 2 * cells_b == 128 and width == 2 and cells_a // width >= STEPS:
        fields = forecasts(state, transform, rest, speed)
    else:
        fields = shared_transport(analyses(state, transform), speed, width, count)
    back = exchange(fields.reshape(count * owners, local, -1))
    return unpack_state(back.reshape(slabs, width, owners, local, -1), cells_a)


def solution(mesh):
    in_specs = (
        P(None, "mem", "sub", None),
        P(None, "mem", "sub", None, None),
        P(None, "sub", "mem", None),
        P(None, "sub", "mem", None),
        P(),
    )
    out_specs = P(None, "mem", "sub", None)
    return jax.shard_map(advance, mesh=mesh, in_specs=in_specs, out_specs=out_specs, check_vma=False)
```

```python
import jax
import jax.numpy as jnp
from jax import lax
from jax.experimental import pallas as pl
from jax.experimental.pallas import tpu as pltpu
from jax.sharding import PartitionSpec as P

ITERS = 4
STEPS = 4
PIECES = 2
F32 = jnp.float32
BF16 = jnp.bfloat16
MIB = 1024 * 1024
WHOLE = pl.BlockSpec(memory_space=pltpu.VMEM)
ANY = pl.BlockSpec(memory_space=pl.ANY)


def params(count, limit=48):
    return pltpu.CompilerParams(
        dimension_semantics=("arbitrary",) * count, vmem_limit_bytes=limit * MIB
    )


def split(value, size):
    return value >> (size.bit_length() - 1), value & (size - 1)


def iota(rows, cols, dim):
    return lax.broadcasted_iota(jnp.int32, (rows, cols), dim)


def dot_bf16(left, right):
    return jnp.dot(left, right, preferred_element_type=F32)


def moved(left, right):
    return dot_bf16(left, right).astype(BF16)


def ones_at(condition):
    return jnp.where(condition, 1.0, 0.0).astype(BF16)


def pack_obs_kernel(rows, out, order, held, packed, in_sems, out_sems):
    slabs, width, owners, local, own = packed.shape
    patches = width * owners
    block = order.shape[0] // patches
    count = local // block
    copies = [
        pltpu.make_async_copy(
            rows.at[slab, pl.ds(at * block, block)],
            held.at[slab, pl.ds(at * block, block)],
            in_sems.at[slab * count + at],
        )
        for slab in range(slabs)
        for at in range(count)
    ]
    for copy in copies:
        copy.start()
    rest, member = split(iota(*order.shape, 0), block)
    side, owner = split(rest, owners)
    order[...] = ones_at(iota(*order.shape, 1) == member * patches + owner * width + side)
    sent = []
    for slab in range(slabs):
        for at in range(count):
            copies[slab * count + at].wait()
            here = slice(at * block, (at + 1) * block)
            flat = moved(order[...], held[slab, here].reshape(block * patches, own))
            packed[slab, :, :, here, :] = flat.reshape(width, owners, block, own)
            rows_here = pl.ds(at * block, block)
            sent.append(
                pltpu.make_async_copy(
                    packed.at[slab, :, :, rows_here],
                    out.at[slab, :, :, rows_here],
                    out_sems.at[slab * count + at],
                )
            )
            sent[-1].start()
    for copy in sent:
        copy.wait()


def pack_obs(hx_values, width):
    slabs, local, _, patches, own = hx_values.shape
    owners = patches // width
    block = 16
    return pl.pallas_call(
        pack_obs_kernel,
        in_specs=[ANY],
        out_specs=ANY,
        out_shape=jax.ShapeDtypeStruct((slabs, width, owners, local, own), BF16),
        scratch_shapes=[
            pltpu.VMEM((block * patches, block * patches), BF16),
            pltpu.VMEM((slabs, local, patches, own), BF16),
            pltpu.VMEM((slabs, width, owners, local, own), BF16),
            pltpu.SemaphoreType.DMA((slabs * local // block,)),
            pltpu.SemaphoreType.DMA((slabs * local // block,)),
        ],
        compiler_params=pltpu.CompilerParams(vmem_limit_bytes=60 * MIB),
        name="pack_obs",
    )(hx_values.reshape(slabs, local, patches, own))


def swapped(width, lanes):
    size = width * lanes
    outer, cell = split(iota(size, size, 1), lanes // width)
    first, second = split(outer, width)
    return ones_at(iota(size, size, 0) == (second * width + first) * (lanes // width) + cell)


def transposed(outer, inner):
    size = outer * inner
    first, second = split(iota(size, size, 0), inner)
    return ones_at(iota(size, size, 1) == second * outer + first)


def pack_state_kernel(cells, out, order, swap):
    _, width, owners, block, size = out.shape
    lanes = cells.shape[3] // owners
    tiles = size // lanes

    @pl.when((pl.program_id(0) == 0) & (pl.program_id(1) == 0))
    def _():
        order[...] = transposed(cells.shape[2], block)
        swap[...] = swapped(width, lanes)

    rows = moved(order[...], cells[...].reshape(order.shape[0], cells.shape[3]))
    parts = []
    for owner in range(owners):
        for tile in range(tiles):
            pieces = [
                rows[
                    (half * tiles + tile) * block : (half * tiles + tile + 1) * block,
                    owner * lanes : (owner + 1) * lanes,
                ]
                for half in range(width)
            ]
            parts.append(jnp.concatenate(pieces, axis=1))
    mixed = moved(jnp.concatenate(parts, axis=0), swap[...])
    for owner in range(owners):
        for tile in range(tiles):
            at = (owner * tiles + tile) * block
            for part in range(width):
                out[0, part, owner, :, tile * lanes : (tile + 1) * lanes] = mixed[
                    at : at + block, part * lanes : (part + 1) * lanes
                ]


def pack_state(member_state, width, owners):
    slabs, local, cells_a, cols = member_state.shape
    lanes = cols // owners
    size = cells_a * lanes // width
    block = 32
    return pl.pallas_call(
        pack_state_kernel,
        grid=(slabs, local // block),
        in_specs=[
            pl.BlockSpec((1, block, cells_a, cols), lambda s, g: (s, g, 0, 0)),
        ],
        out_specs=pl.BlockSpec((1, width, owners, block, size), lambda s, g: (s, 0, 0, g, 0)),
        out_shape=jax.ShapeDtypeStruct((slabs, width, owners, local, size), BF16),
        scratch_shapes=[
            pltpu.VMEM((block * cells_a, block * cells_a), BF16),
            pltpu.VMEM((width * lanes, width * lanes), BF16),
        ],
        compiler_params=params(2, 63),
        name="pack_state",
    )(member_state)


def unpack_state_kernel(packed, out, held, sems):
    slabs, width, owners, local, size = packed.shape
    cells_a = out.shape[2]
    tiles = cells_a // width
    lanes = size // tiles
    count = sems.shape[0] // slabs
    block = local // count
    order = transposed(block, cells_a)
    swap = swapped(width, lanes)
    sent = []
    for slab in range(slabs):
        for at in range(count):
            here = slice(at * block, (at + 1) * block)
            parts = []
            for owner in range(owners):
                for tile in range(tiles):
                    pieces = [
                        packed[slab, part, owner, here, tile * lanes : (tile + 1) * lanes]
                        for part in range(width)
                    ]
                    parts.append(jnp.concatenate(pieces, axis=1))
            mixed = moved(jnp.concatenate(parts, axis=0), swap)
            columns = []
            for owner in range(owners):
                rows = []
                for cell in range(cells_a):
                    half, tile = cell // tiles, cell % tiles
                    start = (owner * tiles + tile) * block
                    rows.append(mixed[start : start + block, half * lanes : (half + 1) * lanes])
                columns.append(jnp.concatenate(rows, axis=0))
            rows = moved(order, jnp.concatenate(columns, axis=1))
            held[slab, here] = rows.reshape(block, cells_a, owners * lanes)
            sent.append(
                pltpu.make_async_copy(
                    held.at[slab, pl.ds(at * block, block)],
                    out.at[slab, pl.ds(at * block, block)],
                    sems.at[slab * count + at],
                )
            )
            sent[-1].start()
    for copy in sent:
        copy.wait()


def unpack_state(packed, cells_a):
    slabs, width, owners, local, size = packed.shape
    lanes = size * width // cells_a
    shape = (slabs, local, cells_a, owners * lanes)
    block = 32
    return pl.pallas_call(
        unpack_state_kernel,
        in_specs=[WHOLE],
        out_specs=ANY,
        out_shape=jax.ShapeDtypeStruct(shape, BF16),
        scratch_shapes=[
            pltpu.VMEM(shape, BF16),
            pltpu.SemaphoreType.DMA((slabs * local // block,)),
        ],
        compiler_params=pltpu.CompilerParams(vmem_limit_bytes=48 * MIB),
        name="unpack_state",
    )(packed)


def transform_kernel(before, middle, after, obs, scale, *refs):
    *outs, rest, pert, weighted = refs
    total = middle.shape[1]
    half = before.shape[2]
    projected = jnp.zeros((total, 1), F32)
    start = 0
    for part in (before, middle, after):
        span = part.shape[2]
        for at in range(0, span, half):
            cols = slice(start, start + half)
            values = part[0, :, at : at + half].astype(F32)
            mean = jnp.sum(values, axis=0, keepdims=True) * (1.0 / total)
            centred = values - mean
            pert[:, cols] = centred.astype(BF16)
            scaled = (centred * scale[0, :, cols]).astype(BF16)
            weighted[:, cols] = scaled
            innovation = obs[0, :, cols] - mean
            projected += jnp.sum(scaled.astype(F32) * innovation, axis=1, keepdims=True)
            start += half
    diagonal = iota(total, total, 0) == iota(total, total, 1)
    gram = lax.dot_general(
        weighted[...], pert[...], (((1,), (1,)), ((), ())), preferred_element_type=F32
    )
    system = jnp.where(diagonal, total - 1.0, 0.0) + gram
    bound = jnp.max(jnp.sum(jnp.abs(system), axis=1, keepdims=True), axis=0, keepdims=True)
    root = (system / bound).astype(BF16)
    inverse = None
    for iteration in range(ITERS):
        product = root.astype(F32) if inverse is None else dot_bf16(inverse.astype(BF16), root)
        correction = (jnp.where(diagonal, 1.5, 0.0) - 0.5 * product).astype(BF16)
        if iteration + 1 < ITERS:
            root = moved(root, correction)
        if inverse is None:
            inverse = correction.astype(F32)
        else:
            inverse = dot_bf16(correction, inverse.astype(BF16))
    flipped = inverse.T
    halfway = jnp.sum(flipped * projected, axis=0, keepdims=True)
    weight = jnp.sum(inverse * halfway, axis=1, keepdims=True)
    weight = jnp.broadcast_to(weight, (total, 128)).T[0:1, :] / bound
    result = (jnp.sqrt((total - 1.0) / bound) * flipped + weight).astype(BF16)
    a = pl.program_id(0)
    span = pl.num_programs(0) // len(outs)
    for number, out in enumerate(outs):

        @pl.when((a >= number * span) & (a < (number + 1) * span))
        def _(out=out):
            out[0] = result

    sums = jnp.sum(result.astype(F32), axis=1, keepdims=True)
    rest[0] = jnp.broadcast_to(1.0 - sums, (total, 128))


def transforms(hx_rows, obs_rows, scale_rows, count, wraps):
    held, total, own = hx_rows.shape
    half = own // 2
    shift = 0 if wraps else 1
    flops = count * (2 * total * total * 2 * own + 18 * total**3)
    span = count // PIECES

    def held_at(number):
        return lambda a: (jnp.clip(a - number * span, 0, span - 1), 0, 0)

    return pl.pallas_call(
        transform_kernel,
        grid=(count,),
        in_specs=[
            pl.BlockSpec((1, total, half), lambda a: ((a + shift + held - 1) % held, 0, 1)),
            pl.BlockSpec((1, total, own), lambda a: (a + shift, 0, 0)),
            pl.BlockSpec((1, total, half), lambda a: ((a + shift + 1) % held, 0, 0)),
            pl.BlockSpec((1, 1, 2 * own), lambda a: (a, 0, 0)),
            pl.BlockSpec((1, 1, 2 * own), lambda a: (a, 0, 0)),
        ],
        out_specs=[
            *[pl.BlockSpec((1, total, total), held_at(number)) for number in range(PIECES)],
            pl.BlockSpec((1, total, 128), lambda a: (a, 0, 0)),
        ],
        out_shape=[
            *[jax.ShapeDtypeStruct((span, total, total), BF16)] * PIECES,
            jax.ShapeDtypeStruct((count, total, 128), F32),
        ],
        scratch_shapes=[pltpu.VMEM((total, 2 * own), BF16), pltpu.VMEM((total, 2 * own), BF16)],
        compiler_params=params(1, 32),
        cost_estimate=pl.CostEstimate(
            flops=flops, bytes_accessed=4 * count * total * total * 2, transcendentals=0
        ),
        name="transform",
    )(hx_rows, hx_rows, hx_rows, obs_rows, scale_rows)


def centred(values):
    values = values.astype(F32)
    mean = jnp.sum(values, axis=0, keepdims=True) * (1.0 / values.shape[0])
    return mean, (values - mean).astype(BF16)


def stencil(c):
    step = [0.5 * (c * c + c), 1.0 - c * c, 0.5 * (c * c - c)]
    taps = step
    for _ in range(STEPS - 1):
        longer = [jnp.zeros_like(c)] * (len(taps) + 2)
        for i, tap in enumerate(taps):
            for j, weight in enumerate(step):
                longer[i + j] = longer[i + j] + tap * weight
        taps = longer
    return taps


def transport(tiles, taps, low):
    count, depth = len(tiles), len(tiles[0])
    shift = tiles[0][0].shape[1] // 2
    turned = [[pltpu.roll(tile, shift, 1) for tile in column] for column in tiles]
    results = []
    for a in range(count):
        before = [jnp.where(low, u, v) for u, v in zip(turned[(a - 1) % count], turned[a])]
        after = [jnp.where(low, u, v) for u, v in zip(turned[a], turned[(a + 1) % count])]
        line = before + tiles[a] + after
        start = depth - STEPS
        results.append(
            [sum(taps[t] * line[start + k + t] for t in range(len(taps))) for k in range(depth)]
        )
    return results


def forecast_kernel(state, *refs):
    *transforms, rest, speed, out, fields = refs
    count, total, size = out.shape
    span = count // len(transforms)
    lanes = speed.shape[1]
    for a in range(count):
        mean = jnp.sum(state[a].astype(F32), axis=0, keepdims=True) * (1.0 / total)
        values = dot_bf16(transforms[a // span][a % span], state[a])
        for k in range(size // lanes):
            part = slice(k * lanes, (k + 1) * lanes)
            analysis = values[:, part] + rest[a] * mean[:, part]
            fields[a, :, part] = analysis
    chunk = 16
    taps = stencil(jnp.broadcast_to(speed[...], (8, lanes)))
    low = iota(8, lanes, 1) < lanes // 2

    def rows_at(step, carry):
        parts = []
        for half in range(chunk // 8):
            at = pl.ds(pl.multiple_of(step * chunk + half * 8, 8), 8)
            tiles = [
                [fields[a, at, k * lanes : (k + 1) * lanes] for k in range(size // lanes)]
                for a in range(count)
            ]
            parts.append(transport(tiles, taps, low))
        at = pl.ds(pl.multiple_of(step * chunk, chunk), chunk)
        for a in range(count):
            for k in range(size // lanes):
                value = jnp.concatenate([part[a][k] for part in parts], axis=0)
                out[a, at, k * lanes : (k + 1) * lanes] = value.astype(BF16)
        return carry

    lax.fori_loop(0, total // chunk, rows_at, 0)


def forecasts(state, transform, rest, speed):
    count, total, size = state.shape
    return pl.pallas_call(
        forecast_kernel,
        in_specs=[WHOLE] * (3 + len(transform)),
        out_specs=WHOLE,
        out_shape=jax.ShapeDtypeStruct((count, total, size), BF16),
        scratch_shapes=[pltpu.VMEM((count, total, size), F32)],
        compiler_params=pltpu.CompilerParams(vmem_limit_bytes=20 * MIB),
        name="forecast",
    )(state, *transform, rest, speed)


def analysis_kernel(state, transform, out):
    mean, pert = centred(state[0])
    out[0] = (dot_bf16(transform[0], pert) + mean).astype(BF16)


def analyses(state, transform):
    count, total, size = state.shape
    return pl.pallas_call(
        analysis_kernel,
        grid=(count,),
        in_specs=[
            pl.BlockSpec((1, total, size), lambda a: (a, 0, 0)),
            pl.BlockSpec((1, total, total), lambda a: (a, 0, 0)),
        ],
        out_specs=pl.BlockSpec((1, total, size), lambda a: (a, 0, 0)),
        out_shape=jax.ShapeDtypeStruct((count, total, size), BF16),
        compiler_params=params(1),
        name="analysis",
    )(state, transform)


def shared_transport(analysis, speed, width, jump):
    count, total, size = analysis.shape
    lanes = speed.shape[1]
    cells = lanes // width
    tiles = size // lanes
    fields = widened(analysis, jump).reshape(count + 2, total, tiles, width, cells)
    fields = fields.transpose(1, 0, 3, 2, 4).reshape(total, -1, cells).astype(F32)
    c = speed[0, :cells]
    for _ in range(STEPS):
        prior, here, after = fields[:, :-2], fields[:, 1:-1], fields[:, 2:]
        fields = (1.0 - c * c) * here + 0.5 * (c * c - c) * after + 0.5 * (c * c + c) * prior
    spare = tiles * width - STEPS
    fields = fields[:, spare : fields.shape[1] - spare].astype(BF16)
    fields = fields.reshape(total, count, width, tiles, cells)
    return fields.transpose(1, 0, 3, 2, 4).reshape(count, total, size)


def widened(blocks, jump):
    count = lax.axis_size("sub")
    forward = [(i, (i + jump) % count) for i in range(count)]
    backward = [(target, source) for source, target in forward]
    low = lax.ppermute(blocks[-1:], "sub", forward)
    high = lax.ppermute(blocks[:1], "sub", backward)
    return jnp.concatenate([low, blocks, high], axis=0)


def advance(member_state, hx_values, obs_value, obs_var, courant):
    slabs, local, cells_a, cols = member_state.shape
    patches, own = hx_values.shape[3:]
    owners = lax.axis_size("mem")
    lines = lax.axis_size("sub")
    width = patches // owners
    count = slabs * width
    groups = lines // count
    total = local * owners
    cells_b = cols // patches
    lane_cells = width * cells_b
    place = lax.axis_index("sub") % count
    slab, part = place // width, place % width

    index_groups = None
    if groups > 1:
        held = count * owners
        index_groups = [list(range(g * held, (g + 1) * held)) for g in range(groups)]

    def exchange(blocks):
        return lax.all_to_all(
            blocks,
            ("sub", "mem"),
            split_axis=0,
            concat_axis=0,
            tiled=True,
            axis_index_groups=index_groups,
        )

    hx_rows = exchange(pack_obs(hx_values, width).reshape(count * owners, local, own))
    hx_rows = hx_rows.reshape(count, total, own)

    stats = jnp.stack([obs_value[:, 0], obs_var[:, 0]], axis=2)
    stats = lax.all_gather(stats, "sub", axis=0)
    stats = lax.dynamic_slice(stats, (0, slab, part, 0, 0), (lines, 1, 1, 2, own))
    stats = stats.reshape(lines, 2, own).astype(F32)
    half = own // 2
    stats = jnp.concatenate(
        [jnp.roll(stats, 1, 0)[:, :, half:], stats, jnp.roll(stats, -1, 0)[:, :, :half]], axis=2
    )
    if groups > 1:
        first = lax.axis_index("sub") // count * count
        stats = lax.dynamic_slice_in_dim(stats, first, count, axis=0)
    taper = (jnp.arange(half, dtype=F32) + 1.0) / (half + 1.0)
    local_weight = jnp.concatenate([taper, jnp.ones((own,), F32), taper[::-1]])
    obs_rows = stats[:, 0:1]
    scale_rows = local_weight / stats[:, 1:2]

    state = exchange(pack_state(member_state, width, owners).reshape(count * owners, local, -1))
    state = state.reshape(count, total, -1)

    held_rows = hx_rows if groups == 1 else widened(hx_rows, count)
    *transform, rest = transforms(held_rows, obs_rows, scale_rows, count, groups == 1)

    column = (lax.axis_index("mem") * width + part) * cells_b
    speed = lax.dynamic_slice(courant, (slab, column), (1, cells_b))
    speed = jnp.concatenate([speed] * width, axis=1)
    if groups == 1 and 2 * cells_b == 128 and width == 2 and cells_a // width >= STEPS:
        fields = forecasts(state, transform, rest, speed)
    else:
        fields = shared_transport(analyses(state, jnp.concatenate(transform)), speed, width, count)
    back = exchange(fields.reshape(count * owners, local, -1))
    return unpack_state(back.reshape(slabs, width, owners, local, -1), cells_a)


def solution(mesh):
    in_specs = (
        P(None, "mem", "sub", None),
        P(None, "mem", "sub", None, None),
        P(None, "sub", "mem", None),
        P(None, "sub", "mem", None),
        P(),
    )
    out_specs = P(None, "mem", "sub", None)
    return jax.shard_map(advance, mesh=mesh, in_specs=in_specs, out_specs=out_specs, check_vma=False)
```

```python
import jax
import jax.numpy as jnp
from jax import lax
from jax.experimental import pallas as pl
from jax.experimental.pallas import tpu as pltpu
from jax.sharding import PartitionSpec as P

ITERS = 4
STEPS = 4
F32 = jnp.float32
BF16 = jnp.bfloat16
MIB = 1024 * 1024
WHOLE = pl.BlockSpec(memory_space=pltpu.VMEM)
ANY = pl.BlockSpec(memory_space=pl.ANY)


def params(count, limit=48):
    return pltpu.CompilerParams(
        dimension_semantics=("arbitrary",) * count, vmem_limit_bytes=limit * MIB
    )


def split(value, size):
    return value >> (size.bit_length() - 1), value & (size - 1)


def iota(rows, cols, dim):
    return lax.broadcasted_iota(jnp.int32, (rows, cols), dim)


def dot_bf16(left, right):
    return jnp.dot(left, right, preferred_element_type=F32)


def moved(left, right):
    return dot_bf16(left, right).astype(BF16)


def ones_at(condition):
    return jnp.where(condition, 1.0, 0.0).astype(BF16)


def pack_obs_kernel(rows, out, order, held, packed, in_sems, out_sems):
    slabs, width, owners, local, own = packed.shape
    patches = width * owners
    block = order.shape[0] // patches
    count = local // block
    copies = [
        pltpu.make_async_copy(
            rows.at[slab, pl.ds(at * block, block)],
            held.at[slab, pl.ds(at * block, block)],
            in_sems.at[slab * count + at],
        )
        for slab in range(slabs)
        for at in range(count)
    ]
    for copy in copies:
        copy.start()
    rest, member = split(iota(*order.shape, 0), block)
    side, owner = split(rest, owners)
    order[...] = ones_at(iota(*order.shape, 1) == member * patches + owner * width + side)
    sent = []
    for slab in range(slabs):
        for at in range(count):
            copies[slab * count + at].wait()
            here = slice(at * block, (at + 1) * block)
            flat = moved(order[...], held[slab, here].reshape(block * patches, own))
            packed[slab, :, :, here, :] = flat.reshape(width, owners, block, own)
            rows_here = pl.ds(at * block, block)
            sent.append(
                pltpu.make_async_copy(
                    packed.at[slab, :, :, rows_here],
                    out.at[slab, :, :, rows_here],
                    out_sems.at[slab * count + at],
                )
            )
            sent[-1].start()
    for copy in sent:
        copy.wait()


def pack_obs(hx_values, width):
    slabs, local, _, patches, own = hx_values.shape
    owners = patches // width
    block = 16
    return pl.pallas_call(
        pack_obs_kernel,
        in_specs=[ANY],
        out_specs=ANY,
        out_shape=jax.ShapeDtypeStruct((slabs, width, owners, local, own), BF16),
        scratch_shapes=[
            pltpu.VMEM((block * patches, block * patches), BF16),
            pltpu.VMEM((slabs, local, patches, own), BF16),
            pltpu.VMEM((slabs, width, owners, local, own), BF16),
            pltpu.SemaphoreType.DMA((slabs * local // block,)),
            pltpu.SemaphoreType.DMA((slabs * local // block,)),
        ],
        compiler_params=pltpu.CompilerParams(vmem_limit_bytes=60 * MIB),
        name="pack_obs",
    )(hx_values.reshape(slabs, local, patches, own))


def swapped(width, lanes):
    size = width * lanes
    outer, cell = split(iota(size, size, 1), lanes // width)
    first, second = split(outer, width)
    return ones_at(iota(size, size, 0) == (second * width + first) * (lanes // width) + cell)


def transposed(outer, inner):
    size = outer * inner
    first, second = split(iota(size, size, 0), inner)
    return ones_at(iota(size, size, 1) == second * outer + first)


def pack_state_kernel(cells, out, order, swap):
    _, width, owners, block, size = out.shape
    lanes = cells.shape[3] // owners
    tiles = size // lanes

    @pl.when((pl.program_id(0) == 0) & (pl.program_id(1) == 0))
    def _():
        order[...] = transposed(cells.shape[2], block)
        swap[...] = swapped(width, lanes)

    rows = moved(order[...], cells[...].reshape(order.shape[0], cells.shape[3]))
    parts = []
    for owner in range(owners):
        for tile in range(tiles):
            pieces = [
                rows[
                    (half * tiles + tile) * block : (half * tiles + tile + 1) * block,
                    owner * lanes : (owner + 1) * lanes,
                ]
                for half in range(width)
            ]
            parts.append(jnp.concatenate(pieces, axis=1))
    mixed = moved(jnp.concatenate(parts, axis=0), swap[...])
    for owner in range(owners):
        for tile in range(tiles):
            at = (owner * tiles + tile) * block
            for part in range(width):
                out[0, part, owner, :, tile * lanes : (tile + 1) * lanes] = mixed[
                    at : at + block, part * lanes : (part + 1) * lanes
                ]


def pack_state(member_state, width, owners):
    slabs, local, cells_a, cols = member_state.shape
    lanes = cols // owners
    size = cells_a * lanes // width
    block = 32
    return pl.pallas_call(
        pack_state_kernel,
        grid=(slabs, local // block),
        in_specs=[
            pl.BlockSpec((1, block, cells_a, cols), lambda s, g: (s, g, 0, 0)),
        ],
        out_specs=pl.BlockSpec((1, width, owners, block, size), lambda s, g: (s, 0, 0, g, 0)),
        out_shape=jax.ShapeDtypeStruct((slabs, width, owners, local, size), BF16),
        scratch_shapes=[
            pltpu.VMEM((block * cells_a, block * cells_a), BF16),
            pltpu.VMEM((width * lanes, width * lanes), BF16),
        ],
        compiler_params=params(2, 63),
        name="pack_state",
    )(member_state)


def unpack_state_kernel(packed, out, held, sems):
    slabs, width, owners, local, size = packed.shape
    cells_a = out.shape[2]
    tiles = cells_a // width
    lanes = size // tiles
    count = sems.shape[0] // slabs
    block = local // count
    order = transposed(block, cells_a)
    swap = swapped(width, lanes)
    sent = []
    for slab in range(slabs):
        for at in range(count):
            here = slice(at * block, (at + 1) * block)
            parts = []
            for owner in range(owners):
                for tile in range(tiles):
                    pieces = [
                        packed[slab, part, owner, here, tile * lanes : (tile + 1) * lanes]
                        for part in range(width)
                    ]
                    parts.append(jnp.concatenate(pieces, axis=1))
            mixed = moved(jnp.concatenate(parts, axis=0), swap)
            columns = []
            for owner in range(owners):
                rows = []
                for cell in range(cells_a):
                    half, tile = cell // tiles, cell % tiles
                    start = (owner * tiles + tile) * block
                    rows.append(mixed[start : start + block, half * lanes : (half + 1) * lanes])
                columns.append(jnp.concatenate(rows, axis=0))
            rows = moved(order, jnp.concatenate(columns, axis=1))
            held[slab, here] = rows.reshape(block, cells_a, owners * lanes)
            sent.append(
                pltpu.make_async_copy(
                    held.at[slab, pl.ds(at * block, block)],
                    out.at[slab, pl.ds(at * block, block)],
                    sems.at[slab * count + at],
                )
            )
            sent[-1].start()
    for copy in sent:
        copy.wait()


def unpack_state(packed, cells_a):
    slabs, width, owners, local, size = packed.shape
    lanes = size * width // cells_a
    shape = (slabs, local, cells_a, owners * lanes)
    block = 32
    return pl.pallas_call(
        unpack_state_kernel,
        in_specs=[WHOLE],
        out_specs=ANY,
        out_shape=jax.ShapeDtypeStruct(shape, BF16),
        scratch_shapes=[
            pltpu.VMEM(shape, BF16),
            pltpu.SemaphoreType.DMA((slabs * local // block,)),
        ],
        compiler_params=pltpu.CompilerParams(vmem_limit_bytes=48 * MIB),
        name="unpack_state",
    )(packed)


def transform_kernel(before, middle, after, obs, scale, out, pert, weighted):
    total = middle.shape[1]
    half = before.shape[2]
    projected = jnp.zeros((total, 1), F32)
    start = 0
    for part in (before, middle, after):
        span = part.shape[2]
        for at in range(0, span, half):
            cols = slice(start, start + half)
            values = part[0, :, at : at + half].astype(F32)
            mean = jnp.sum(values, axis=0, keepdims=True) * (1.0 / total)
            centred = values - mean
            pert[:, cols] = centred.astype(BF16)
            scaled = (centred * scale[0, :, cols]).astype(BF16)
            weighted[:, cols] = scaled
            innovation = obs[0, :, cols] - mean
            projected += jnp.sum(scaled.astype(F32) * innovation, axis=1, keepdims=True)
            start += half
    diagonal = iota(total, total, 0) == iota(total, total, 1)
    gram = lax.dot_general(
        weighted[...], pert[...], (((1,), (1,)), ((), ())), preferred_element_type=F32
    )
    system = jnp.where(diagonal, total - 1.0, 0.0) + gram
    bound = jnp.max(jnp.sum(jnp.abs(system), axis=1, keepdims=True), axis=0, keepdims=True)
    root = (system / bound).astype(BF16)
    inverse = None
    for iteration in range(ITERS):
        product = root.astype(F32) if inverse is None else dot_bf16(inverse.astype(BF16), root)
        correction = (jnp.where(diagonal, 1.5, 0.0) - 0.5 * product).astype(BF16)
        if iteration + 1 < ITERS:
            root = moved(root, correction)
        if inverse is None:
            inverse = correction.astype(F32)
        else:
            inverse = dot_bf16(correction, inverse.astype(BF16))
    flipped = inverse.T
    halfway = jnp.sum(flipped * projected, axis=0, keepdims=True)
    weight = jnp.sum(inverse * halfway, axis=1, keepdims=True)
    weight = jnp.broadcast_to(weight, (total, 128)).T[0:1, :] / bound
    out[0] = (jnp.sqrt((total - 1.0) / bound) * flipped + weight).astype(BF16)


def transforms(hx_rows, obs_rows, scale_rows, count, wraps):
    held, total, own = hx_rows.shape
    half = own // 2
    shift = 0 if wraps else 1
    flops = count * (2 * total * total * 2 * own + 18 * total**3)
    return pl.pallas_call(
        transform_kernel,
        grid=(count,),
        in_specs=[
            pl.BlockSpec((1, total, half), lambda a: ((a + shift + held - 1) % held, 0, 1)),
            pl.BlockSpec((1, total, own), lambda a: (a + shift, 0, 0)),
            pl.BlockSpec((1, total, half), lambda a: ((a + shift + 1) % held, 0, 0)),
            pl.BlockSpec((1, 1, 2 * own), lambda a: (a, 0, 0)),
            pl.BlockSpec((1, 1, 2 * own), lambda a: (a, 0, 0)),
        ],
        out_specs=pl.BlockSpec((1, total, total), lambda a: (a, 0, 0)),
        out_shape=jax.ShapeDtypeStruct((count, total, total), BF16),
        scratch_shapes=[pltpu.VMEM((total, 2 * own), BF16), pltpu.VMEM((total, 2 * own), BF16)],
        compiler_params=params(1, 32),
        cost_estimate=pl.CostEstimate(
            flops=flops, bytes_accessed=4 * count * total * total * 2, transcendentals=0
        ),
        name="transform",
    )(hx_rows, hx_rows, hx_rows, obs_rows, scale_rows)


def centred(values):
    values = values.astype(F32)
    mean = jnp.sum(values, axis=0, keepdims=True) * (1.0 / values.shape[0])
    return mean, (values - mean).astype(BF16)


def stencil(c):
    step = [0.5 * (c * c + c), 1.0 - c * c, 0.5 * (c * c - c)]
    taps = step
    for _ in range(STEPS - 1):
        longer = [jnp.zeros_like(c)] * (len(taps) + 2)
        for i, tap in enumerate(taps):
            for j, weight in enumerate(step):
                longer[i + j] = longer[i + j] + tap * weight
        taps = longer
    return taps


def transport(tiles, taps, low):
    count, depth = len(tiles), len(tiles[0])
    shift = tiles[0][0].shape[1] // 2
    turned = [[pltpu.roll(tile, shift, 1) for tile in column] for column in tiles]
    results = []
    for a in range(count):
        before = [jnp.where(low, u, v) for u, v in zip(turned[(a - 1) % count], turned[a])]
        after = [jnp.where(low, u, v) for u, v in zip(turned[a], turned[(a + 1) % count])]
        line = before + tiles[a] + after
        start = depth - STEPS
        results.append(
            [sum(taps[t] * line[start + k + t] for t in range(len(taps))) for k in range(depth)]
        )
    return results


def forecast_kernel(state, transform, speed, out, fields):
    count, total, size = out.shape
    lanes = speed.shape[1]
    for a in range(count):
        mean = jnp.sum(state[a].astype(F32), axis=0, keepdims=True) * (1.0 / total)
        values = dot_bf16(transform[a], state[a])
        rest = 1.0 - dot_bf16(transform[a], jnp.ones((total, lanes), BF16))
        for k in range(size // lanes):
            part = slice(k * lanes, (k + 1) * lanes)
            fields[a, :, part] = values[:, part] + rest * mean[:, part]
    chunk = 16
    taps = stencil(jnp.broadcast_to(speed[...], (8, lanes)))
    low = iota(8, lanes, 1) < lanes // 2

    def rows_at(step, carry):
        parts = []
        for half in range(chunk // 8):
            at = pl.ds(pl.multiple_of(step * chunk + half * 8, 8), 8)
            tiles = [
                [fields[a, at, k * lanes : (k + 1) * lanes] for k in range(size // lanes)]
                for a in range(count)
            ]
            parts.append(transport(tiles, taps, low))
        at = pl.ds(pl.multiple_of(step * chunk, chunk), chunk)
        for a in range(count):
            for k in range(size // lanes):
                value = jnp.concatenate([part[a][k] for part in parts], axis=0)
                out[a, at, k * lanes : (k + 1) * lanes] = value.astype(BF16)
        return carry

    lax.fori_loop(0, total // chunk, rows_at, 0)


def forecasts(state, transform, speed):
    count, total, size = state.shape
    return pl.pallas_call(
        forecast_kernel,
        in_specs=[WHOLE] * 3,
        out_specs=WHOLE,
        out_shape=jax.ShapeDtypeStruct((count, total, size), BF16),
        scratch_shapes=[pltpu.VMEM((count, total, size), F32)],
        compiler_params=pltpu.CompilerParams(vmem_limit_bytes=20 * MIB),
        name="forecast",
    )(state, transform, speed)


def analysis_kernel(state, transform, out):
    mean, pert = centred(state[0])
    out[0] = (dot_bf16(transform[0], pert) + mean).astype(BF16)


def analyses(state, transform):
    count, total, size = state.shape
    return pl.pallas_call(
        analysis_kernel,
        grid=(count,),
        in_specs=[
            pl.BlockSpec((1, total, size), lambda a: (a, 0, 0)),
            pl.BlockSpec((1, total, total), lambda a: (a, 0, 0)),
        ],
        out_specs=pl.BlockSpec((1, total, size), lambda a: (a, 0, 0)),
        out_shape=jax.ShapeDtypeStruct((count, total, size), BF16),
        compiler_params=params(1),
        name="analysis",
    )(state, transform)


def shared_transport(analysis, speed, width, jump):
    count, total, size = analysis.shape
    lanes = speed.shape[1]
    cells = lanes // width
    tiles = size // lanes
    fields = widened(analysis, jump).reshape(count + 2, total, tiles, width, cells)
    fields = fields.transpose(1, 0, 3, 2, 4).reshape(total, -1, cells).astype(F32)
    c = speed[0, :cells]
    for _ in range(STEPS):
        prior, here, after = fields[:, :-2], fields[:, 1:-1], fields[:, 2:]
        fields = (1.0 - c * c) * here + 0.5 * (c * c - c) * after + 0.5 * (c * c + c) * prior
    spare = tiles * width - STEPS
    fields = fields[:, spare : fields.shape[1] - spare].astype(BF16)
    fields = fields.reshape(total, count, width, tiles, cells)
    return fields.transpose(1, 0, 3, 2, 4).reshape(count, total, size)


def widened(blocks, jump):
    count = lax.axis_size("sub")
    forward = [(i, (i + jump) % count) for i in range(count)]
    backward = [(target, source) for source, target in forward]
    low = lax.ppermute(blocks[-1:], "sub", forward)
    high = lax.ppermute(blocks[:1], "sub", backward)
    return jnp.concatenate([low, blocks, high], axis=0)


def advance(member_state, hx_values, obs_value, obs_var, courant):
    slabs, local, cells_a, cols = member_state.shape
    patches, own = hx_values.shape[3:]
    owners = lax.axis_size("mem")
    lines = lax.axis_size("sub")
    width = patches // owners
    count = slabs * width
    groups = lines // count
    total = local * owners
    cells_b = cols // patches
    lane_cells = width * cells_b
    place = lax.axis_index("sub") % count
    slab, part = place // width, place % width

    index_groups = None
    if groups > 1:
        held = count * owners
        index_groups = [list(range(g * held, (g + 1) * held)) for g in range(groups)]

    def exchange(blocks):
        return lax.all_to_all(
            blocks,
            ("sub", "mem"),
            split_axis=0,
            concat_axis=0,
            tiled=True,
            axis_index_groups=index_groups,
        )

    hx_rows = exchange(pack_obs(hx_values, width).reshape(count * owners, local, own))
    hx_rows = hx_rows.reshape(count, total, own)

    stats = jnp.stack([obs_value[:, 0], obs_var[:, 0]], axis=2)
    stats = lax.all_gather(stats, "sub", axis=0)
    stats = lax.dynamic_slice(stats, (0, slab, part, 0, 0), (lines, 1, 1, 2, own))
    stats = stats.reshape(lines, 2, own).astype(F32)
    half = own // 2
    stats = jnp.concatenate(
        [jnp.roll(stats, 1, 0)[:, :, half:], stats, jnp.roll(stats, -1, 0)[:, :, :half]], axis=2
    )
    if groups > 1:
        first = lax.axis_index("sub") // count * count
        stats = lax.dynamic_slice_in_dim(stats, first, count, axis=0)
    taper = (jnp.arange(half, dtype=F32) + 1.0) / (half + 1.0)
    local_weight = jnp.concatenate([taper, jnp.ones((own,), F32), taper[::-1]])
    obs_rows = stats[:, 0:1]
    scale_rows = local_weight / stats[:, 1:2]

    state = exchange(pack_state(member_state, width, owners).reshape(count * owners, local, -1))
    state = state.reshape(count, total, -1)

    held_rows = hx_rows if groups == 1 else widened(hx_rows, count)
    transform = transforms(held_rows, obs_rows, scale_rows, count, groups == 1)

    column = (lax.axis_index("mem") * width + part) * cells_b
    speed = lax.dynamic_slice(courant, (slab, column), (1, cells_b))
    speed = jnp.concatenate([speed] * width, axis=1)
    if groups == 1 and width == 2 and cells_a // width >= STEPS:
        fields = forecasts(state, transform, speed)
    else:
        fields = shared_transport(analyses(state, transform), speed, width, count)
    back = exchange(fields.reshape(count * owners, local, -1))
    return unpack_state(back.reshape(slabs, width, owners, local, -1), cells_a)


def solution(mesh):
    in_specs = (
        P(None, "mem", "sub", None),
        P(None, "mem", "sub", None, None),
        P(None, "sub", "mem", None),
        P(None, "sub", "mem", None),
        P(),
    )
    out_specs = P(None, "mem", "sub", None)
    return jax.shard_map(advance, mesh=mesh, in_specs=in_specs, out_specs=out_specs, check_vma=False)
```

```python
import jax
import jax.numpy as jnp
from jax import lax
from jax.experimental import pallas as pl
from jax.experimental.pallas import tpu as pltpu
from jax.sharding import PartitionSpec as P

ITERS = 4
STEPS = 4
F32 = jnp.float32
BF16 = jnp.bfloat16
MIB = 1024 * 1024
WHOLE = pl.BlockSpec(memory_space=pltpu.VMEM)
ANY = pl.BlockSpec(memory_space=pl.ANY)


def params(count, limit=48):
    return pltpu.CompilerParams(
        dimension_semantics=("arbitrary",) * count, vmem_limit_bytes=limit * MIB
    )


def split(value, size):
    return value >> (size.bit_length() - 1), value & (size - 1)


def iota(rows, cols, dim):
    return lax.broadcasted_iota(jnp.int32, (rows, cols), dim)


def dot_bf16(left, right):
    return jnp.dot(left, right, preferred_element_type=F32)


def moved(left, right):
    return dot_bf16(left, right).astype(BF16)


def ones_at(condition):
    return jnp.where(condition, 1.0, 0.0).astype(BF16)


def pack_obs_kernel(rows, out, order, held, packed, in_sems, out_sems):
    slabs, width, owners, local, own = packed.shape
    patches = width * owners
    block = order.shape[0] // patches
    count = local // block
    copies = [
        pltpu.make_async_copy(
            rows.at[slab, pl.ds(at * block, block)],
            held.at[slab, pl.ds(at * block, block)],
            in_sems.at[slab * count + at],
        )
        for slab in range(slabs)
        for at in range(count)
    ]
    for copy in copies:
        copy.start()
    rest, member = split(iota(*order.shape, 0), block)
    side, owner = split(rest, owners)
    order[...] = ones_at(iota(*order.shape, 1) == member * patches + owner * width + side)
    sent = []
    for slab in range(slabs):
        for at in range(count):
            copies[slab * count + at].wait()
            here = slice(at * block, (at + 1) * block)
            flat = moved(order[...], held[slab, here].reshape(block * patches, own))
            packed[slab, :, :, here, :] = flat.reshape(width, owners, block, own)
            rows_here = pl.ds(at * block, block)
            sent.append(
                pltpu.make_async_copy(
                    packed.at[slab, :, :, rows_here],
                    out.at[slab, :, :, rows_here],
                    out_sems.at[slab * count + at],
                )
            )
            sent[-1].start()
    for copy in sent:
        copy.wait()


def pack_obs(hx_values, width):
    slabs, local, _, patches, own = hx_values.shape
    owners = patches // width
    block = 16
    return pl.pallas_call(
        pack_obs_kernel,
        in_specs=[ANY],
        out_specs=ANY,
        out_shape=jax.ShapeDtypeStruct((slabs, width, owners, local, own), BF16),
        scratch_shapes=[
            pltpu.VMEM((block * patches, block * patches), BF16),
            pltpu.VMEM((slabs, local, patches, own), BF16),
            pltpu.VMEM((slabs, width, owners, local, own), BF16),
            pltpu.SemaphoreType.DMA((slabs * local // block,)),
            pltpu.SemaphoreType.DMA((slabs * local // block,)),
        ],
        compiler_params=pltpu.CompilerParams(vmem_limit_bytes=60 * MIB),
        name="pack_obs",
    )(hx_values.reshape(slabs, local, patches, own))


def swapped(width, lanes):
    size = width * lanes
    outer, cell = split(iota(size, size, 1), lanes // width)
    first, second = split(outer, width)
    return ones_at(iota(size, size, 0) == (second * width + first) * (lanes // width) + cell)


def transposed(outer, inner):
    size = outer * inner
    first, second = split(iota(size, size, 0), inner)
    return ones_at(iota(size, size, 1) == second * outer + first)


def pack_state_kernel(cells, out, order, swap):
    _, width, owners, block, size = out.shape
    lanes = cells.shape[3] // owners
    tiles = size // lanes

    @pl.when((pl.program_id(0) == 0) & (pl.program_id(1) == 0))
    def _():
        order[...] = transposed(cells.shape[2], block)
        swap[...] = swapped(width, lanes)

    rows = moved(order[...], cells[...].reshape(order.shape[0], cells.shape[3]))
    parts = []
    for owner in range(owners):
        for tile in range(tiles):
            pieces = [
                rows[
                    (half * tiles + tile) * block : (half * tiles + tile + 1) * block,
                    owner * lanes : (owner + 1) * lanes,
                ]
                for half in range(width)
            ]
            parts.append(jnp.concatenate(pieces, axis=1))
    mixed = moved(jnp.concatenate(parts, axis=0), swap[...])
    for owner in range(owners):
        for tile in range(tiles):
            at = (owner * tiles + tile) * block
            for part in range(width):
                out[0, part, owner, :, tile * lanes : (tile + 1) * lanes] = mixed[
                    at : at + block, part * lanes : (part + 1) * lanes
                ]


def pack_state(member_state, width, owners):
    slabs, local, cells_a, cols = member_state.shape
    lanes = cols // owners
    size = cells_a * lanes // width
    block = 32
    return pl.pallas_call(
        pack_state_kernel,
        grid=(slabs, local // block),
        in_specs=[
            pl.BlockSpec((1, block, cells_a, cols), lambda s, g: (s, g, 0, 0)),
        ],
        out_specs=pl.BlockSpec((1, width, owners, block, size), lambda s, g: (s, 0, 0, g, 0)),
        out_shape=jax.ShapeDtypeStruct((slabs, width, owners, local, size), BF16),
        scratch_shapes=[
            pltpu.VMEM((block * cells_a, block * cells_a), BF16),
            pltpu.VMEM((width * lanes, width * lanes), BF16),
        ],
        compiler_params=params(2, 63),
        name="pack_state",
    )(member_state)


def unpack_state_kernel(packed, out, held, sems):
    slabs, width, owners, local, size = packed.shape
    cells_a = out.shape[2]
    tiles = cells_a // width
    lanes = size // tiles
    count = sems.shape[0] // slabs
    block = local // count
    order = transposed(block, cells_a)
    swap = swapped(width, lanes)
    sent = []
    for slab in range(slabs):
        for at in range(count):
            here = slice(at * block, (at + 1) * block)
            parts = []
            for owner in range(owners):
                for tile in range(tiles):
                    pieces = [
                        packed[slab, part, owner, here, tile * lanes : (tile + 1) * lanes]
                        for part in range(width)
                    ]
                    parts.append(jnp.concatenate(pieces, axis=1))
            mixed = moved(jnp.concatenate(parts, axis=0), swap)
            columns = []
            for owner in range(owners):
                rows = []
                for cell in range(cells_a):
                    half, tile = cell // tiles, cell % tiles
                    start = (owner * tiles + tile) * block
                    rows.append(mixed[start : start + block, half * lanes : (half + 1) * lanes])
                columns.append(jnp.concatenate(rows, axis=0))
            rows = moved(order, jnp.concatenate(columns, axis=1))
            held[slab, here] = rows.reshape(block, cells_a, owners * lanes)
            sent.append(
                pltpu.make_async_copy(
                    held.at[slab, pl.ds(at * block, block)],
                    out.at[slab, pl.ds(at * block, block)],
                    sems.at[slab * count + at],
                )
            )
            sent[-1].start()
    for copy in sent:
        copy.wait()


def unpack_state(packed, cells_a):
    slabs, width, owners, local, size = packed.shape
    lanes = size * width // cells_a
    shape = (slabs, local, cells_a, owners * lanes)
    block = 32
    return pl.pallas_call(
        unpack_state_kernel,
        in_specs=[WHOLE],
        out_specs=ANY,
        out_shape=jax.ShapeDtypeStruct(shape, BF16),
        scratch_shapes=[
            pltpu.VMEM(shape, BF16),
            pltpu.SemaphoreType.DMA((slabs * local // block,)),
        ],
        compiler_params=pltpu.CompilerParams(vmem_limit_bytes=48 * MIB),
        name="unpack_state",
    )(packed)


def transform_kernel(before, middle, after, obs, scale, out, pert, weighted):
    total = middle.shape[1]
    half = before.shape[2]
    projected = jnp.zeros((total, 1), F32)
    start = 0
    for part in (before, middle, after):
        span = part.shape[2]
        for at in range(0, span, half):
            cols = slice(start, start + half)
            values = part[0, :, at : at + half].astype(F32)
            mean = jnp.sum(values, axis=0, keepdims=True) * (1.0 / total)
            centred = values - mean
            pert[:, cols] = centred.astype(BF16)
            scaled = (centred * scale[0, :, cols]).astype(BF16)
            weighted[:, cols] = scaled
            innovation = obs[0, :, cols] - mean
            projected += jnp.sum(scaled.astype(F32) * innovation, axis=1, keepdims=True)
            start += half
    diagonal = iota(total, total, 0) == iota(total, total, 1)
    gram = lax.dot_general(
        weighted[...], pert[...], (((1,), (1,)), ((), ())), preferred_element_type=F32
    )
    system = jnp.where(diagonal, total - 1.0, 0.0) + gram
    bound = jnp.max(jnp.sum(jnp.abs(system), axis=1, keepdims=True), axis=0, keepdims=True)
    root = (system / bound).astype(BF16)
    inverse = None
    for iteration in range(ITERS):
        product = root.astype(F32) if inverse is None else dot_bf16(inverse.astype(BF16), root)
        correction = (jnp.where(diagonal, 1.5, 0.0) - 0.5 * product).astype(BF16)
        if iteration + 1 < ITERS:
            root = moved(root, correction)
        if inverse is None:
            inverse = correction.astype(F32)
        else:
            inverse = dot_bf16(correction, inverse.astype(BF16))
    flipped = inverse.T
    halfway = jnp.sum(flipped * projected, axis=0, keepdims=True)
    weight = jnp.sum(inverse * halfway, axis=1, keepdims=True)
    weight = jnp.broadcast_to(weight, (total, 128)).T[0:1, :] / bound
    out[0] = (jnp.sqrt((total - 1.0) / bound) * flipped + weight).astype(BF16)


def transforms(hx_rows, obs_rows, scale_rows, count, wraps):
    held, total, own = hx_rows.shape
    half = own // 2
    shift = 0 if wraps else 1
    flops = count * (2 * total * total * 2 * own + 18 * total**3)
    return pl.pallas_call(
        transform_kernel,
        grid=(count,),
        in_specs=[
            pl.BlockSpec((1, total, half), lambda a: ((a + shift + held - 1) % held, 0, 1)),
            pl.BlockSpec((1, total, own), lambda a: (a + shift, 0, 0)),
            pl.BlockSpec((1, total, half), lambda a: ((a + shift + 1) % held, 0, 0)),
            pl.BlockSpec((1, 1, 2 * own), lambda a: (a, 0, 0)),
            pl.BlockSpec((1, 1, 2 * own), lambda a: (a, 0, 0)),
        ],
        out_specs=pl.BlockSpec((1, total, total), lambda a: (a, 0, 0)),
        out_shape=jax.ShapeDtypeStruct((count, total, total), BF16),
        scratch_shapes=[pltpu.VMEM((total, 2 * own), BF16), pltpu.VMEM((total, 2 * own), BF16)],
        compiler_params=params(1, 32),
        cost_estimate=pl.CostEstimate(
            flops=flops, bytes_accessed=4 * count * total * total * 2, transcendentals=0
        ),
        name="transform",
    )(hx_rows, hx_rows, hx_rows, obs_rows, scale_rows)


def centred(values):
    values = values.astype(F32)
    mean = jnp.sum(values, axis=0, keepdims=True) * (1.0 / values.shape[0])
    return mean, (values - mean).astype(BF16)


def stencil(c):
    step = [0.5 * (c * c + c), 1.0 - c * c, 0.5 * (c * c - c)]
    taps = step
    for _ in range(STEPS - 1):
        longer = [jnp.zeros_like(c)] * (len(taps) + 2)
        for i, tap in enumerate(taps):
            for j, weight in enumerate(step):
                longer[i + j] = longer[i + j] + tap * weight
        taps = longer
    return taps


def transport(tiles, taps, low):
    count, depth = len(tiles), len(tiles[0])
    shift = tiles[0][0].shape[1] // 2
    turned = [[pltpu.roll(tile, shift, 1) for tile in column] for column in tiles]
    results = []
    for a in range(count):
        before = [jnp.where(low, u, v) for u, v in zip(turned[(a - 1) % count], turned[a])]
        after = [jnp.where(low, u, v) for u, v in zip(turned[a], turned[(a + 1) % count])]
        line = before + tiles[a] + after
        start = depth - STEPS
        results.append(
            [sum(taps[t] * line[start + k + t] for t in range(len(taps))) for k in range(depth)]
        )
    return results


def forecast_kernel(state, transforms, speed, out, transform, fields, sems):
    count, total, size = out.shape
    lanes = speed.shape[1]
    copies = [
        pltpu.make_async_copy(transforms.at[a], transform.at[a], sems.at[a]) for a in range(count)
    ]
    for copy in copies:
        copy.start()
    means = [
        jnp.sum(state[a].astype(F32), axis=0, keepdims=True) * (1.0 / total) for a in range(count)
    ]
    for a, mean in enumerate(means):
        copies[a].wait()
        values = dot_bf16(transform[a], state[a])
        rest = 1.0 - dot_bf16(transform[a], jnp.ones((total, lanes), BF16))
        for k in range(size // lanes):
            part = slice(k * lanes, (k + 1) * lanes)
            fields[a, :, part] = values[:, part] + rest * mean[:, part]
    chunk = 16
    taps = stencil(jnp.broadcast_to(speed[...], (8, lanes)))
    low = iota(8, lanes, 1) < lanes // 2

    def rows_at(step, carry):
        parts = []
        for half in range(chunk // 8):
            at = pl.ds(pl.multiple_of(step * chunk + half * 8, 8), 8)
            tiles = [
                [fields[a, at, k * lanes : (k + 1) * lanes] for k in range(size // lanes)]
                for a in range(count)
            ]
            parts.append(transport(tiles, taps, low))
        at = pl.ds(pl.multiple_of(step * chunk, chunk), chunk)
        for a in range(count):
            for k in range(size // lanes):
                value = jnp.concatenate([part[a][k] for part in parts], axis=0)
                out[a, at, k * lanes : (k + 1) * lanes] = value.astype(BF16)
        return carry

    lax.fori_loop(0, total // chunk, rows_at, 0)


def forecasts(state, transform, speed):
    count, total, size = state.shape
    return pl.pallas_call(
        forecast_kernel,
        in_specs=[WHOLE, ANY, WHOLE],
        out_specs=WHOLE,
        out_shape=jax.ShapeDtypeStruct((count, total, size), BF16),
        scratch_shapes=[
            pltpu.VMEM((count, total, total), BF16),
            pltpu.VMEM((count, total, size), F32),
            pltpu.SemaphoreType.DMA((count,)),
        ],
        compiler_params=pltpu.CompilerParams(vmem_limit_bytes=56 * MIB),
        name="forecast",
    )(state, transform, speed)


def analysis_kernel(state, transform, out):
    mean, pert = centred(state[0])
    out[0] = (dot_bf16(transform[0], pert) + mean).astype(BF16)


def analyses(state, transform):
    count, total, size = state.shape
    return pl.pallas_call(
        analysis_kernel,
        grid=(count,),
        in_specs=[
            pl.BlockSpec((1, total, size), lambda a: (a, 0, 0)),
            pl.BlockSpec((1, total, total), lambda a: (a, 0, 0)),
        ],
        out_specs=pl.BlockSpec((1, total, size), lambda a: (a, 0, 0)),
        out_shape=jax.ShapeDtypeStruct((count, total, size), BF16),
        compiler_params=params(1),
        name="analysis",
    )(state, transform)


def shared_transport(analysis, speed, width, jump):
    count, total, size = analysis.shape
    lanes = speed.shape[1]
    cells = lanes // width
    tiles = size // lanes
    fields = widened(analysis, jump).reshape(count + 2, total, tiles, width, cells)
    fields = fields.transpose(1, 0, 3, 2, 4).reshape(total, -1, cells).astype(F32)
    c = speed[0, :cells]
    for _ in range(STEPS):
        prior, here, after = fields[:, :-2], fields[:, 1:-1], fields[:, 2:]
        fields = (1.0 - c * c) * here + 0.5 * (c * c - c) * after + 0.5 * (c * c + c) * prior
    spare = tiles * width - STEPS
    fields = fields[:, spare : fields.shape[1] - spare].astype(BF16)
    fields = fields.reshape(total, count, width, tiles, cells)
    return fields.transpose(1, 0, 3, 2, 4).reshape(count, total, size)


def widened(blocks, jump):
    count = lax.axis_size("sub")
    forward = [(i, (i + jump) % count) for i in range(count)]
    backward = [(target, source) for source, target in forward]
    low = lax.ppermute(blocks[-1:], "sub", forward)
    high = lax.ppermute(blocks[:1], "sub", backward)
    return jnp.concatenate([low, blocks, high], axis=0)


def advance(member_state, hx_values, obs_value, obs_var, courant):
    slabs, local, cells_a, cols = member_state.shape
    patches, own = hx_values.shape[3:]
    owners = lax.axis_size("mem")
    lines = lax.axis_size("sub")
    width = patches // owners
    count = slabs * width
    groups = lines // count
    total = local * owners
    cells_b = cols // patches
    lane_cells = width * cells_b
    place = lax.axis_index("sub") % count
    slab, part = place // width, place % width

    index_groups = None
    if groups > 1:
        held = count * owners
        index_groups = [list(range(g * held, (g + 1) * held)) for g in range(groups)]

    def exchange(blocks):
        return lax.all_to_all(
            blocks,
            ("sub", "mem"),
            split_axis=0,
            concat_axis=0,
            tiled=True,
            axis_index_groups=index_groups,
        )

    hx_rows = exchange(pack_obs(hx_values, width).reshape(count * owners, local, own))
    hx_rows = hx_rows.reshape(count, total, own)

    stats = jnp.stack([obs_value[:, 0], obs_var[:, 0]], axis=2)
    stats = lax.all_gather(stats, "sub", axis=0)
    stats = lax.dynamic_slice(stats, (0, slab, part, 0, 0), (lines, 1, 1, 2, own))
    stats = stats.reshape(lines, 2, own).astype(F32)
    half = own // 2
    stats = jnp.concatenate(
        [jnp.roll(stats, 1, 0)[:, :, half:], stats, jnp.roll(stats, -1, 0)[:, :, :half]], axis=2
    )
    if groups > 1:
        first = lax.axis_index("sub") // count * count
        stats = lax.dynamic_slice_in_dim(stats, first, count, axis=0)
    taper = (jnp.arange(half, dtype=F32) + 1.0) / (half + 1.0)
    local_weight = jnp.concatenate([taper, jnp.ones((own,), F32), taper[::-1]])
    obs_rows = stats[:, 0:1]
    scale_rows = local_weight / stats[:, 1:2]

    state = exchange(pack_state(member_state, width, owners).reshape(count * owners, local, -1))
    state = state.reshape(count, total, -1)

    held_rows = hx_rows if groups == 1 else widened(hx_rows, count)
    transform = transforms(held_rows, obs_rows, scale_rows, count, groups == 1)

    column = (lax.axis_index("mem") * width + part) * cells_b
    speed = lax.dynamic_slice(courant, (slab, column), (1, cells_b))
    speed = jnp.concatenate([speed] * width, axis=1)
    if groups == 1 and width == 2 and cells_a // width >= STEPS:
        fields = forecasts(state, transform, speed)
    else:
        fields = shared_transport(analyses(state, transform), speed, width, count)
    back = exchange(fields.reshape(count * owners, local, -1))
    return unpack_state(back.reshape(slabs, width, owners, local, -1), cells_a)


def solution(mesh):
    in_specs = (
        P(None, "mem", "sub", None),
        P(None, "mem", "sub", None, None),
        P(None, "sub", "mem", None),
        P(None, "sub", "mem", None),
        P(),
    )
    out_specs = P(None, "mem", "sub", None)
    return jax.shard_map(advance, mesh=mesh, in_specs=in_specs, out_specs=out_specs, check_vma=False)
```

```python
import jax
import jax.numpy as jnp
from jax import lax
from jax.experimental import pallas as pl
from jax.experimental.pallas import tpu as pltpu
from jax.sharding import PartitionSpec as P

ITERS = 4
STEPS = 4
F32 = jnp.float32
BF16 = jnp.bfloat16
MIB = 1024 * 1024
WHOLE = pl.BlockSpec(memory_space=pltpu.VMEM)
ANY = pl.BlockSpec(memory_space=pl.ANY)


def params(count, limit=48):
    return pltpu.CompilerParams(
        dimension_semantics=("arbitrary",) * count, vmem_limit_bytes=limit * MIB
    )


def split(value, size):
    return value >> (size.bit_length() - 1), value & (size - 1)


def iota(rows, cols, dim):
    return lax.broadcasted_iota(jnp.int32, (rows, cols), dim)


def dot_bf16(left, right):
    return jnp.dot(left, right, preferred_element_type=F32)


def moved(left, right):
    return dot_bf16(left, right).astype(BF16)


def ones_at(condition):
    return jnp.where(condition, 1.0, 0.0).astype(BF16)


def pack_obs_kernel(rows, out, order, held, packed, in_sems, out_sems):
    slabs, width, owners, local, own = packed.shape
    patches = width * owners
    block = order.shape[0] // patches
    count = local // block
    copies = [
        pltpu.make_async_copy(
            rows.at[slab, pl.ds(at * block, block)],
            held.at[slab, pl.ds(at * block, block)],
            in_sems.at[slab * count + at],
        )
        for slab in range(slabs)
        for at in range(count)
    ]
    for copy in copies:
        copy.start()
    rest, member = split(iota(*order.shape, 0), block)
    side, owner = split(rest, owners)
    order[...] = ones_at(iota(*order.shape, 1) == member * patches + owner * width + side)
    sent = []
    for slab in range(slabs):
        for at in range(count):
            copies[slab * count + at].wait()
            here = slice(at * block, (at + 1) * block)
            flat = moved(order[...], held[slab, here].reshape(block * patches, own))
            packed[slab, :, :, here, :] = flat.reshape(width, owners, block, own)
            rows_here = pl.ds(at * block, block)
            sent.append(
                pltpu.make_async_copy(
                    packed.at[slab, :, :, rows_here],
                    out.at[slab, :, :, rows_here],
                    out_sems.at[slab * count + at],
                )
            )
            sent[-1].start()
    for copy in sent:
        copy.wait()


def pack_obs(hx_values, width):
    slabs, local, _, patches, own = hx_values.shape
    owners = patches // width
    block = 16
    return pl.pallas_call(
        pack_obs_kernel,
        in_specs=[ANY],
        out_specs=ANY,
        out_shape=jax.ShapeDtypeStruct((slabs, width, owners, local, own), BF16),
        scratch_shapes=[
            pltpu.VMEM((block * patches, block * patches), BF16),
            pltpu.VMEM((slabs, local, patches, own), BF16),
            pltpu.VMEM((slabs, width, owners, local, own), BF16),
            pltpu.SemaphoreType.DMA((slabs * local // block,)),
            pltpu.SemaphoreType.DMA((slabs * local // block,)),
        ],
        compiler_params=pltpu.CompilerParams(vmem_limit_bytes=60 * MIB),
        name="pack_obs",
    )(hx_values.reshape(slabs, local, patches, own))


def swapped(width, lanes):
    size = width * lanes
    outer, cell = split(iota(size, size, 1), lanes // width)
    first, second = split(outer, width)
    return ones_at(iota(size, size, 0) == (second * width + first) * (lanes // width) + cell)


def transposed(outer, inner):
    size = outer * inner
    first, second = split(iota(size, size, 0), inner)
    return ones_at(iota(size, size, 1) == second * outer + first)


def pack_state_kernel(cells, out, order, swap):
    _, width, owners, block, size = out.shape
    lanes = cells.shape[3] // owners
    tiles = size // lanes

    @pl.when((pl.program_id(0) == 0) & (pl.program_id(1) == 0))
    def _():
        order[...] = transposed(cells.shape[2], block)
        swap[...] = swapped(width, lanes)

    rows = moved(order[...], cells[...].reshape(order.shape[0], cells.shape[3]))
    parts = []
    for owner in range(owners):
        for tile in range(tiles):
            pieces = [
                rows[
                    (half * tiles + tile) * block : (half * tiles + tile + 1) * block,
                    owner * lanes : (owner + 1) * lanes,
                ]
                for half in range(width)
            ]
            parts.append(jnp.concatenate(pieces, axis=1))
    mixed = moved(jnp.concatenate(parts, axis=0), swap[...])
    for owner in range(owners):
        for tile in range(tiles):
            at = (owner * tiles + tile) * block
            for part in range(width):
                out[0, part, owner, :, tile * lanes : (tile + 1) * lanes] = mixed[
                    at : at + block, part * lanes : (part + 1) * lanes
                ]


def pack_state(member_state, width, owners):
    slabs, local, cells_a, cols = member_state.shape
    lanes = cols // owners
    size = cells_a * lanes // width
    block = 32
    return pl.pallas_call(
        pack_state_kernel,
        grid=(slabs, local // block),
        in_specs=[
            pl.BlockSpec((1, block, cells_a, cols), lambda s, g: (s, g, 0, 0)),
        ],
        out_specs=pl.BlockSpec((1, width, owners, block, size), lambda s, g: (s, 0, 0, g, 0)),
        out_shape=jax.ShapeDtypeStruct((slabs, width, owners, local, size), BF16),
        scratch_shapes=[
            pltpu.VMEM((block * cells_a, block * cells_a), BF16),
            pltpu.VMEM((width * lanes, width * lanes), BF16),
        ],
        compiler_params=params(2, 63),
        name="pack_state",
    )(member_state)


def unpack_state_kernel(packed, out, held, sems):
    slabs, width, owners, local, size = packed.shape
    cells_a = out.shape[2]
    tiles = cells_a // width
    lanes = size // tiles
    count = sems.shape[0] // slabs
    block = local // count
    order = transposed(block, cells_a)
    swap = swapped(width, lanes)
    sent = []
    for slab in range(slabs):
        for at in range(count):
            here = slice(at * block, (at + 1) * block)
            parts = []
            for owner in range(owners):
                for tile in range(tiles):
                    pieces = [
                        packed[slab, part, owner, here, tile * lanes : (tile + 1) * lanes]
                        for part in range(width)
                    ]
                    parts.append(jnp.concatenate(pieces, axis=1))
            mixed = moved(jnp.concatenate(parts, axis=0), swap)
            columns = []
            for owner in range(owners):
                rows = []
                for cell in range(cells_a):
                    half, tile = cell // tiles, cell % tiles
                    start = (owner * tiles + tile) * block
                    rows.append(mixed[start : start + block, half * lanes : (half + 1) * lanes])
                columns.append(jnp.concatenate(rows, axis=0))
            rows = moved(order, jnp.concatenate(columns, axis=1))
            held[slab, here] = rows.reshape(block, cells_a, owners * lanes)
            sent.append(
                pltpu.make_async_copy(
                    held.at[slab, pl.ds(at * block, block)],
                    out.at[slab, pl.ds(at * block, block)],
                    sems.at[slab * count + at],
                )
            )
            sent[-1].start()
    for copy in sent:
        copy.wait()


def unpack_state(packed, cells_a):
    slabs, width, owners, local, size = packed.shape
    lanes = size * width // cells_a
    shape = (slabs, local, cells_a, owners * lanes)
    block = 32
    return pl.pallas_call(
        unpack_state_kernel,
        in_specs=[WHOLE],
        out_specs=ANY,
        out_shape=jax.ShapeDtypeStruct(shape, BF16),
        scratch_shapes=[
            pltpu.VMEM(shape, BF16),
            pltpu.SemaphoreType.DMA((slabs * local // block,)),
        ],
        compiler_params=pltpu.CompilerParams(vmem_limit_bytes=48 * MIB),
        name="unpack_state",
    )(packed)


def transform_kernel(before, middle, after, obs, scale, out, pert, weighted):
    total = middle.shape[1]
    half = before.shape[2]
    projected = jnp.zeros((total, 1), F32)
    start = 0
    for part in (before, middle, after):
        span = part.shape[2]
        for at in range(0, span, half):
            cols = slice(start, start + half)
            values = part[0, :, at : at + half].astype(F32)
            mean = jnp.sum(values, axis=0, keepdims=True) * (1.0 / total)
            centred = values - mean
            pert[:, cols] = centred.astype(BF16)
            scaled = (centred * scale[0, :, cols]).astype(BF16)
            weighted[:, cols] = scaled
            innovation = obs[0, :, cols] - mean
            projected += jnp.sum(scaled.astype(F32) * innovation, axis=1, keepdims=True)
            start += half
    diagonal = iota(total, total, 0) == iota(total, total, 1)
    gram = lax.dot_general(
        weighted[...], pert[...], (((1,), (1,)), ((), ())), preferred_element_type=F32
    )
    system = jnp.where(diagonal, total - 1.0, 0.0) + gram
    bound = jnp.max(jnp.sum(jnp.abs(system), axis=1, keepdims=True), axis=0, keepdims=True)
    root = (system / bound).astype(BF16)
    inverse = None
    for iteration in range(ITERS):
        product = root.astype(F32) if inverse is None else dot_bf16(inverse.astype(BF16), root)
        correction = (jnp.where(diagonal, 1.5, 0.0) - 0.5 * product).astype(BF16)
        if iteration + 1 < ITERS:
            root = moved(root, correction)
        if inverse is None:
            inverse = correction.astype(F32)
        else:
            inverse = dot_bf16(correction, inverse.astype(BF16))
    flipped = inverse.T
    halfway = jnp.sum(flipped * projected, axis=0, keepdims=True)
    weight = jnp.sum(inverse * halfway, axis=1, keepdims=True)
    weight = jnp.broadcast_to(weight, (total, 128)).T[0:1, :] / bound
    out[0] = (jnp.sqrt((total - 1.0) / bound) * flipped + weight).astype(BF16)


def transforms(hx_rows, obs_rows, scale_rows, count, wraps):
    held, total, own = hx_rows.shape
    half = own // 2
    shift = 0 if wraps else 1
    flops = count * (2 * total * total * 2 * own + 18 * total**3)
    return pl.pallas_call(
        transform_kernel,
        grid=(count,),
        in_specs=[
            pl.BlockSpec((1, total, half), lambda a: ((a + shift + held - 1) % held, 0, 1)),
            pl.BlockSpec((1, total, own), lambda a: (a + shift, 0, 0)),
            pl.BlockSpec((1, total, half), lambda a: ((a + shift + 1) % held, 0, 0)),
            pl.BlockSpec((1, 1, 2 * own), lambda a: (a, 0, 0)),
            pl.BlockSpec((1, 1, 2 * own), lambda a: (a, 0, 0)),
        ],
        out_specs=pl.BlockSpec((1, total, total), lambda a: (a, 0, 0)),
        out_shape=jax.ShapeDtypeStruct((count, total, total), BF16),
        scratch_shapes=[pltpu.VMEM((total, 2 * own), BF16), pltpu.VMEM((total, 2 * own), BF16)],
        compiler_params=params(1, 32),
        cost_estimate=pl.CostEstimate(
            flops=flops, bytes_accessed=4 * count * total * total * 2, transcendentals=0
        ),
        name="transform",
    )(hx_rows, hx_rows, hx_rows, obs_rows, scale_rows)


def centred(values):
    values = values.astype(F32)
    mean = jnp.sum(values, axis=0, keepdims=True) * (1.0 / values.shape[0])
    return mean, (values - mean).astype(BF16)


def stencil(c):
    step = [0.5 * (c * c + c), 1.0 - c * c, 0.5 * (c * c - c)]
    taps = step
    for _ in range(STEPS - 1):
        longer = [jnp.zeros_like(c)] * (len(taps) + 2)
        for i, tap in enumerate(taps):
            for j, weight in enumerate(step):
                longer[i + j] = longer[i + j] + tap * weight
        taps = longer
    return taps


def transport(tiles, taps, low):
    count, depth = len(tiles), len(tiles[0])
    shift = tiles[0][0].shape[1] // 2
    turned = [[pltpu.roll(tile, shift, 1) for tile in column] for column in tiles]
    results = []
    for a in range(count):
        before = [jnp.where(low, u, v) for u, v in zip(turned[(a - 1) % count], turned[a])]
        after = [jnp.where(low, u, v) for u, v in zip(turned[a], turned[(a + 1) % count])]
        line = before + tiles[a] + after
        start = depth - STEPS
        results.append(
            [sum(taps[t] * line[start + k + t] for t in range(len(taps))) for k in range(depth)]
        )
    return results


def forecast_kernel(state, transforms, speed, out, transform, fields, sems):
    count, total, size = out.shape
    lanes = speed.shape[1]
    copies = [
        pltpu.make_async_copy(transforms.at[a], transform.at[a], sems.at[a]) for a in range(count)
    ]
    for copy in copies:
        copy.start()
    means = [
        jnp.sum(state[a].astype(F32), axis=0, keepdims=True) * (1.0 / total) for a in range(count)
    ]
    for a, mean in enumerate(means):
        copies[a].wait()
        values = dot_bf16(transform[a], state[a])
        rest = 1.0 - dot_bf16(transform[a], jnp.ones((total, lanes), BF16))
        for k in range(size // lanes):
            part = slice(k * lanes, (k + 1) * lanes)
            fields[a, :, part] = values[:, part] + rest * mean[:, part]
    chunk = 16
    taps = stencil(jnp.broadcast_to(speed[...], (8, lanes)))
    low = iota(8, lanes, 1) < lanes // 2

    def rows_at(step, carry):
        parts = []
        for half in range(chunk // 8):
            at = pl.ds(pl.multiple_of(step * chunk + half * 8, 8), 8)
            tiles = [
                [fields[a, at, k * lanes : (k + 1) * lanes] for k in range(size // lanes)]
                for a in range(count)
            ]
            parts.append(transport(tiles, taps, low))
        at = pl.ds(pl.multiple_of(step * chunk, chunk), chunk)
        for a in range(count):
            for k in range(size // lanes):
                value = jnp.concatenate([part[a][k] for part in parts], axis=0)
                out[a, at, k * lanes : (k + 1) * lanes] = value.astype(BF16)
        return carry

    lax.fori_loop(0, total // chunk, rows_at, 0)


def forecasts(state, transform, speed):
    count, total, size = state.shape
    return pl.pallas_call(
        forecast_kernel,
        in_specs=[WHOLE, ANY, WHOLE],
        out_specs=WHOLE,
        out_shape=jax.ShapeDtypeStruct((count, total, size), BF16),
        scratch_shapes=[
            pltpu.VMEM((count, total, total), BF16),
            pltpu.VMEM((count, total, size), F32),
            pltpu.SemaphoreType.DMA((count,)),
        ],
        compiler_params=pltpu.CompilerParams(vmem_limit_bytes=48 * MIB),
        name="forecast",
    )(state, transform, speed)


def analysis_kernel(state, transform, out):
    mean, pert = centred(state[0])
    out[0] = (dot_bf16(transform[0], pert) + mean).astype(BF16)


def analyses(state, transform):
    count, total, size = state.shape
    return pl.pallas_call(
        analysis_kernel,
        grid=(count,),
        in_specs=[
            pl.BlockSpec((1, total, size), lambda a: (a, 0, 0)),
            pl.BlockSpec((1, total, total), lambda a: (a, 0, 0)),
        ],
        out_specs=pl.BlockSpec((1, total, size), lambda a: (a, 0, 0)),
        out_shape=jax.ShapeDtypeStruct((count, total, size), BF16),
        compiler_params=params(1),
        name="analysis",
    )(state, transform)


def shared_transport(analysis, speed, width, jump):
    count, total, size = analysis.shape
    lanes = speed.shape[1]
    cells = lanes // width
    tiles = size // lanes
    fields = widened(analysis, jump).reshape(count + 2, total, tiles, width, cells)
    fields = fields.transpose(1, 0, 3, 2, 4).reshape(total, -1, cells).astype(F32)
    c = speed[0, :cells]
    for _ in range(STEPS):
        prior, here, after = fields[:, :-2], fields[:, 1:-1], fields[:, 2:]
        fields = (1.0 - c * c) * here + 0.5 * (c * c - c) * after + 0.5 * (c * c + c) * prior
    spare = tiles * width - STEPS
    fields = fields[:, spare : fields.shape[1] - spare].astype(BF16)
    fields = fields.reshape(total, count, width, tiles, cells)
    return fields.transpose(1, 0, 3, 2, 4).reshape(count, total, size)


def widened(blocks, jump):
    count = lax.axis_size("sub")
    forward = [(i, (i + jump) % count) for i in range(count)]
    backward = [(target, source) for source, target in forward]
    low = lax.ppermute(blocks[-1:], "sub", forward)
    high = lax.ppermute(blocks[:1], "sub", backward)
    return jnp.concatenate([low, blocks, high], axis=0)


def advance(member_state, hx_values, obs_value, obs_var, courant):
    slabs, local, cells_a, cols = member_state.shape
    patches, own = hx_values.shape[3:]
    owners = lax.axis_size("mem")
    lines = lax.axis_size("sub")
    width = patches // owners
    count = slabs * width
    groups = lines // count
    total = local * owners
    cells_b = cols // patches
    lane_cells = width * cells_b
    place = lax.axis_index("sub") % count
    slab, part = place // width, place % width

    index_groups = None
    if groups > 1:
        held = count * owners
        index_groups = [list(range(g * held, (g + 1) * held)) for g in range(groups)]

    def exchange(blocks):
        return lax.all_to_all(
            blocks,
            ("sub", "mem"),
            split_axis=0,
            concat_axis=0,
            tiled=True,
            axis_index_groups=index_groups,
        )

    hx_rows = exchange(pack_obs(hx_values, width).reshape(count * owners, local, own))
    hx_rows = hx_rows.reshape(count, total, own)

    stats = jnp.stack([obs_value[:, 0], obs_var[:, 0]], axis=2)
    stats = lax.all_gather(stats, "sub", axis=0)
    stats = lax.dynamic_slice(stats, (0, slab, part, 0, 0), (lines, 1, 1, 2, own))
    stats = stats.reshape(lines, 2, own).astype(F32)
    half = own // 2
    stats = jnp.concatenate(
        [jnp.roll(stats, 1, 0)[:, :, half:], stats, jnp.roll(stats, -1, 0)[:, :, :half]], axis=2
    )
    if groups > 1:
        first = lax.axis_index("sub") // count * count
        stats = lax.dynamic_slice_in_dim(stats, first, count, axis=0)
    taper = (jnp.arange(half, dtype=F32) + 1.0) / (half + 1.0)
    local_weight = jnp.concatenate([taper, jnp.ones((own,), F32), taper[::-1]])
    obs_rows = stats[:, 0:1]
    scale_rows = local_weight / stats[:, 1:2]

    state = exchange(pack_state(member_state, width, owners).reshape(count * owners, local, -1))
    state = state.reshape(count, total, -1)

    held_rows = hx_rows if groups == 1 else widened(hx_rows, count)
    transform = transforms(held_rows, obs_rows, scale_rows, count, groups == 1)

    column = (lax.axis_index("mem") * width + part) * cells_b
    speed = lax.dynamic_slice(courant, (slab, column), (1, cells_b))
    speed = jnp.concatenate([speed] * width, axis=1)
    if groups == 1 and width == 2 and cells_a // width >= STEPS:
        fields = forecasts(state, transform, speed)
    else:
        fields = shared_transport(analyses(state, transform), speed, width, count)
    back = exchange(fields.reshape(count * owners, local, -1))
    return unpack_state(back.reshape(slabs, width, owners, local, -1), cells_a)


def solution(mesh):
    in_specs = (
        P(None, "mem", "sub", None),
        P(None, "mem", "sub", None, None),
        P(None, "sub", "mem", None),
        P(None, "sub", "mem", None),
        P(),
    )
    out_specs = P(None, "mem", "sub", None)
    return jax.shard_map(advance, mesh=mesh, in_specs=in_specs, out_specs=out_specs, check_vma=False)
```

```python
import jax
import jax.numpy as jnp
from jax import lax
from jax.experimental import pallas as pl
from jax.experimental.pallas import tpu as pltpu
from jax.sharding import PartitionSpec as P

ITERS = 4
STEPS = 4
F32 = jnp.float32
BF16 = jnp.bfloat16
MIB = 1024 * 1024
WHOLE = pl.BlockSpec(memory_space=pltpu.VMEM)
ANY = pl.BlockSpec(memory_space=pl.ANY)


def params(count, limit=48):
    return pltpu.CompilerParams(
        dimension_semantics=("arbitrary",) * count, vmem_limit_bytes=limit * MIB
    )


def split(value, size):
    return value >> (size.bit_length() - 1), value & (size - 1)


def iota(rows, cols, dim):
    return lax.broadcasted_iota(jnp.int32, (rows, cols), dim)


def dot_bf16(left, right):
    return jnp.dot(left, right, preferred_element_type=F32)


def moved(left, right):
    return dot_bf16(left, right).astype(BF16)


def ones_at(condition):
    return jnp.where(condition, 1.0, 0.0).astype(BF16)


def pack_obs_kernel(rows, out, order, held, packed, in_sems, out_sems):
    slabs, width, owners, local, own = packed.shape
    patches = width * owners
    block = order.shape[0] // patches
    count = local // block
    copies = [
        pltpu.make_async_copy(
            rows.at[slab, pl.ds(at * block, block)],
            held.at[slab, pl.ds(at * block, block)],
            in_sems.at[slab * count + at],
        )
        for slab in range(slabs)
        for at in range(count)
    ]
    for copy in copies:
        copy.start()
    rest, member = split(iota(*order.shape, 0), block)
    side, owner = split(rest, owners)
    order[...] = ones_at(iota(*order.shape, 1) == member * patches + owner * width + side)
    sent = []
    for slab in range(slabs):
        for at in range(count):
            copies[slab * count + at].wait()
            here = slice(at * block, (at + 1) * block)
            flat = moved(order[...], held[slab, here].reshape(block * patches, own))
            packed[slab, :, :, here, :] = flat.reshape(width, owners, block, own)
            rows_here = pl.ds(at * block, block)
            sent.append(
                pltpu.make_async_copy(
                    packed.at[slab, :, :, rows_here],
                    out.at[slab, :, :, rows_here],
                    out_sems.at[slab * count + at],
                )
            )
            sent[-1].start()
    for copy in sent:
        copy.wait()


def pack_obs(hx_values, width):
    slabs, local, _, patches, own = hx_values.shape
    owners = patches // width
    block = 16
    return pl.pallas_call(
        pack_obs_kernel,
        in_specs=[ANY],
        out_specs=ANY,
        out_shape=jax.ShapeDtypeStruct((slabs, width, owners, local, own), BF16),
        scratch_shapes=[
            pltpu.VMEM((block * patches, block * patches), BF16),
            pltpu.VMEM((slabs, local, patches, own), BF16),
            pltpu.VMEM((slabs, width, owners, local, own), BF16),
            pltpu.SemaphoreType.DMA((slabs * local // block,)),
            pltpu.SemaphoreType.DMA((slabs * local // block,)),
        ],
        compiler_params=pltpu.CompilerParams(vmem_limit_bytes=60 * MIB),
        name="pack_obs",
    )(hx_values.reshape(slabs, local, patches, own))


def swapped(width, lanes):
    size = width * lanes
    outer, cell = split(iota(size, size, 1), lanes // width)
    first, second = split(outer, width)
    return ones_at(iota(size, size, 0) == (second * width + first) * (lanes // width) + cell)


def transposed(outer, inner):
    size = outer * inner
    first, second = split(iota(size, size, 0), inner)
    return ones_at(iota(size, size, 1) == second * outer + first)


def pack_state_kernel(cells, out, order, swap):
    _, width, owners, block, size = out.shape
    lanes = cells.shape[3] // owners
    tiles = size // lanes

    @pl.when((pl.program_id(0) == 0) & (pl.program_id(1) == 0))
    def _():
        order[...] = transposed(cells.shape[2], block)
        swap[...] = swapped(width, lanes)

    rows = moved(order[...], cells[...].reshape(order.shape[0], cells.shape[3]))
    parts = []
    for owner in range(owners):
        for tile in range(tiles):
            pieces = [
                rows[
                    (half * tiles + tile) * block : (half * tiles + tile + 1) * block,
                    owner * lanes : (owner + 1) * lanes,
                ]
                for half in range(width)
            ]
            parts.append(jnp.concatenate(pieces, axis=1))
    mixed = moved(jnp.concatenate(parts, axis=0), swap[...])
    for owner in range(owners):
        for tile in range(tiles):
            at = (owner * tiles + tile) * block
            for part in range(width):
                out[0, part, owner, :, tile * lanes : (tile + 1) * lanes] = mixed[
                    at : at + block, part * lanes : (part + 1) * lanes
                ]


def pack_state(member_state, width, owners):
    slabs, local, cells_a, cols = member_state.shape
    lanes = cols // owners
    size = cells_a * lanes // width
    block = 32
    return pl.pallas_call(
        pack_state_kernel,
        grid=(slabs, local // block),
        in_specs=[
            pl.BlockSpec((1, block, cells_a, cols), lambda s, g: (s, g, 0, 0)),
        ],
        out_specs=pl.BlockSpec((1, width, owners, block, size), lambda s, g: (s, 0, 0, g, 0)),
        out_shape=jax.ShapeDtypeStruct((slabs, width, owners, local, size), BF16),
        scratch_shapes=[
            pltpu.VMEM((block * cells_a, block * cells_a), BF16),
            pltpu.VMEM((width * lanes, width * lanes), BF16),
        ],
        compiler_params=params(2, 63),
        name="pack_state",
    )(member_state)


def unpack_state_kernel(packed, out, held, sems):
    slabs, width, owners, local, size = packed.shape
    cells_a = out.shape[2]
    tiles = cells_a // width
    lanes = size // tiles
    count = sems.shape[0] // slabs
    block = local // count
    order = transposed(block, cells_a)
    swap = swapped(width, lanes)
    sent = []
    for slab in range(slabs):
        for at in range(count):
            here = slice(at * block, (at + 1) * block)
            parts = []
            for owner in range(owners):
                for tile in range(tiles):
                    pieces = [
                        packed[slab, part, owner, here, tile * lanes : (tile + 1) * lanes]
                        for part in range(width)
                    ]
                    parts.append(jnp.concatenate(pieces, axis=1))
            mixed = moved(jnp.concatenate(parts, axis=0), swap)
            columns = []
            for owner in range(owners):
                rows = []
                for cell in range(cells_a):
                    half, tile = cell // tiles, cell % tiles
                    start = (owner * tiles + tile) * block
                    rows.append(mixed[start : start + block, half * lanes : (half + 1) * lanes])
                columns.append(jnp.concatenate(rows, axis=0))
            rows = moved(order, jnp.concatenate(columns, axis=1))
            held[slab, here] = rows.reshape(block, cells_a, owners * lanes)
            sent.append(
                pltpu.make_async_copy(
                    held.at[slab, pl.ds(at * block, block)],
                    out.at[slab, pl.ds(at * block, block)],
                    sems.at[slab * count + at],
                )
            )
            sent[-1].start()
    for copy in sent:
        copy.wait()


def unpack_state(packed, cells_a):
    slabs, width, owners, local, size = packed.shape
    lanes = size * width // cells_a
    shape = (slabs, local, cells_a, owners * lanes)
    block = 32
    return pl.pallas_call(
        unpack_state_kernel,
        in_specs=[WHOLE],
        out_specs=ANY,
        out_shape=jax.ShapeDtypeStruct(shape, BF16),
        scratch_shapes=[
            pltpu.VMEM(shape, BF16),
            pltpu.SemaphoreType.DMA((slabs * local // block,)),
        ],
        compiler_params=pltpu.CompilerParams(vmem_limit_bytes=48 * MIB),
        name="unpack_state",
    )(packed)


def transform_kernel(before, middle, after, obs, scale, out, rest, pert, weighted):
    total = middle.shape[1]
    half = before.shape[2]
    projected = jnp.zeros((total, 1), F32)
    start = 0
    for part in (before, middle, after):
        span = part.shape[2]
        for at in range(0, span, half):
            cols = slice(start, start + half)
            values = part[0, :, at : at + half].astype(F32)
            mean = jnp.sum(values, axis=0, keepdims=True) * (1.0 / total)
            centred = values - mean
            pert[:, cols] = centred.astype(BF16)
            scaled = (centred * scale[0, :, cols]).astype(BF16)
            weighted[:, cols] = scaled
            innovation = obs[0, :, cols] - mean
            projected += jnp.sum(scaled.astype(F32) * innovation, axis=1, keepdims=True)
            start += half
    diagonal = iota(total, total, 0) == iota(total, total, 1)
    gram = lax.dot_general(
        weighted[...], pert[...], (((1,), (1,)), ((), ())), preferred_element_type=F32
    )
    system = jnp.where(diagonal, total - 1.0, 0.0) + gram
    bound = jnp.max(jnp.sum(jnp.abs(system), axis=1, keepdims=True), axis=0, keepdims=True)
    root = (system / bound).astype(BF16)
    inverse = None
    for iteration in range(ITERS):
        product = root.astype(F32) if inverse is None else dot_bf16(inverse.astype(BF16), root)
        correction = (jnp.where(diagonal, 1.5, 0.0) - 0.5 * product).astype(BF16)
        if iteration + 1 < ITERS:
            root = moved(root, correction)
        if inverse is None:
            inverse = correction.astype(F32)
        else:
            inverse = dot_bf16(correction, inverse.astype(BF16))
    flipped = inverse.T
    halfway = jnp.sum(flipped * projected, axis=0, keepdims=True)
    weight = jnp.sum(inverse * halfway, axis=1, keepdims=True)
    weight = jnp.broadcast_to(weight, (total, 128)).T[0:1, :] / bound
    result = (jnp.sqrt((total - 1.0) / bound) * flipped + weight).astype(BF16)
    out[0] = result
    sums = jnp.sum(result.astype(F32), axis=1, keepdims=True)
    rest[0] = jnp.broadcast_to(1.0 - sums, (total, 128))


def transforms(hx_rows, obs_rows, scale_rows, count, wraps):
    held, total, own = hx_rows.shape
    half = own // 2
    shift = 0 if wraps else 1
    flops = count * (2 * total * total * 2 * own + 18 * total**3)
    return pl.pallas_call(
        transform_kernel,
        grid=(count,),
        in_specs=[
            pl.BlockSpec((1, total, half), lambda a: ((a + shift + held - 1) % held, 0, 1)),
            pl.BlockSpec((1, total, own), lambda a: (a + shift, 0, 0)),
            pl.BlockSpec((1, total, half), lambda a: ((a + shift + 1) % held, 0, 0)),
            pl.BlockSpec((1, 1, 2 * own), lambda a: (a, 0, 0)),
            pl.BlockSpec((1, 1, 2 * own), lambda a: (a, 0, 0)),
        ],
        out_specs=[
            pl.BlockSpec((1, total, total), lambda a: (a, 0, 0)),
            pl.BlockSpec((1, total, 128), lambda a: (a, 0, 0)),
        ],
        out_shape=[
            jax.ShapeDtypeStruct((count, total, total), BF16),
            jax.ShapeDtypeStruct((count, total, 128), F32),
        ],
        scratch_shapes=[pltpu.VMEM((total, 2 * own), BF16), pltpu.VMEM((total, 2 * own), BF16)],
        compiler_params=params(1, 32),
        cost_estimate=pl.CostEstimate(
            flops=flops, bytes_accessed=4 * count * total * total * 2, transcendentals=0
        ),
        name="transform",
    )(hx_rows, hx_rows, hx_rows, obs_rows, scale_rows)


def centred(values):
    values = values.astype(F32)
    mean = jnp.sum(values, axis=0, keepdims=True) * (1.0 / values.shape[0])
    return mean, (values - mean).astype(BF16)


def stencil(c):
    step = [0.5 * (c * c + c), 1.0 - c * c, 0.5 * (c * c - c)]
    taps = step
    for _ in range(STEPS - 1):
        longer = [jnp.zeros_like(c)] * (len(taps) + 2)
        for i, tap in enumerate(taps):
            for j, weight in enumerate(step):
                longer[i + j] = longer[i + j] + tap * weight
        taps = longer
    return taps


def transport(tiles, taps, low):
    count, depth = len(tiles), len(tiles[0])
    shift = tiles[0][0].shape[1] // 2
    turned = [[pltpu.roll(tile, shift, 1) for tile in column] for column in tiles]
    results = []
    for a in range(count):
        before = [jnp.where(low, u, v) for u, v in zip(turned[(a - 1) % count], turned[a])]
        after = [jnp.where(low, u, v) for u, v in zip(turned[a], turned[(a + 1) % count])]
        line = before + tiles[a] + after
        start = depth - STEPS
        results.append(
            [sum(taps[t] * line[start + k + t] for t in range(len(taps))) for k in range(depth)]
        )
    return results


def forecast_kernel(state, transform, rest, speed, out, fields):
    count, total, size = out.shape
    lanes = speed.shape[1]
    for a in range(count):
        mean = jnp.sum(state[a].astype(F32), axis=0, keepdims=True) * (1.0 / total)
        values = dot_bf16(transform[a], state[a])
        for k in range(size // lanes):
            part = slice(k * lanes, (k + 1) * lanes)
            fields[a, :, part] = values[:, part] + rest[a] * mean[:, part]
    chunk = 16
    taps = stencil(jnp.broadcast_to(speed[...], (8, lanes)))
    low = iota(8, lanes, 1) < lanes // 2

    def rows_at(step, carry):
        parts = []
        for half in range(chunk // 8):
            at = pl.ds(pl.multiple_of(step * chunk + half * 8, 8), 8)
            tiles = [
                [fields[a, at, k * lanes : (k + 1) * lanes] for k in range(size // lanes)]
                for a in range(count)
            ]
            parts.append(transport(tiles, taps, low))
        at = pl.ds(pl.multiple_of(step * chunk, chunk), chunk)
        for a in range(count):
            for k in range(size // lanes):
                value = jnp.concatenate([part[a][k] for part in parts], axis=0)
                out[a, at, k * lanes : (k + 1) * lanes] = value.astype(BF16)
        return carry

    lax.fori_loop(0, total // chunk, rows_at, 0, unroll=2)


def forecasts(state, transform, rest, speed):
    count, total, size = state.shape
    return pl.pallas_call(
        forecast_kernel,
        in_specs=[WHOLE] * 4,
        out_specs=WHOLE,
        out_shape=jax.ShapeDtypeStruct((count, total, size), BF16),
        scratch_shapes=[pltpu.VMEM((count, total, size), F32)],
        compiler_params=pltpu.CompilerParams(vmem_limit_bytes=20 * MIB),
        name="forecast",
    )(state, transform, rest, speed)


def analysis_kernel(state, transform, out):
    mean, pert = centred(state[0])
    out[0] = (dot_bf16(transform[0], pert) + mean).astype(BF16)


def analyses(state, transform):
    count, total, size = state.shape
    return pl.pallas_call(
        analysis_kernel,
        grid=(count,),
        in_specs=[
            pl.BlockSpec((1, total, size), lambda a: (a, 0, 0)),
            pl.BlockSpec((1, total, total), lambda a: (a, 0, 0)),
        ],
        out_specs=pl.BlockSpec((1, total, size), lambda a: (a, 0, 0)),
        out_shape=jax.ShapeDtypeStruct((count, total, size), BF16),
        compiler_params=params(1),
        name="analysis",
    )(state, transform)


def shared_transport(analysis, speed, width, jump):
    count, total, size = analysis.shape
    lanes = speed.shape[1]
    cells = lanes // width
    tiles = size // lanes
    fields = widened(analysis, jump).reshape(count + 2, total, tiles, width, cells)
    fields = fields.transpose(1, 0, 3, 2, 4).reshape(total, -1, cells).astype(F32)
    c = speed[0, :cells]
    for _ in range(STEPS):
        prior, here, after = fields[:, :-2], fields[:, 1:-1], fields[:, 2:]
        fields = (1.0 - c * c) * here + 0.5 * (c * c - c) * after + 0.5 * (c * c + c) * prior
    spare = tiles * width - STEPS
    fields = fields[:, spare : fields.shape[1] - spare].astype(BF16)
    fields = fields.reshape(total, count, width, tiles, cells)
    return fields.transpose(1, 0, 3, 2, 4).reshape(count, total, size)


def widened(blocks, jump):
    count = lax.axis_size("sub")
    forward = [(i, (i + jump) % count) for i in range(count)]
    backward = [(target, source) for source, target in forward]
    low = lax.ppermute(blocks[-1:], "sub", forward)
    high = lax.ppermute(blocks[:1], "sub", backward)
    return jnp.concatenate([low, blocks, high], axis=0)


def advance(member_state, hx_values, obs_value, obs_var, courant):
    slabs, local, cells_a, cols = member_state.shape
    patches, own = hx_values.shape[3:]
    owners = lax.axis_size("mem")
    lines = lax.axis_size("sub")
    width = patches // owners
    count = slabs * width
    groups = lines // count
    total = local * owners
    cells_b = cols // patches
    lane_cells = width * cells_b
    place = lax.axis_index("sub") % count
    slab, part = place // width, place % width

    index_groups = None
    if groups > 1:
        held = count * owners
        index_groups = [list(range(g * held, (g + 1) * held)) for g in range(groups)]

    def exchange(blocks):
        return lax.all_to_all(
            blocks,
            ("sub", "mem"),
            split_axis=0,
            concat_axis=0,
            tiled=True,
            axis_index_groups=index_groups,
        )

    hx_rows = exchange(pack_obs(hx_values, width).reshape(count * owners, local, own))
    hx_rows = hx_rows.reshape(count, total, own)

    stats = jnp.stack([obs_value[:, 0], obs_var[:, 0]], axis=2)
    stats = lax.all_gather(stats, "sub", axis=0)
    stats = lax.dynamic_slice(stats, (0, slab, part, 0, 0), (lines, 1, 1, 2, own))
    stats = stats.reshape(lines, 2, own).astype(F32)
    half = own // 2
    stats = jnp.concatenate(
        [jnp.roll(stats, 1, 0)[:, :, half:], stats, jnp.roll(stats, -1, 0)[:, :, :half]], axis=2
    )
    if groups > 1:
        first = lax.axis_index("sub") // count * count
        stats = lax.dynamic_slice_in_dim(stats, first, count, axis=0)
    taper = (jnp.arange(half, dtype=F32) + 1.0) / (half + 1.0)
    local_weight = jnp.concatenate([taper, jnp.ones((own,), F32), taper[::-1]])
    obs_rows = stats[:, 0:1]
    scale_rows = local_weight / stats[:, 1:2]

    state = exchange(pack_state(member_state, width, owners).reshape(count * owners, local, -1))
    state = state.reshape(count, total, -1)

    held_rows = hx_rows if groups == 1 else widened(hx_rows, count)
    transform, rest = transforms(held_rows, obs_rows, scale_rows, count, groups == 1)

    column = (lax.axis_index("mem") * width + part) * cells_b
    speed = lax.dynamic_slice(courant, (slab, column), (1, cells_b))
    speed = jnp.concatenate([speed] * width, axis=1)
    if groups == 1 and 2 * cells_b == 128 and width == 2 and cells_a // width >= STEPS:
        fields = forecasts(state, transform, rest, speed)
    else:
        fields = shared_transport(analyses(state, transform), speed, width, count)
    back = exchange(fields.reshape(count * owners, local, -1))
    return unpack_state(back.reshape(slabs, width, owners, local, -1), cells_a)


def solution(mesh):
    in_specs = (
        P(None, "mem", "sub", None),
        P(None, "mem", "sub", None, None),
        P(None, "sub", "mem", None),
        P(None, "sub", "mem", None),
        P(),
    )
    out_specs = P(None, "mem", "sub", None)
    return jax.shard_map(advance, mesh=mesh, in_specs=in_specs, out_specs=out_specs, check_vma=False)
```

```python
import jax
import jax.numpy as jnp
from jax import lax
from jax.experimental import pallas as pl
from jax.experimental.pallas import tpu as pltpu
from jax.sharding import PartitionSpec as P

ITERS = 4
STEPS = 4
F32 = jnp.float32
BF16 = jnp.bfloat16
MIB = 1024 * 1024
WHOLE = pl.BlockSpec(memory_space=pltpu.VMEM)
ANY = pl.BlockSpec(memory_space=pl.ANY)


def params(count, limit=48):
    return pltpu.CompilerParams(
        dimension_semantics=("arbitrary",) * count, vmem_limit_bytes=limit * MIB
    )


def split(value, size):
    return value >> (size.bit_length() - 1), value & (size - 1)


def iota(rows, cols, dim):
    return lax.broadcasted_iota(jnp.int32, (rows, cols), dim)


def dot_bf16(left, right):
    return jnp.dot(left, right, preferred_element_type=F32)


def moved(left, right):
    return dot_bf16(left, right).astype(BF16)


def ones_at(condition):
    return jnp.where(condition, 1.0, 0.0).astype(BF16)


def pack_obs_kernel(rows, out, order, held, packed, in_sems, out_sems):
    slabs, width, owners, local, own = packed.shape
    patches = width * owners
    block = order.shape[0] // patches
    count = local // block
    copies = [
        pltpu.make_async_copy(
            rows.at[slab, pl.ds(at * block, block)],
            held.at[slab, pl.ds(at * block, block)],
            in_sems.at[slab * count + at],
        )
        for slab in range(slabs)
        for at in range(count)
    ]
    for copy in copies:
        copy.start()
    rest, member = split(iota(*order.shape, 0), block)
    side, owner = split(rest, owners)
    order[...] = ones_at(iota(*order.shape, 1) == member * patches + owner * width + side)
    sent = []
    for slab in range(slabs):
        for at in range(count):
            copies[slab * count + at].wait()
            here = slice(at * block, (at + 1) * block)
            flat = moved(order[...], held[slab, here].reshape(block * patches, own))
            packed[slab, :, :, here, :] = flat.reshape(width, owners, block, own)
            rows_here = pl.ds(at * block, block)
            sent.append(
                pltpu.make_async_copy(
                    packed.at[slab, :, :, rows_here],
                    out.at[slab, :, :, rows_here],
                    out_sems.at[slab * count + at],
                )
            )
            sent[-1].start()
    for copy in sent:
        copy.wait()


def pack_obs(hx_values, width):
    slabs, local, _, patches, own = hx_values.shape
    owners = patches // width
    block = 16
    return pl.pallas_call(
        pack_obs_kernel,
        in_specs=[ANY],
        out_specs=ANY,
        out_shape=jax.ShapeDtypeStruct((slabs, width, owners, local, own), BF16),
        scratch_shapes=[
            pltpu.VMEM((block * patches, block * patches), BF16),
            pltpu.VMEM((slabs, local, patches, own), BF16),
            pltpu.VMEM((slabs, width, owners, local, own), BF16),
            pltpu.SemaphoreType.DMA((slabs * local // block,)),
            pltpu.SemaphoreType.DMA((slabs * local // block,)),
        ],
        compiler_params=pltpu.CompilerParams(vmem_limit_bytes=60 * MIB),
        name="pack_obs",
    )(hx_values.reshape(slabs, local, patches, own))


def swapped(width, lanes):
    size = width * lanes
    outer, cell = split(iota(size, size, 1), lanes // width)
    first, second = split(outer, width)
    return ones_at(iota(size, size, 0) == (second * width + first) * (lanes // width) + cell)


def transposed(outer, inner):
    size = outer * inner
    first, second = split(iota(size, size, 0), inner)
    return ones_at(iota(size, size, 1) == second * outer + first)


def pack_state_kernel(cells, out, order, swap):
    _, width, owners, block, size = out.shape
    lanes = cells.shape[3] // owners
    tiles = size // lanes

    @pl.when((pl.program_id(0) == 0) & (pl.program_id(1) == 0))
    def _():
        order[...] = transposed(cells.shape[2], block)
        swap[...] = swapped(width, lanes)

    rows = moved(order[...], cells[...].reshape(order.shape[0], cells.shape[3]))
    parts = []
    for owner in range(owners):
        for tile in range(tiles):
            pieces = [
                rows[
                    (half * tiles + tile) * block : (half * tiles + tile + 1) * block,
                    owner * lanes : (owner + 1) * lanes,
                ]
                for half in range(width)
            ]
            parts.append(jnp.concatenate(pieces, axis=1))
    mixed = moved(jnp.concatenate(parts, axis=0), swap[...])
    for owner in range(owners):
        for tile in range(tiles):
            at = (owner * tiles + tile) * block
            for part in range(width):
                out[0, part, owner, :, tile * lanes : (tile + 1) * lanes] = mixed[
                    at : at + block, part * lanes : (part + 1) * lanes
                ]


def pack_state(member_state, width, owners):
    slabs, local, cells_a, cols = member_state.shape
    lanes = cols // owners
    size = cells_a * lanes // width
    block = 32
    return pl.pallas_call(
        pack_state_kernel,
        grid=(slabs, local // block),
        in_specs=[
            pl.BlockSpec((1, block, cells_a, cols), lambda s, g: (s, g, 0, 0)),
        ],
        out_specs=pl.BlockSpec((1, width, owners, block, size), lambda s, g: (s, 0, 0, g, 0)),
        out_shape=jax.ShapeDtypeStruct((slabs, width, owners, local, size), BF16),
        scratch_shapes=[
            pltpu.VMEM((block * cells_a, block * cells_a), BF16),
            pltpu.VMEM((width * lanes, width * lanes), BF16),
        ],
        compiler_params=params(2, 63),
        name="pack_state",
    )(member_state)


def unpack_state_kernel(packed, out, held, sems):
    slabs, width, owners, local, size = packed.shape
    cells_a = out.shape[2]
    tiles = cells_a // width
    lanes = size // tiles
    count = sems.shape[0] // slabs
    block = local // count
    order = transposed(block, cells_a)
    swap = swapped(width, lanes)
    sent = []
    for slab in range(slabs):
        for at in range(count):
            here = slice(at * block, (at + 1) * block)
            parts = []
            for owner in range(owners):
                for tile in range(tiles):
                    pieces = [
                        packed[slab, part, owner, here, tile * lanes : (tile + 1) * lanes]
                        for part in range(width)
                    ]
                    parts.append(jnp.concatenate(pieces, axis=1))
            mixed = moved(jnp.concatenate(parts, axis=0), swap)
            columns = []
            for owner in range(owners):
                rows = []
                for cell in range(cells_a):
                    half, tile = cell // tiles, cell % tiles
                    start = (owner * tiles + tile) * block
                    rows.append(mixed[start : start + block, half * lanes : (half + 1) * lanes])
                columns.append(jnp.concatenate(rows, axis=0))
            rows = moved(order, jnp.concatenate(columns, axis=1))
            held[slab, here] = rows.reshape(block, cells_a, owners * lanes)
            sent.append(
                pltpu.make_async_copy(
                    held.at[slab, pl.ds(at * block, block)],
                    out.at[slab, pl.ds(at * block, block)],
                    sems.at[slab * count + at],
                )
            )
            sent[-1].start()
    for copy in sent:
        copy.wait()


def unpack_state(packed, cells_a):
    slabs, width, owners, local, size = packed.shape
    lanes = size * width // cells_a
    shape = (slabs, local, cells_a, owners * lanes)
    block = 32
    return pl.pallas_call(
        unpack_state_kernel,
        in_specs=[WHOLE],
        out_specs=ANY,
        out_shape=jax.ShapeDtypeStruct(shape, BF16),
        scratch_shapes=[
            pltpu.VMEM(shape, BF16),
            pltpu.SemaphoreType.DMA((slabs * local // block,)),
        ],
        compiler_params=pltpu.CompilerParams(vmem_limit_bytes=48 * MIB),
        name="unpack_state",
    )(packed)


def transform_kernel(before, middle, after, obs, scale, out, rest, pert, weighted):
    total = middle.shape[1]
    half = before.shape[2]
    projected = jnp.zeros((total, 1), F32)
    start = 0
    for part in (before, middle, after):
        span = part.shape[2]
        for at in range(0, span, half):
            cols = slice(start, start + half)
            values = part[0, :, at : at + half].astype(F32)
            mean = jnp.sum(values, axis=0, keepdims=True) * (1.0 / total)
            centred = values - mean
            pert[:, cols] = centred.astype(BF16)
            scaled = (centred * scale[0, :, cols]).astype(BF16)
            weighted[:, cols] = scaled
            innovation = obs[0, :, cols] - mean
            projected += jnp.sum(scaled.astype(F32) * innovation, axis=1, keepdims=True)
            start += half
    diagonal = iota(total, total, 0) == iota(total, total, 1)
    gram = lax.dot_general(
        weighted[...], pert[...], (((1,), (1,)), ((), ())), preferred_element_type=F32
    )
    system = jnp.where(diagonal, total - 1.0, 0.0) + gram
    bound = jnp.max(jnp.sum(jnp.abs(system), axis=1, keepdims=True), axis=0, keepdims=True)
    root = (system / bound).astype(BF16)
    inverse = None
    for iteration in range(ITERS):
        product = root.astype(F32) if inverse is None else dot_bf16(inverse.astype(BF16), root)
        correction = (jnp.where(diagonal, 1.5, 0.0) - 0.5 * product).astype(BF16)
        if iteration + 1 < ITERS:
            root = moved(root, correction)
        if inverse is None:
            inverse = correction.astype(F32)
        else:
            inverse = dot_bf16(correction, inverse.astype(BF16))
    flipped = inverse.T
    halfway = jnp.sum(flipped * projected, axis=0, keepdims=True)
    weight = jnp.sum(inverse * halfway, axis=1, keepdims=True)
    weight = jnp.broadcast_to(weight, (total, 128)).T[0:1, :] / bound
    result = (jnp.sqrt((total - 1.0) / bound) * flipped + weight).astype(BF16)
    out[0] = result
    sums = jnp.sum(result.astype(F32), axis=1, keepdims=True)
    rest[0] = jnp.broadcast_to(1.0 - sums, (total, 128))


def transforms(hx_rows, obs_rows, scale_rows, count, wraps):
    held, total, own = hx_rows.shape
    half = own // 2
    shift = 0 if wraps else 1
    flops = count * (2 * total * total * 2 * own + 18 * total**3)
    return pl.pallas_call(
        transform_kernel,
        grid=(count,),
        in_specs=[
            pl.BlockSpec((1, total, half), lambda a: ((a + shift + held - 1) % held, 0, 1)),
            pl.BlockSpec((1, total, own), lambda a: (a + shift, 0, 0)),
            pl.BlockSpec((1, total, half), lambda a: ((a + shift + 1) % held, 0, 0)),
            pl.BlockSpec((1, 1, 2 * own), lambda a: (a, 0, 0)),
            pl.BlockSpec((1, 1, 2 * own), lambda a: (a, 0, 0)),
        ],
        out_specs=[
            pl.BlockSpec((1, total, total), lambda a: (a, 0, 0)),
            pl.BlockSpec((1, total, 128), lambda a: (a, 0, 0)),
        ],
        out_shape=[
            jax.ShapeDtypeStruct((count, total, total), BF16),
            jax.ShapeDtypeStruct((count, total, 128), F32),
        ],
        scratch_shapes=[pltpu.VMEM((total, 2 * own), BF16), pltpu.VMEM((total, 2 * own), BF16)],
        compiler_params=params(1, 32),
        cost_estimate=pl.CostEstimate(
            flops=flops, bytes_accessed=4 * count * total * total * 2, transcendentals=0
        ),
        name="transform",
    )(hx_rows, hx_rows, hx_rows, obs_rows, scale_rows)


def centred(values):
    values = values.astype(F32)
    mean = jnp.sum(values, axis=0, keepdims=True) * (1.0 / values.shape[0])
    return mean, (values - mean).astype(BF16)


def stencil(c):
    step = [0.5 * (c * c + c), 1.0 - c * c, 0.5 * (c * c - c)]
    taps = step
    for _ in range(STEPS - 1):
        longer = [jnp.zeros_like(c)] * (len(taps) + 2)
        for i, tap in enumerate(taps):
            for j, weight in enumerate(step):
                longer[i + j] = longer[i + j] + tap * weight
        taps = longer
    return taps


def transport(tiles, taps, low):
    count, depth = len(tiles), len(tiles[0])
    shift = tiles[0][0].shape[1] // 2
    turned = [[pltpu.roll(tile, shift, 1) for tile in column] for column in tiles]
    results = []
    for a in range(count):
        before = [jnp.where(low, u, v) for u, v in zip(turned[(a - 1) % count], turned[a])]
        after = [jnp.where(low, u, v) for u, v in zip(turned[a], turned[(a + 1) % count])]
        line = before + tiles[a] + after
        start = depth - STEPS
        results.append(
            [sum(taps[t] * line[start + k + t] for t in range(len(taps))) for k in range(depth)]
        )
    return results


def forecast_kernel(state, transform, rest, speed, out, fields):
    count, total, size = out.shape
    lanes = speed.shape[1]
    for a in range(count):
        mean = jnp.sum(state[a].astype(F32), axis=0, keepdims=True) * (1.0 / total)
        values = dot_bf16(transform[a], state[a])
        for k in range(size // lanes):
            part = slice(k * lanes, (k + 1) * lanes)
            fields[a, :, part] = values[:, part] + rest[a] * mean[:, part]
    chunk = 16
    taps = stencil(jnp.broadcast_to(speed[...], (8, lanes)))
    low = iota(8, lanes, 1) < lanes // 2

    def rows_at(step, carry):
        parts = []
        for half in range(chunk // 8):
            at = pl.ds(pl.multiple_of(step * chunk + half * 8, 8), 8)
            tiles = [
                [fields[a, at, k * lanes : (k + 1) * lanes] for k in range(size // lanes)]
                for a in range(count)
            ]
            parts.append(transport(tiles, taps, low))
        at = pl.ds(pl.multiple_of(step * chunk, chunk), chunk)
        for a in range(count):
            for k in range(size // lanes):
                value = jnp.concatenate([part[a][k] for part in parts], axis=0)
                out[a, at, k * lanes : (k + 1) * lanes] = value.astype(BF16)
        return carry

    lax.fori_loop(0, total // chunk, rows_at, 0, unroll=4)


def forecasts(state, transform, rest, speed):
    count, total, size = state.shape
    return pl.pallas_call(
        forecast_kernel,
        in_specs=[WHOLE] * 4,
        out_specs=WHOLE,
        out_shape=jax.ShapeDtypeStruct((count, total, size), BF16),
        scratch_shapes=[pltpu.VMEM((count, total, size), F32)],
        compiler_params=pltpu.CompilerParams(vmem_limit_bytes=20 * MIB),
        name="forecast",
    )(state, transform, rest, speed)


def analysis_kernel(state, transform, out):
    mean, pert = centred(state[0])
    out[0] = (dot_bf16(transform[0], pert) + mean).astype(BF16)


def analyses(state, transform):
    count, total, size = state.shape
    return pl.pallas_call(
        analysis_kernel,
        grid=(count,),
        in_specs=[
            pl.BlockSpec((1, total, size), lambda a: (a, 0, 0)),
            pl.BlockSpec((1, total, total), lambda a: (a, 0, 0)),
        ],
        out_specs=pl.BlockSpec((1, total, size), lambda a: (a, 0, 0)),
        out_shape=jax.ShapeDtypeStruct((count, total, size), BF16),
        compiler_params=params(1),
        name="analysis",
    )(state, transform)


def shared_transport(analysis, speed, width, jump):
    count, total, size = analysis.shape
    lanes = speed.shape[1]
    cells = lanes // width
    tiles = size // lanes
    fields = widened(analysis, jump).reshape(count + 2, total, tiles, width, cells)
    fields = fields.transpose(1, 0, 3, 2, 4).reshape(total, -1, cells).astype(F32)
    c = speed[0, :cells]
    for _ in range(STEPS):
        prior, here, after = fields[:, :-2], fields[:, 1:-1], fields[:, 2:]
        fields = (1.0 - c * c) * here + 0.5 * (c * c - c) * after + 0.5 * (c * c + c) * prior
    spare = tiles * width - STEPS
    fields = fields[:, spare : fields.shape[1] - spare].astype(BF16)
    fields = fields.reshape(total, count, width, tiles, cells)
    return fields.transpose(1, 0, 3, 2, 4).reshape(count, total, size)


def widened(blocks, jump):
    count = lax.axis_size("sub")
    forward = [(i, (i + jump) % count) for i in range(count)]
    backward = [(target, source) for source, target in forward]
    low = lax.ppermute(blocks[-1:], "sub", forward)
    high = lax.ppermute(blocks[:1], "sub", backward)
    return jnp.concatenate([low, blocks, high], axis=0)


def advance(member_state, hx_values, obs_value, obs_var, courant):
    slabs, local, cells_a, cols = member_state.shape
    patches, own = hx_values.shape[3:]
    owners = lax.axis_size("mem")
    lines = lax.axis_size("sub")
    width = patches // owners
    count = slabs * width
    groups = lines // count
    total = local * owners
    cells_b = cols // patches
    lane_cells = width * cells_b
    place = lax.axis_index("sub") % count
    slab, part = place // width, place % width

    index_groups = None
    if groups > 1:
        held = count * owners
        index_groups = [list(range(g * held, (g + 1) * held)) for g in range(groups)]

    def exchange(blocks):
        return lax.all_to_all(
            blocks,
            ("sub", "mem"),
            split_axis=0,
            concat_axis=0,
            tiled=True,
            axis_index_groups=index_groups,
        )

    hx_rows = exchange(pack_obs(hx_values, width).reshape(count * owners, local, own))
    hx_rows = hx_rows.reshape(count, total, own)

    stats = jnp.stack([obs_value[:, 0], obs_var[:, 0]], axis=2)
    stats = lax.all_gather(stats, "sub", axis=0)
    stats = lax.dynamic_slice(stats, (0, slab, part, 0, 0), (lines, 1, 1, 2, own))
    stats = stats.reshape(lines, 2, own).astype(F32)
    half = own // 2
    stats = jnp.concatenate(
        [jnp.roll(stats, 1, 0)[:, :, half:], stats, jnp.roll(stats, -1, 0)[:, :, :half]], axis=2
    )
    if groups > 1:
        first = lax.axis_index("sub") // count * count
        stats = lax.dynamic_slice_in_dim(stats, first, count, axis=0)
    taper = (jnp.arange(half, dtype=F32) + 1.0) / (half + 1.0)
    local_weight = jnp.concatenate([taper, jnp.ones((own,), F32), taper[::-1]])
    obs_rows = stats[:, 0:1]
    scale_rows = local_weight / stats[:, 1:2]

    state = exchange(pack_state(member_state, width, owners).reshape(count * owners, local, -1))
    state = state.reshape(count, total, -1)

    held_rows = hx_rows if groups == 1 else widened(hx_rows, count)
    transform, rest = transforms(held_rows, obs_rows, scale_rows, count, groups == 1)

    column = (lax.axis_index("mem") * width + part) * cells_b
    speed = lax.dynamic_slice(courant, (slab, column), (1, cells_b))
    speed = jnp.concatenate([speed] * width, axis=1)
    if groups == 1 and 2 * cells_b == 128 and width == 2 and cells_a // width >= STEPS:
        fields = forecasts(state, transform, rest, speed)
    else:
        fields = shared_transport(analyses(state, transform), speed, width, count)
    back = exchange(fields.reshape(count * owners, local, -1))
    return unpack_state(back.reshape(slabs, width, owners, local, -1), cells_a)


def solution(mesh):
    in_specs = (
        P(None, "mem", "sub", None),
        P(None, "mem", "sub", None, None),
        P(None, "sub", "mem", None),
        P(None, "sub", "mem", None),
        P(),
    )
    out_specs = P(None, "mem", "sub", None)
    return jax.shard_map(advance, mesh=mesh, in_specs=in_specs, out_specs=out_specs, check_vma=False)
```

```python
import jax
import jax.numpy as jnp
from jax import lax
from jax.experimental import pallas as pl
from jax.experimental.pallas import tpu as pltpu
from jax.sharding import PartitionSpec as P

ITERS = 4
STEPS = 4
F32 = jnp.float32
BF16 = jnp.bfloat16
MIB = 1024 * 1024
WHOLE = pl.BlockSpec(memory_space=pltpu.VMEM)
ANY = pl.BlockSpec(memory_space=pl.ANY)


def params(count, limit=48):
    return pltpu.CompilerParams(
        dimension_semantics=("arbitrary",) * count, vmem_limit_bytes=limit * MIB
    )


def split(value, size):
    return value >> (size.bit_length() - 1), value & (size - 1)


def iota(rows, cols, dim):
    return lax.broadcasted_iota(jnp.int32, (rows, cols), dim)


def dot_bf16(left, right):
    return jnp.dot(left, right, preferred_element_type=F32)


def moved(left, right):
    return dot_bf16(left, right).astype(BF16)


def ones_at(condition):
    return jnp.where(condition, 1.0, 0.0).astype(BF16)


def pack_obs_kernel(rows, out, order, held, packed, in_sems, out_sems):
    slabs, width, owners, local, own = packed.shape
    patches = width * owners
    block = order.shape[0] // patches
    count = local // block
    copies = [
        pltpu.make_async_copy(
            rows.at[slab, pl.ds(at * block, block)],
            held.at[slab, pl.ds(at * block, block)],
            in_sems.at[slab * count + at],
        )
        for slab in range(slabs)
        for at in range(count)
    ]
    for copy in copies:
        copy.start()
    rest, member = split(iota(*order.shape, 0), block)
    side, owner = split(rest, owners)
    order[...] = ones_at(iota(*order.shape, 1) == member * patches + owner * width + side)
    sent = []
    for slab in range(slabs):
        for at in range(count):
            copies[slab * count + at].wait()
            here = slice(at * block, (at + 1) * block)
            flat = moved(order[...], held[slab, here].reshape(block * patches, own))
            packed[slab, :, :, here, :] = flat.reshape(width, owners, block, own)
            rows_here = pl.ds(at * block, block)
            sent.append(
                pltpu.make_async_copy(
                    packed.at[slab, :, :, rows_here],
                    out.at[slab, :, :, rows_here],
                    out_sems.at[slab * count + at],
                )
            )
            sent[-1].start()
    for copy in sent:
        copy.wait()


def pack_obs(hx_values, width):
    slabs, local, _, patches, own = hx_values.shape
    owners = patches // width
    block = 16
    return pl.pallas_call(
        pack_obs_kernel,
        in_specs=[ANY],
        out_specs=ANY,
        out_shape=jax.ShapeDtypeStruct((slabs, width, owners, local, own), BF16),
        scratch_shapes=[
            pltpu.VMEM((block * patches, block * patches), BF16),
            pltpu.VMEM((slabs, local, patches, own), BF16),
            pltpu.VMEM((slabs, width, owners, local, own), BF16),
            pltpu.SemaphoreType.DMA((slabs * local // block,)),
            pltpu.SemaphoreType.DMA((slabs * local // block,)),
        ],
        compiler_params=pltpu.CompilerParams(vmem_limit_bytes=60 * MIB),
        name="pack_obs",
    )(hx_values.reshape(slabs, local, patches, own))


def swapped(width, lanes):
    size = width * lanes
    outer, cell = split(iota(size, size, 1), lanes // width)
    first, second = split(outer, width)
    return ones_at(iota(size, size, 0) == (second * width + first) * (lanes // width) + cell)


def transposed(outer, inner):
    size = outer * inner
    first, second = split(iota(size, size, 0), inner)
    return ones_at(iota(size, size, 1) == second * outer + first)


def pack_state_kernel(cells, out, order, swap):
    _, width, owners, block, size = out.shape
    lanes = cells.shape[3] // owners
    tiles = size // lanes

    @pl.when((pl.program_id(0) == 0) & (pl.program_id(1) == 0))
    def _():
        order[...] = transposed(cells.shape[2], block)
        swap[...] = swapped(width, lanes)

    rows = moved(order[...], cells[...].reshape(order.shape[0], cells.shape[3]))
    parts = []
    for owner in range(owners):
        for tile in range(tiles):
            pieces = [
                rows[
                    (half * tiles + tile) * block : (half * tiles + tile + 1) * block,
                    owner * lanes : (owner + 1) * lanes,
                ]
                for half in range(width)
            ]
            parts.append(jnp.concatenate(pieces, axis=1))
    mixed = moved(jnp.concatenate(parts, axis=0), swap[...])
    for owner in range(owners):
        for tile in range(tiles):
            at = (owner * tiles + tile) * block
            for part in range(width):
                out[0, part, owner, :, tile * lanes : (tile + 1) * lanes] = mixed[
                    at : at + block, part * lanes : (part + 1) * lanes
                ]


def pack_state(member_state, width, owners):
    slabs, local, cells_a, cols = member_state.shape
    lanes = cols // owners
    size = cells_a * lanes // width
    block = 32
    return pl.pallas_call(
        pack_state_kernel,
        grid=(slabs, local // block),
        in_specs=[
            pl.BlockSpec((1, block, cells_a, cols), lambda s, g: (s, g, 0, 0)),
        ],
        out_specs=pl.BlockSpec((1, width, owners, block, size), lambda s, g: (s, 0, 0, g, 0)),
        out_shape=jax.ShapeDtypeStruct((slabs, width, owners, local, size), BF16),
        scratch_shapes=[
            pltpu.VMEM((block * cells_a, block * cells_a), BF16),
            pltpu.VMEM((width * lanes, width * lanes), BF16),
        ],
        compiler_params=params(2, 63),
        name="pack_state",
    )(member_state)


def unpack_state_kernel(packed, out, held, sems):
    slabs, width, owners, local, size = packed.shape
    cells_a = out.shape[2]
    tiles = cells_a // width
    lanes = size // tiles
    count = sems.shape[0] // slabs
    block = local // count
    order = transposed(block, cells_a)
    swap = swapped(width, lanes)
    sent = []
    for slab in range(slabs):
        for at in range(count):
            here = slice(at * block, (at + 1) * block)
            parts = []
            for owner in range(owners):
                for tile in range(tiles):
                    pieces = [
                        packed[slab, part, owner, here, tile * lanes : (tile + 1) * lanes]
                        for part in range(width)
                    ]
                    parts.append(jnp.concatenate(pieces, axis=1))
            mixed = moved(jnp.concatenate(parts, axis=0), swap)
            columns = []
            for owner in range(owners):
                rows = []
                for cell in range(cells_a):
                    half, tile = cell // tiles, cell % tiles
                    start = (owner * tiles + tile) * block
                    rows.append(mixed[start : start + block, half * lanes : (half + 1) * lanes])
                columns.append(jnp.concatenate(rows, axis=0))
            rows = moved(order, jnp.concatenate(columns, axis=1))
            held[slab, here] = rows.reshape(block, cells_a, owners * lanes)
            sent.append(
                pltpu.make_async_copy(
                    held.at[slab, pl.ds(at * block, block)],
                    out.at[slab, pl.ds(at * block, block)],
                    sems.at[slab * count + at],
                )
            )
            sent[-1].start()
    for copy in sent:
        copy.wait()


def unpack_state(packed, cells_a):
    slabs, width, owners, local, size = packed.shape
    lanes = size * width // cells_a
    shape = (slabs, local, cells_a, owners * lanes)
    block = 16
    return pl.pallas_call(
        unpack_state_kernel,
        in_specs=[WHOLE],
        out_specs=ANY,
        out_shape=jax.ShapeDtypeStruct(shape, BF16),
        scratch_shapes=[
            pltpu.VMEM(shape, BF16),
            pltpu.SemaphoreType.DMA((slabs * local // block,)),
        ],
        compiler_params=pltpu.CompilerParams(vmem_limit_bytes=48 * MIB),
        name="unpack_state",
    )(packed)


def transform_kernel(before, middle, after, obs, scale, out, rest, pert, weighted):
    total = middle.shape[1]
    half = before.shape[2]
    projected = jnp.zeros((total, 1), F32)
    start = 0
    for part in (before, middle, after):
        span = part.shape[2]
        for at in range(0, span, half):
            cols = slice(start, start + half)
            values = part[0, :, at : at + half].astype(F32)
            mean = jnp.sum(values, axis=0, keepdims=True) * (1.0 / total)
            centred = values - mean
            pert[:, cols] = centred.astype(BF16)
            scaled = (centred * scale[0, :, cols]).astype(BF16)
            weighted[:, cols] = scaled
            innovation = obs[0, :, cols] - mean
            projected += jnp.sum(scaled.astype(F32) * innovation, axis=1, keepdims=True)
            start += half
    diagonal = iota(total, total, 0) == iota(total, total, 1)
    gram = lax.dot_general(
        weighted[...], pert[...], (((1,), (1,)), ((), ())), preferred_element_type=F32
    )
    system = jnp.where(diagonal, total - 1.0, 0.0) + gram
    bound = jnp.max(jnp.sum(jnp.abs(system), axis=1, keepdims=True), axis=0, keepdims=True)
    root = (system / bound).astype(BF16)
    inverse = None
    for iteration in range(ITERS):
        product = root.astype(F32) if inverse is None else dot_bf16(inverse.astype(BF16), root)
        correction = (jnp.where(diagonal, 1.5, 0.0) - 0.5 * product).astype(BF16)
        if iteration + 1 < ITERS:
            root = moved(root, correction)
        if inverse is None:
            inverse = correction.astype(F32)
        else:
            inverse = dot_bf16(correction, inverse.astype(BF16))
    flipped = inverse.T
    halfway = jnp.sum(flipped * projected, axis=0, keepdims=True)
    weight = jnp.sum(inverse * halfway, axis=1, keepdims=True)
    weight = jnp.broadcast_to(weight, (total, 128)).T[0:1, :] / bound
    result = (jnp.sqrt((total - 1.0) / bound) * flipped + weight).astype(BF16)
    out[0] = result
    sums = jnp.sum(result.astype(F32), axis=1, keepdims=True)
    rest[0] = jnp.broadcast_to(1.0 - sums, (total, 128))


def transforms(hx_rows, obs_rows, scale_rows, count, wraps):
    held, total, own = hx_rows.shape
    half = own // 2
    shift = 0 if wraps else 1
    flops = count * (2 * total * total * 2 * own + 18 * total**3)
    return pl.pallas_call(
        transform_kernel,
        grid=(count,),
        in_specs=[
            pl.BlockSpec((1, total, half), lambda a: ((a + shift + held - 1) % held, 0, 1)),
            pl.BlockSpec((1, total, own), lambda a: (a + shift, 0, 0)),
            pl.BlockSpec((1, total, half), lambda a: ((a + shift + 1) % held, 0, 0)),
            pl.BlockSpec((1, 1, 2 * own), lambda a: (a, 0, 0)),
            pl.BlockSpec((1, 1, 2 * own), lambda a: (a, 0, 0)),
        ],
        out_specs=[
            pl.BlockSpec((1, total, total), lambda a: (a, 0, 0)),
            pl.BlockSpec((1, total, 128), lambda a: (a, 0, 0)),
        ],
        out_shape=[
            jax.ShapeDtypeStruct((count, total, total), BF16),
            jax.ShapeDtypeStruct((count, total, 128), F32),
        ],
        scratch_shapes=[pltpu.VMEM((total, 2 * own), BF16), pltpu.VMEM((total, 2 * own), BF16)],
        compiler_params=params(1, 32),
        cost_estimate=pl.CostEstimate(
            flops=flops, bytes_accessed=4 * count * total * total * 2, transcendentals=0
        ),
        name="transform",
    )(hx_rows, hx_rows, hx_rows, obs_rows, scale_rows)


def centred(values):
    values = values.astype(F32)
    mean = jnp.sum(values, axis=0, keepdims=True) * (1.0 / values.shape[0])
    return mean, (values - mean).astype(BF16)


def stencil(c):
    step = [0.5 * (c * c + c), 1.0 - c * c, 0.5 * (c * c - c)]
    taps = step
    for _ in range(STEPS - 1):
        longer = [jnp.zeros_like(c)] * (len(taps) + 2)
        for i, tap in enumerate(taps):
            for j, weight in enumerate(step):
                longer[i + j] = longer[i + j] + tap * weight
        taps = longer
    return taps


def transport(tiles, taps, low):
    count, depth = len(tiles), len(tiles[0])
    shift = tiles[0][0].shape[1] // 2
    turned = [[pltpu.roll(tile, shift, 1) for tile in column] for column in tiles]
    results = []
    for a in range(count):
        before = [jnp.where(low, u, v) for u, v in zip(turned[(a - 1) % count], turned[a])]
        after = [jnp.where(low, u, v) for u, v in zip(turned[a], turned[(a + 1) % count])]
        line = before + tiles[a] + after
        start = depth - STEPS
        results.append(
            [sum(taps[t] * line[start + k + t] for t in range(len(taps))) for k in range(depth)]
        )
    return results


def forecast_kernel(state, transform, rest, speed, out, fields):
    count, total, size = out.shape
    lanes = speed.shape[1]
    for a in range(count):
        mean = jnp.sum(state[a].astype(F32), axis=0, keepdims=True) * (1.0 / total)
        values = dot_bf16(transform[a], state[a])
        for k in range(size // lanes):
            part = slice(k * lanes, (k + 1) * lanes)
            fields[a, :, part] = values[:, part] + rest[a] * mean[:, part]
    chunk = 16
    taps = stencil(jnp.broadcast_to(speed[...], (8, lanes)))
    low = iota(8, lanes, 1) < lanes // 2

    def rows_at(step, carry):
        parts = []
        for half in range(chunk // 8):
            at = pl.ds(pl.multiple_of(step * chunk + half * 8, 8), 8)
            tiles = [
                [fields[a, at, k * lanes : (k + 1) * lanes] for k in range(size // lanes)]
                for a in range(count)
            ]
            parts.append(transport(tiles, taps, low))
        at = pl.ds(pl.multiple_of(step * chunk, chunk), chunk)
        for a in range(count):
            for k in range(size // lanes):
                value = jnp.concatenate([part[a][k] for part in parts], axis=0)
                out[a, at, k * lanes : (k + 1) * lanes] = value.astype(BF16)
        return carry

    lax.fori_loop(0, total // chunk, rows_at, 0, unroll=2)


def forecasts(state, transform, rest, speed):
    count, total, size = state.shape
    return pl.pallas_call(
        forecast_kernel,
        in_specs=[WHOLE] * 4,
        out_specs=WHOLE,
        out_shape=jax.ShapeDtypeStruct((count, total, size), BF16),
        scratch_shapes=[pltpu.VMEM((count, total, size), F32)],
        compiler_params=pltpu.CompilerParams(vmem_limit_bytes=20 * MIB),
        name="forecast",
    )(state, transform, rest, speed)


def analysis_kernel(state, transform, out):
    mean, pert = centred(state[0])
    out[0] = (dot_bf16(transform[0], pert) + mean).astype(BF16)


def analyses(state, transform):
    count, total, size = state.shape
    return pl.pallas_call(
        analysis_kernel,
        grid=(count,),
        in_specs=[
            pl.BlockSpec((1, total, size), lambda a: (a, 0, 0)),
            pl.BlockSpec((1, total, total), lambda a: (a, 0, 0)),
        ],
        out_specs=pl.BlockSpec((1, total, size), lambda a: (a, 0, 0)),
        out_shape=jax.ShapeDtypeStruct((count, total, size), BF16),
        compiler_params=params(1),
        name="analysis",
    )(state, transform)


def shared_transport(analysis, speed, width, jump):
    count, total, size = analysis.shape
    lanes = speed.shape[1]
    cells = lanes // width
    tiles = size // lanes
    fields = widened(analysis, jump).reshape(count + 2, total, tiles, width, cells)
    fields = fields.transpose(1, 0, 3, 2, 4).reshape(total, -1, cells).astype(F32)
    c = speed[0, :cells]
    for _ in range(STEPS):
        prior, here, after = fields[:, :-2], fields[:, 1:-1], fields[:, 2:]
        fields = (1.0 - c * c) * here + 0.5 * (c * c - c) * after + 0.5 * (c * c + c) * prior
    spare = tiles * width - STEPS
    fields = fields[:, spare : fields.shape[1] - spare].astype(BF16)
    fields = fields.reshape(total, count, width, tiles, cells)
    return fields.transpose(1, 0, 3, 2, 4).reshape(count, total, size)


def widened(blocks, jump):
    count = lax.axis_size("sub")
    forward = [(i, (i + jump) % count) for i in range(count)]
    backward = [(target, source) for source, target in forward]
    low = lax.ppermute(blocks[-1:], "sub", forward)
    high = lax.ppermute(blocks[:1], "sub", backward)
    return jnp.concatenate([low, blocks, high], axis=0)


def advance(member_state, hx_values, obs_value, obs_var, courant):
    slabs, local, cells_a, cols = member_state.shape
    patches, own = hx_values.shape[3:]
    owners = lax.axis_size("mem")
    lines = lax.axis_size("sub")
    width = patches // owners
    count = slabs * width
    groups = lines // count
    total = local * owners
    cells_b = cols // patches
    lane_cells = width * cells_b
    place = lax.axis_index("sub") % count
    slab, part = place // width, place % width

    index_groups = None
    if groups > 1:
        held = count * owners
        index_groups = [list(range(g * held, (g + 1) * held)) for g in range(groups)]

    def exchange(blocks):
        return lax.all_to_all(
            blocks,
            ("sub", "mem"),
            split_axis=0,
            concat_axis=0,
            tiled=True,
            axis_index_groups=index_groups,
        )

    hx_rows = exchange(pack_obs(hx_values, width).reshape(count * owners, local, own))
    hx_rows = hx_rows.reshape(count, total, own)

    stats = jnp.stack([obs_value[:, 0], obs_var[:, 0]], axis=2)
    stats = lax.all_gather(stats, "sub", axis=0)
    stats = lax.dynamic_slice(stats, (0, slab, part, 0, 0), (lines, 1, 1, 2, own))
    stats = stats.reshape(lines, 2, own).astype(F32)
    half = own // 2
    stats = jnp.concatenate(
        [jnp.roll(stats, 1, 0)[:, :, half:], stats, jnp.roll(stats, -1, 0)[:, :, :half]], axis=2
    )
    if groups > 1:
        first = lax.axis_index("sub") // count * count
        stats = lax.dynamic_slice_in_dim(stats, first, count, axis=0)
    taper = (jnp.arange(half, dtype=F32) + 1.0) / (half + 1.0)
    local_weight = jnp.concatenate([taper, jnp.ones((own,), F32), taper[::-1]])
    obs_rows = stats[:, 0:1]
    scale_rows = local_weight / stats[:, 1:2]

    state = exchange(pack_state(member_state, width, owners).reshape(count * owners, local, -1))
    state = state.reshape(count, total, -1)

    held_rows = hx_rows if groups == 1 else widened(hx_rows, count)
    transform, rest = transforms(held_rows, obs_rows, scale_rows, count, groups == 1)

    column = (lax.axis_index("mem") * width + part) * cells_b
    speed = lax.dynamic_slice(courant, (slab, column), (1, cells_b))
    speed = jnp.concatenate([speed] * width, axis=1)
    if groups == 1 and 2 * cells_b == 128 and width == 2 and cells_a // width >= STEPS:
        fields = forecasts(state, transform, rest, speed)
    else:
        fields = shared_transport(analyses(state, transform), speed, width, count)
    back = exchange(fields.reshape(count * owners, local, -1))
    return unpack_state(back.reshape(slabs, width, owners, local, -1), cells_a)


def solution(mesh):
    in_specs = (
        P(None, "mem", "sub", None),
        P(None, "mem", "sub", None, None),
        P(None, "sub", "mem", None),
        P(None, "sub", "mem", None),
        P(),
    )
    out_specs = P(None, "mem", "sub", None)
    return jax.shard_map(advance, mesh=mesh, in_specs=in_specs, out_specs=out_specs, check_vma=False)
```
